256 devices in a mesh: grp: 16 (over x, z_lo), kin: 16 (over z_hi, y, core).
Axes of the slice: x: 4, y: 4, z: 8 (z_hi: 2, z_lo: 4; z = z_hi * 4 + z_lo), core: 2. Of those that a mesh axis runs over, the one named last changes fastest.
Arguments:
- waves: bfloat16 [256, 2, 8, 1024], P(('grp', 'kin')), may hold values from -6 to 6
- vector: float32 [256, 2, 16], P(('grp', 'kin')), may hold values from -6 to 6
- energies: float32 [256, 16], P(('grp', 'kin')), may hold values from 0.5 to 1.5
- basis: bfloat16 [2, 1024, 1536], replicated, may hold values from -0.1875 to 0.1875
- screening: float32 [256, 1536], replicated, may hold values from 0.05 to 1
- coulomb: float32 [1536], replicated, may hold values from 0.01 to 0.2
- qmap: int32 [256, 256], P(('grp', 'kin')), may hold values from 0 to 255, as said below
Outputs:
- applied: float32 [256, 2, 16], P(('grp', 'kin'))
The draws below stay inside these ranges and needn't reach their ends.
Inputs may be any that keep to these rules, and one draw needn't show every extreme that they name: qmap[s, s2] is the index, on the periodic 16 x 16 k-grid, of the difference of the grid points of the stored k-points s and s2 (grid point x * 16 + y); the stored k-points are a permutation of the grid points, so each row holds every value once.
All inputs are finite; a program needn't handle non-finite values.
Results may differ from the reference program's by a relative error of at most 0.0057.
Values may be sent and summed in bfloat16 or wider, within the bound.
No kernel may reach another device: no remote copies, remote signals or barrier semaphores. Data moves between devices by JAX's collectives and lax.ppermute only.
A program may use at most 64 MiB of HBM per device.

```python
import math
import jax
import jax.numpy as jnp
from jax import lax

NV = 4
NC = 4
NB = 8
NT = 16
NMU = 1024
NG = 1536
KD = 1
NK = 256
KX = 16
KY = 16
N_GRP = 16
N_KIN = 16


def draw_qmap(key, part):
    key = jax.random.fold_in(key, 11)
    order = jax.random.permutation(key, NK).astype(jnp.int32)
    first = order // KY
    second = order % KY
    step_x = (first[:, None] - first[None, :]) % KX
    step_y = (second[:, None] - second[None, :]) % KY
    return (step_x * KY + step_y).astype(jnp.int32)


def block_scale(own_key, extent, cuts, smallest, top_value):
    gain, own = 1.0, jax.random.fold_in(own_key, 6)
    for axis_at, parts in cuts:
        steps = jnp.exp(jax.random.uniform(jax.random.fold_in(own, axis_at), (parts,), jnp.float32, smallest / len(cuts), top_value / len(cuts)))
        gain = gain * jnp.repeat(steps, extent[axis_at] // parts).reshape([-1 if axis == axis_at else 1 for axis in range(len(extent))])
    return gain


def noise(own_key, dims, spread, reach, pieces=(), kind=jnp.bfloat16):
    entries = spread * jax.random.normal(own_key, dims, jnp.float32)
    if pieces:
        entries = entries * block_scale(own_key, dims, pieces, -0.22, 0.18)
    return jnp.clip(entries, -reach, reach).astype(kind)


def setup_inputs(seed: int = 0) -> dict:
    seeds = jax.random.split(jax.random.key(seed), 8)
    return {
        "waves": noise(seeds[0], (NK, 2, NB, NMU), 1.0, 6.0, ((0, 256),)),
        "vector": noise(seeds[1], (NK, 2, NT), 1.0, 6.0, ((0, 256),), jnp.float32),
        "energies": jnp.clip(0.5 + 1.0 * jax.random.uniform(seeds[2], (NK, NT), jnp.float32) ** block_scale(seeds[2], (NK, NT), ((0, 256),), -0.2, 0.2), 0.5, 1.5),
        "basis": noise(seeds[3], (2, NMU, NG), NMU ** -0.5, 0.1875),
        "screening": jnp.clip(jnp.exp(jax.random.uniform(seeds[4], (NK, NG), jnp.float32, math.log(0.05), math.log(1.0))), 0.05, 1.0),
        "coulomb": jnp.clip(jnp.exp(jax.random.uniform(seeds[5], (NG,), jnp.float32, math.log(0.01), math.log(0.2))), 0.01, 0.2),
        "qmap": draw_qmap(jax.random.fold_in(seeds[7], 71), 0),
    }


def conj_products(left, right):
    left_re = left[:, 0].astype(jnp.float32)[:, None, :, None, :]
    left_im = left[:, 1].astype(jnp.float32)[:, None, :, None, :]
    right_re = right[:, 0].astype(jnp.float32)[None, :, None, :, :]
    right_im = right[:, 1].astype(jnp.float32)[None, :, None, :, :]
    real_part = (left_re * right_re + left_im * right_im).astype(jnp.bfloat16)
    imag_part = (left_re * right_im - left_im * right_re).astype(jnp.bfloat16)
    return real_part, imag_part


def densities(pair_re, pair_im, basis):
    rows = pair_re.shape[0]
    stacked = jnp.concatenate([pair_re, pair_im], 0)
    first = jnp.dot(stacked, basis[0], preferred_element_type=jnp.float32)
    second = jnp.dot(stacked, basis[1], preferred_element_type=jnp.float32)
    real_part = (first[:rows] - second[rows:]).astype(jnp.bfloat16)
    imag_part = (second[:rows] + first[rows:]).astype(jnp.bfloat16)
    return real_part, imag_part


def block_terms(own_waves, own_vector, part_waves, part_vector, weights, basis):
    highest = lax.Precision.HIGHEST
    owners = own_waves.shape[0]
    partners = part_waves.shape[0]
    points = own_waves.shape[3]
    cond_re, cond_im = conj_products(own_waves[:, :, NV:], part_waves[:, :, NV:])
    val_re, val_im = conj_products(own_waves[:, :, :NV], part_waves[:, :, :NV])
    pair_re = jnp.concatenate([cond_re.reshape(owners, partners, NC * NC, points), val_re.reshape(owners, partners, NV * NV, points)], 2).reshape(-1, points)
    pair_im = jnp.concatenate([cond_im.reshape(owners, partners, NC * NC, points), val_im.reshape(owners, partners, NV * NV, points)], 2).reshape(-1, points)
    dens_re, dens_im = densities(pair_re, pair_im, basis)
    dens_re = dens_re.reshape(owners, partners, NC * NC + NV * NV, -1)
    dens_im = dens_im.reshape(owners, partners, NC * NC + NV * NV, -1)
    wcond_re = dens_re[:, :, :NC * NC].astype(jnp.float32) * weights[:, :, None, :]
    wcond_im = dens_im[:, :, :NC * NC].astype(jnp.float32) * weights[:, :, None, :]
    val_dre = dens_re[:, :, NC * NC:].astype(jnp.float32)
    val_dim = dens_im[:, :, NC * NC:].astype(jnp.float32)
    kern_re = jnp.einsum("abpg,abqg->abpq", wcond_re, val_dre, precision=highest) + jnp.einsum("abpg,abqg->abpq", wcond_im, val_dim, precision=highest)
    kern_im = jnp.einsum("abpg,abqg->abpq", wcond_re, val_dim, precision=highest) - jnp.einsum("abpg,abqg->abpq", wcond_im, val_dre, precision=highest)
    kern_re = kern_re.reshape(owners, partners, NC, NC, NV, NV)
    kern_im = kern_im.reshape(owners, partners, NC, NC, NV, NV)
    own_x = own_vector.astype(jnp.float32).reshape(owners, 2, NV, NC)
    part_x = part_vector.astype(jnp.float32).reshape(partners, 2, NV, NC)
    form_d = "abcdvw,bwd->avc"
    direct_re = jnp.einsum(form_d, kern_re, part_x[:, 0], precision=highest) - jnp.einsum(form_d, kern_im, part_x[:, 1], precision=highest)
    direct_im = jnp.einsum(form_d, kern_re, part_x[:, 1], precision=highest) + jnp.einsum(form_d, kern_im, part_x[:, 0], precision=highest)
    form_h = "abcdvw,avc->bwd"
    herm_re = jnp.einsum(form_h, kern_re, own_x[:, 0], precision=highest) + jnp.einsum(form_h, kern_im, own_x[:, 1], precision=highest)
    herm_im = jnp.einsum(form_h, kern_re, own_x[:, 1], precision=highest) - jnp.einsum(form_h, kern_im, own_x[:, 0], precision=highest)
    direct = jnp.stack([direct_re.reshape(owners, NT), direct_im.reshape(owners, NT)], 1)
    hermitian = jnp.stack([herm_re.reshape(partners, NT), herm_im.reshape(partners, NT)], 1)
    return direct, hermitian


def own_densities(waves, basis):
    count = waves.shape[0]
    points = waves.shape[3]
    val_re = waves[:, 0, :NV].astype(jnp.float32)[:, :, None, :]
    val_im = waves[:, 1, :NV].astype(jnp.float32)[:, :, None, :]
    con_re = waves[:, 0, NV:].astype(jnp.float32)[:, None, :, :]
    con_im = waves[:, 1, NV:].astype(jnp.float32)[:, None, :, :]
    pair_re = (val_re * con_re + val_im * con_im).astype(jnp.bfloat16).reshape(-1, points)
    pair_im = (val_re * con_im - val_im * con_re).astype(jnp.bfloat16).reshape(-1, points)
    dens_re, dens_im = densities(pair_re, pair_im, basis)
    return dens_re.reshape(count, NT, -1), dens_im.reshape(count, NT, -1)


def reference(waves, vector, energies, basis, screening, coulomb, qmap):
    highest = lax.Precision.HIGHEST
    offset = N_GRP // 4
    block = KD * N_KIN
    total = block * N_GRP
    coarse = vector.astype(jnp.bfloat16)

    def one_group(group):
        partner = (group - offset) % N_GRP
        own_start = (group * block).astype(jnp.int32)
        part_start = (partner * block).astype(jnp.int32)
        own_waves = lax.dynamic_slice_in_dim(waves, own_start, block, 0)
        part_waves = lax.dynamic_slice_in_dim(waves, part_start, block, 0)
        own_vector = lax.dynamic_slice_in_dim(coarse, own_start, block, 0)
        part_vector = lax.dynamic_slice_in_dim(coarse, part_start, block, 0)
        qrows = lax.dynamic_slice(qmap, (own_start, part_start), (block, block))
        weights = jnp.take(screening, qrows.reshape(-1), axis=0).reshape(block, block, -1)
        return block_terms(own_waves, own_vector, part_waves, part_vector, weights, basis)

    direct, hermitian = lax.map(one_group, jnp.arange(N_GRP, dtype=jnp.int32))
    direct = direct.reshape(total, 2, NT)
    hermitian = jnp.roll(hermitian, -offset, axis=0).reshape(total, 2, NT)
    ex_re, ex_im = own_densities(waves, basis)
    ex_re = ex_re.astype(jnp.float32)
    ex_im = ex_im.astype(jnp.float32)
    coarse_x = coarse.astype(jnp.float32)
    sum_re = jnp.einsum("atg,at->g", ex_re, coarse_x[:, 0], precision=highest) - jnp.einsum("atg,at->g", ex_im, coarse_x[:, 1], precision=highest)
    sum_im = jnp.einsum("atg,at->g", ex_re, coarse_x[:, 1], precision=highest) + jnp.einsum("atg,at->g", ex_im, coarse_x[:, 0], precision=highest)
    pot_re = coulomb * sum_re
    pot_im = coulomb * sum_im
    exch_re = jnp.einsum("atg,g->at", ex_re, pot_re, precision=highest) + jnp.einsum("atg,g->at", ex_im, pot_im, precision=highest)
    exch_im = jnp.einsum("atg,g->at", ex_re, pot_im, precision=highest) - jnp.einsum("atg,g->at", ex_im, pot_re, precision=highest)
    exchange = jnp.stack([exch_re, exch_im], 1)
    scale = jnp.float32(1.0 / total)
    return energies[:, None, :] * vector + 2.0 * scale * exchange - scale * (direct + hermitian)
```

```python
import jax
import jax.numpy as jnp
from jax import lax
from jax.experimental import pallas as pl
from jax.experimental.pallas import tpu as pltpu
from jax.sharding import PartitionSpec as P

NV = 4
NC = 4
NT = 16
NMU = 1024
NG = 1536
WIDTH = NMU + 128
CHUNK = 256
PAIRS = 16
HALF = 2 * PAIRS * NT + NT
F32 = jnp.float32
BF16 = jnp.bfloat16


def move(value, rule):
    pairs = []
    for x in range(4):
        for z in range(4):
            for far in range(2):
                for y in range(4):
                    for core in range(2):
                        nx, nz, nfar, ny, ncore = rule(x, z, far, y, core)
                        source = (x * 4 + z) * 16 + far * 8 + y * 2 + core
                        target = (nx % 4 * 4 + nz) * 16 + nfar * 8 + ny * 2 + ncore
                        pairs.append((source, target))
    return lax.ppermute(value, ("grp", "kin"), pairs)


def flip(x=0, z=0, far=0, y=0, core=0, step=0):
    return lambda a, b, c, d, e: ((a + step) ^ x, b ^ z, c ^ far, d ^ y, e ^ core)


def iota(shape, dim):
    return lax.broadcasted_iota(jnp.int32, shape, dim)


def dot(left, right):
    return jnp.dot(left, right, preferred_element_type=F32)


def dot_t(left, right):
    return lax.dot_general(left, right, (((1,), (1,)), ((), ())), preferred_element_type=F32)


def split(value):
    high = value.astype(BF16)
    return high, (value - high.astype(F32)).astype(BF16)


def dot_split(left, right):
    high, low = split(left)
    return dot(high, right) + dot(low, right)


def onehot(condition):
    return jnp.where(condition, 1.0, 0.0).astype(BF16)


def spread(repeat):
    row = iota((64, 16), 0)
    col = iota((64, 16), 1)
    band = (row >> 2) & 3 if repeat else row & 3
    base = jnp.where(row < 32, 4, 0) + jnp.where((row >> 4) & 1 == 1, 8, 0)
    return onehot(col == band + base)


def transitions_kernel(b0, b1, b2, y_ref):
    total_re = jnp.zeros((1, NMU), F32)
    total_im = jnp.zeros((1, NMU), F32)
    for pay in (b0[...], b1[...], b2[0:16], b2[16:32]):
        waves = pay[:, :NMU]
        mixed = dot(pay[:, NMU : NMU + 16], waves)
        waves = waves.astype(F32)
        val_re, val_im = waves[0:4], waves[8:12]
        mix_re, mix_im = mixed[0:4], mixed[4:8]
        total_re += jnp.sum(val_re * mix_re + val_im * mix_im, 0, keepdims=True)
        total_im += jnp.sum(val_re * mix_im - val_im * mix_re, 0, keepdims=True)
    y_ref[...] = jnp.concatenate([total_re, total_im], 0)


def main_kernel(a0, a1, a2, a3, b0, b1, b2, w_ref, z_ref, out_ref, rx_ref, lhs, xa, xb, kre, kim, ca, cb, cc):
    step = pl.program_id(0)

    def put(row, left_re, left_im, right_re, right_im):
        real = left_re * right_re + left_im * right_im
        imag = left_re * right_im - left_im * right_re
        imag_bf = imag.astype(BF16)
        real_bf = real.astype(BF16)
        lhs[row : row + 16, 0:NMU] = real_bf
        lhs[row : row + 16, NMU : 2 * NMU] = -imag_bf
        lhs[HALF + row : HALF + row + 16, 0:NMU] = imag_bf
        lhs[HALF + row : HALF + row + 16, NMU : 2 * NMU] = real_bf

    @pl.when(step == 0)
    def _():
        rep = spread(True)
        til = spread(False)
        for m, pay in enumerate((a0, a1, a2, a3)):
            xa[m] = dot(rep, pay[:, 0:NMU])
        for n, pay in enumerate((b0[:, 0:NMU], b1[:, 0:NMU], b2[0:16, 0:NMU], b2[16:32, 0:NMU])):
            xb[n] = dot(til, pay)
        own = dot(til, a0[:, 0:NMU])
        for m in range(4):
            for n in range(4):
                row = (m * 4 + n) * 16
                put(row, xa[m, 0:16], xa[m, 16:32], xb[n, 0:16], xb[n, 16:32])
                put(256 + row, xa[m, 32:48], xa[m, 48:64], xb[n, 32:48], xb[n, 48:64])
        put(512, xa[0, 32:48], xa[0, 48:64], own[0:16], own[16:32])
        kre[...] = jnp.zeros_like(kre)
        kim[...] = jnp.zeros_like(kim)

    z = z_ref[...]
    weight = w_ref[...]
    con_re = dot(lhs[0:256], z)
    for p in range(PAIRS):
        ca[p * 16 : p * 16 + 16, 0:CHUNK] = (con_re[p * 16 : p * 16 + 16] * weight[p : p + 1]).astype(BF16)
    con_im = dot(lhs[HALF : HALF + 256], z)
    for p in range(PAIRS):
        ca[p * 16 : p * 16 + 16, CHUNK : 2 * CHUNK] = (con_im[p * 16 : p * 16 + 16] * weight[p : p + 1]).astype(BF16)
    val_re = dot(lhs[256:512], z).astype(BF16)
    cb[:, 0:CHUNK] = val_re
    cc[:, CHUNK : 2 * CHUNK] = -val_re
    val_im = dot(lhs[HALF + 256 : HALF + 512], z).astype(BF16)
    cb[:, CHUNK : 2 * CHUNK] = val_im
    cc[:, 0:CHUNK] = val_im
    rx_ref[0:16] = dot(lhs[512:528], z)
    rx_ref[16:32] = dot(lhs[HALF + 512 : HALF + 528], z)
    kre[...] += dot_t(ca[...], cb[...])
    kim[...] += dot_t(ca[...], cc[...])

    @pl.when(step == pl.num_programs(0) - 1)
    def _():
        pick_row = iota((8, 16), 0)
        pick_col = iota((8, 16), 1)
        xv_a = jnp.zeros((8, 128), F32)
        xv_b = jnp.zeros((8, 128), F32)
        for m, pay in enumerate((a0, a1, a2, a3)):
            xv_a += dot(onehot((pick_row == m) & (pick_col == 8)), pay[:, NMU:WIDTH])
        for n, pay in enumerate((b0[:, NMU:WIDTH], b1[:, NMU:WIDTH], b2[0:16, NMU:WIDTH], b2[16:32, NMU:WIDTH])):
            xv_b += dot(onehot((pick_row == n) & (pick_col == 8)), pay)
        row = iota((256, 8), 0)
        col = iota((256, 8), 1)
        of_a = onehot(row >> 6 == col)
        of_b = onehot((row >> 4) & 3 == col)
        row = iota((256, 128), 0)
        lane = iota((256, 128), 1)
        same_c = (lane & 3) == ((row >> 2) & 3)
        same_d = (lane & 3) == (row & 3)
        spread_a = jnp.where(same_c, dot(of_a, xv_a.astype(BF16)), 0.0).astype(BF16)
        spread_b = jnp.where(same_d, dot(of_b, xv_b.astype(BF16)), 0.0).astype(BF16)
        lane = iota((128, 256), 0)
        col = iota((128, 256), 1)
        by_w = (lane >> 2) & 3 == col & 3
        by_v = (lane >> 2) & 3 == (col >> 2) & 3
        first = lane < 16
        second = (lane >= 16) & (lane < 32)
        pair = (iota((256, 256), 0) >> 4) == (iota((256, 256), 1) >> 4)
        k_re = jnp.where(pair, kre[...], 0.0)
        k_im = jnp.where(pair, kim[...], 0.0)
        xd_re = dot(spread_b, onehot(by_w & first))
        xd_im = dot(spread_b, onehot(by_w & second))
        xh_re = dot(spread_a, onehot(by_v & first))
        xh_im = dot(spread_a, onehot(by_v & second))
        lane = iota((256, 128), 1)
        col = iota((256, 128), 0)
        by_w = (lane >> 2) & 3 == col & 3
        by_v = (lane >> 2) & 3 == (col >> 2) & 3
        first = lane < 16
        second = (lane >= 16) & (lane < 32)
        sum_d = dot_split(k_re * xd_re - k_im * xd_im, onehot(by_v & first)) + dot_split(
            k_re * xd_im + k_im * xd_re, onehot(by_v & second)
        )
        sum_h = dot_split(k_re * xh_re + k_im * xh_im, onehot(by_w & first)) + dot_split(
            k_re * xh_im - k_im * xh_re, onehot(by_w & second)
        )
        sum_d = jnp.where(same_c, sum_d, 0.0)
        sum_h = jnp.where(same_d, sum_h, 0.0)
        row = iota((8, 256), 0)
        col = iota((8, 256), 1)
        to_a = onehot(row == col >> 6)
        to_b = onehot(row == 4 + ((col >> 4) & 3))
        high_d, low_d = split(sum_d)
        high_h, low_h = split(sum_h)
        out_ref[...] = dot(to_a, high_d) + dot(to_a, low_d) + dot(to_b, high_h) + dot(to_b, low_h)


def exchange_kernel(y0, y1, y2, y3, c_ref, rx_ref, z_ref, out_ref, lhs, acc_re, acc_im):
    step = pl.program_id(0)

    @pl.when(step == 0)
    def _():
        total = y0[...] + y1[...] + y2[...] + y3[...]
        swap = jnp.concatenate([-total[1:2], total[0:1]], 0)
        high, low = split(jnp.concatenate([total, swap], 1))
        pad = jnp.zeros((12, 2 * NMU), F32)
        lhs[...] = jnp.concatenate([high.astype(F32), low.astype(F32), pad], 0).astype(BF16)
        acc_re[...] = jnp.zeros_like(acc_re)
        acc_im[...] = jnp.zeros_like(acc_im)

    total = dot(lhs[...], z_ref[...])
    pot_re = (total[0:1] + total[2:3]) * c_ref[...]
    pot_im = (total[1:2] + total[3:4]) * c_ref[...]
    rx_re = rx_ref[0:16]
    rx_im = rx_ref[16:32]
    real = rx_re * pot_re + rx_im * pot_im
    imag = rx_re * pot_im - rx_im * pot_re
    for at in range(0, CHUNK, 128):
        acc_re[...] += real[:, at : at + 128]
        acc_im[...] += imag[:, at : at + 128]

    @pl.when(step == pl.num_programs(0) - 1)
    def _():
        ones = jnp.ones((8, 128), BF16)
        out = []
        for acc in (acc_re[...], acc_im[...]):
            high, low = split(acc)
            out.append((dot_t(ones, high) + dot_t(ones, low))[0:1])
        out_ref[...] = jnp.concatenate(out, 0)


def whole(shape):
    return pl.BlockSpec(shape, lambda i: tuple(0 for _ in shape))


def pack(waves, vector):
    block = waves.reshape(16, NMU)
    coarse = vector.astype(BF16).reshape(2, NT)
    real = coarse[0].reshape(NV, NC)
    imag = coarse[1].reshape(NV, NC)
    gap = jnp.zeros((NV, NC), BF16)
    mixer = jnp.concatenate(
        [
            jnp.concatenate([gap, real, gap, -imag], 1),
            jnp.concatenate([gap, imag, gap, real], 1),
        ],
        0,
    )
    mixer = jnp.pad(mixer, ((0, 0), (0, 112)))
    line = jnp.pad(coarse.reshape(1, 32), ((0, 7), (0, 96)))
    return jnp.concatenate([block, jnp.concatenate([mixer, line], 0)], 1)


def pair_rows(qmap):
    own = lax.axis_index("grp")
    member = lax.axis_index("kin")
    partner = (own - 4) % 16
    row = qmap[0]
    from_a = jnp.stack([row[own * 16 + (member ^ (m << 1))] for m in range(4)])
    from_b = jnp.stack([row[partner * 16 + (member ^ n)] for n in (0, 8, 1, 9)])
    step_x = ((from_b >> 4)[None, :] - (from_a >> 4)[:, None]) & 15
    step_y = (from_b[None, :] - from_a[:, None]) & 15
    return (step_x * 16 + step_y).reshape(-1)


def on_device(waves, vector, energies, basis, screening, coulomb, qmap):
    pay = pack(waves, vector)
    b1 = move(pay, flip(step=1, far=1))
    b0 = move(pay, flip(step=1))
    b2 = move(jnp.concatenate([b0, b1], 0), flip(core=1))
    a2 = move(pay, flip(y=2))
    a1 = move(pay, flip(y=1))
    a3 = move(pay, flip(y=3))
    weights = jnp.take(screening, pair_rows(qmap), axis=0)
    stacked = basis.reshape(2 * NMU, NG)
    steps = NG // CHUNK

    y = pl.pallas_call(
        transitions_kernel,
        out_shape=jax.ShapeDtypeStruct((2, NMU), F32),
    )(b0, b1, b2)
    out, rx = pl.pallas_call(
        main_kernel,
        grid=(steps,),
        in_specs=[whole((16, WIDTH))] * 6
        + [
            whole((32, WIDTH)),
            pl.BlockSpec((PAIRS, CHUNK), lambda i: (0, i)),
            pl.BlockSpec((2 * NMU, CHUNK), lambda i: (0, i)),
        ],
        out_specs=[whole((8, 128)), pl.BlockSpec((32, CHUNK), lambda i: (0, i))],
        out_shape=[
            jax.ShapeDtypeStruct((8, 128), F32),
            jax.ShapeDtypeStruct((32, NG), F32),
        ],
        scratch_shapes=[
            pltpu.VMEM((2 * HALF, 2 * NMU), BF16),
            pltpu.VMEM((4, 64, NMU), F32),
            pltpu.VMEM((4, 64, NMU), F32),
            pltpu.VMEM((256, 256), F32),
            pltpu.VMEM((256, 256), F32),
            pltpu.VMEM((256, 2 * CHUNK), BF16),
            pltpu.VMEM((256, 2 * CHUNK), BF16),
            pltpu.VMEM((256, 2 * CHUNK), BF16),
        ],
        compiler_params=pltpu.CompilerParams(vmem_limit_bytes=32 * 1024 * 1024),
        cost_estimate=pl.CostEstimate(
            flops=2 * 2 * HALF * 2 * NMU * NG, bytes_accessed=4 * NMU * NG, transcendentals=0
        ),
    )(a0_of(pay), a1, a2, a3, b0, b1, b2, weights, stacked)

    for rules in (
        [flip(y=n) for n in (2, 1, 3)],
        [flip(x=n) for n in (2, 1, 3)],
    ):
        y = y + move(y, rules[0]) + move(y, rules[1]) + move(y, rules[2])
    others = [move(y, flip(z=n)) for n in (2, 1, 3)]
    exchange = pl.pallas_call(
        exchange_kernel,
        grid=(steps,),
        in_specs=[whole((2, NMU))] * 4
        + [
            pl.BlockSpec((1, CHUNK), lambda i: (0, i)),
            pl.BlockSpec((32, CHUNK), lambda i: (0, i)),
            pl.BlockSpec((2 * NMU, CHUNK), lambda i: (0, i)),
        ],
        out_specs=whole((2, 16)),
        out_shape=jax.ShapeDtypeStruct((2, 16), F32),
        scratch_shapes=[
            pltpu.VMEM((16, 2 * NMU), BF16),
            pltpu.VMEM((16, 128), F32),
            pltpu.VMEM((16, 128), F32),
        ],
        compiler_params=pltpu.CompilerParams(vmem_limit_bytes=32 * 1024 * 1024),
        cost_estimate=pl.CostEstimate(
            flops=2 * 16 * 2 * NMU * NG, bytes_accessed=4 * NMU * NG, transcendentals=0
        ),
    )(y, *others, coulomb.reshape(1, NG), rx, stacked)

    herm = out[4:6] + move(out[6:8], flip(core=1))
    terms = (
        out[0:1]
        + move(out[1:2], flip(y=1))
        + move(out[2:3], flip(y=2))
        + move(out[3:4], flip(y=3))
        + move(herm[0:1], flip(step=3))
        + move(herm[1:2], flip(step=3, far=1))
    )
    terms = terms[:, 0:32].reshape(1, 2, NT)
    scale = jnp.float32(1.0 / 256)
    return energies[:, None, :] * vector + 2.0 * scale * exchange[None] - scale * terms


def a0_of(pay):
    return pay


def solution(mesh):
    return jax.shard_map(
        on_device,
        mesh=mesh,
        in_specs=(
            P(("grp", "kin"), None, None, None),
            P(("grp", "kin"), None, None),
            P(("grp", "kin"), None),
            P(),
            P(),
            P(),
            P(("grp", "kin"), None),
        ),
        out_specs=P(("grp", "kin"), None, None),
        check_vma=False,
    )
```

```python
import functools

import jax
import jax.numpy as jnp
from jax import lax
from jax.experimental import pallas as pl
from jax.experimental.pallas import tpu as pltpu
from jax.sharding import PartitionSpec as P

NT = 16
NMU = 1024
NG = 1536
WIDTH = NMU + 128
CHUNK = 512
ROWS = 128
F32 = jnp.float32
BF16 = jnp.bfloat16
VMEM = pl.BlockSpec(memory_space=pltpu.VMEM)
SMEM = pl.BlockSpec(memory_space=pltpu.SMEM)
ANY = pl.BlockSpec(memory_space=pl.ANY)


def move(value, x=0, z=0, far=0, y=0, core=0, step=0):
    pairs = []
    for a in range(4):
        for b in range(4):
            for c in range(2):
                for d in range(4):
                    for e in range(2):
                        source = (a * 4 + b) * 16 + c * 8 + d * 2 + e
                        group = (((a + step) % 4) ^ x) * 4 + (b ^ z)
                        member = (c ^ far) * 8 + (d ^ y) * 2 + (e ^ core)
                        pairs.append((source, group * 16 + member))
    return lax.ppermute(value, ("grp", "kin"), pairs)


def iota(shape, dim):
    return lax.broadcasted_iota(jnp.int32, shape, dim)


def dot(left, right):
    return jnp.dot(left, right, preferred_element_type=F32)


def dot_t(left, right):
    return lax.dot_general(left, right, (((1,), (1,)), ((), ())), preferred_element_type=F32)


def split(value):
    high = value.astype(BF16)
    return high, (value - high.astype(F32)).astype(BF16)


def dot_split(left, right):
    high, low = split(left)
    return dot(high, right) + dot(low, right)


def onehot(condition):
    return jnp.where(condition, 1.0, 0.0).astype(BF16)


def spread(repeat):
    row = iota((64, 16), 0)
    col = iota((64, 16), 1)
    band = (row >> 2) & 3 if repeat else row & 3
    base = jnp.where(row < 32, 4, 0) + jnp.where((row >> 4) & 1 == 1, 8, 0)
    return onehot(col == band + base)


def conj_product(left_re, left_im, right_re, right_im):
    real = (left_re * right_re + left_im * right_im).astype(BF16)
    imag = (left_re * right_im - left_im * right_re).astype(BF16)
    return real, imag


def pack_kernel(waves_ref, vector_ref, pay_ref):
    coarse = vector_ref[...].astype(BF16).astype(F32)
    real = jnp.broadcast_to(coarse[0:1], (16, 16))
    imag = jnp.broadcast_to(coarse[1:2], (16, 16))
    row = iota((16, 16), 0)
    lane = iota((16, 16), 1)
    of_v = lane >> 2 == row & 3
    by_c = onehot(row & 3 == lane & 3)
    real_v = dot(jnp.where(of_v, real, 0.0).astype(BF16), by_c)
    imag_v = dot(jnp.where(of_v, imag, 0.0).astype(BF16), by_c)
    upper = row < 8
    first = jnp.where(upper, real_v, imag_v)
    second = jnp.where(upper, -imag_v, real_v)
    mixer = jnp.where(lane & 8 == 0, first, second)
    mixer = jnp.where((row & 4 == 0) & (lane & 4 == 4), mixer, 0.0).astype(BF16)
    line_re = jnp.where(row == 12, real, 0.0).astype(BF16)
    line_im = jnp.where(row == 12, imag, 0.0).astype(BF16)
    row = iota((16, 128), 0)
    lane = iota((16, 128), 1)
    block = dot(mixer, onehot(lane == row)) + dot(line_re, onehot(lane == row + 16)) + dot(line_im, onehot(lane == row + 32))
    pay_ref[:, 0:NMU] = waves_ref[...]
    pay_ref[:, NMU:WIDTH] = block.astype(BF16)


def own_kernel(where_ref, qmap_ref, pay_ref, z_ref, screening, rx_ref, first_ref, second_ref, lhs, sems):
    own = where_ref[0]
    member = where_ref[1]
    partner = (own + 12) & 15
    steps = []
    for m, flip in enumerate((8, 9, 0, 1)):
        from_a = qmap_ref[0, own * 16 + (member ^ flip)]
        for n in range(4):
            from_b = qmap_ref[0, partner * 16 + (member ^ (2 * n))]
            index = (((from_b >> 4) - (from_a >> 4)) & 15) * 16 + ((from_b - from_a) & 15)
            target = first_ref if m < 2 else second_ref
            at = (m & 1) * 4 + n
            copy = pltpu.make_async_copy(
                screening.at[pl.ds(index, 1)], target.at[pl.ds(at, 1)], sems.at[m * 4 + n]
            )
            copy.start()
            steps.append(copy)
    waves = pay_ref[:, 0:NMU]
    left = dot(spread(True), waves)
    right = dot(spread(False), waves)
    real, imag = conj_product(left[32:48], left[48:64], right[0:16], right[16:32])
    lhs[0:16, 0:NMU] = real
    lhs[0:16, NMU : 2 * NMU] = -imag
    lhs[16:32, 0:NMU] = imag
    lhs[16:32, NMU : 2 * NMU] = real
    rx_ref[...] = dot(lhs[...], z_ref[...])
    for copy in steps:
        copy.wait()


def transitions_kernel(a0, a1, a2, y_ref):
    total_re = jnp.zeros((8, NMU), F32)
    total_im = jnp.zeros((8, NMU), F32)
    for pay in (a0[...], a1[...], a2[0:16], a2[16:32]):
        waves = pay[:, :NMU]
        mixed = dot(pay[:, NMU : NMU + 16], waves)
        waves = waves.astype(F32)
        val_re, val_im = waves[0:8], waves[8:16]
        mix_re, mix_im = mixed[0:8], mixed[8:16]
        total_re += val_re * mix_re + val_im * mix_im
        total_im += val_re * mix_im - val_im * mix_re
    total_re = jnp.sum(total_re, 0, keepdims=True)
    total_im = jnp.sum(total_im, 0, keepdims=True)
    y_ref[...] = jnp.concatenate([total_re, total_im], 0)


def pair_kernel(from_core, *refs):
    a_near, a_pair, b0, b1, b2, b3, w_ref, z_ref, _, out_ref, lhs, xa, xb, acc, ca, cb = refs
    a_pays = (a_near[...], a_pair[from_core : from_core + 16])
    b_pays = (b0[...], b1[...], b2[...], b3[...])
    half = 2 * ROWS

    def put(row, left, right, at):
        real, imag = conj_product(left[at : at + 16], left[at + 16 : at + 32], right[at : at + 16], right[at + 16 : at + 32])
        lhs[row : row + 16, 0:NMU] = real
        lhs[row : row + 16, NMU : 2 * NMU] = -imag
        lhs[half + row : half + row + 16, 0:NMU] = imag
        lhs[half + row : half + row + 16, NMU : 2 * NMU] = real

    rep = spread(True)
    til = spread(False)
    for m in range(2):
        xa[m] = dot(rep, a_pays[m][:, 0:NMU])
    for n in range(4):
        xb[n] = dot(til, b_pays[n][:, 0:NMU])
    for m in range(2):
        for n in range(4):
            row = (m * 4 + n) * 16
            put(row, xa[m], xb[n], 0)
            put(ROWS + row, xa[m], xb[n], 32)
    acc[...] = jnp.zeros_like(acc)
    for at in range(0, NG, CHUNK):
        z = z_ref[:, at : at + CHUNK]
        con_re = dot(lhs[0:ROWS], z)
        for p in range(8):
            weight = w_ref[p : p + 1, at : at + CHUNK]
            ca[p * 16 : p * 16 + 16, 0:CHUNK] = (con_re[p * 16 : p * 16 + 16] * weight).astype(BF16)
        con_im = dot(lhs[half : half + ROWS], z)
        for p in range(8):
            weight = w_ref[p : p + 1, at : at + CHUNK]
            ca[p * 16 : p * 16 + 16, CHUNK : 2 * CHUNK] = (con_im[p * 16 : p * 16 + 16] * weight).astype(BF16)
        val_re = dot(lhs[ROWS:half], z).astype(BF16)
        cb[0:ROWS, 0:CHUNK] = val_re
        cb[ROWS:half, CHUNK : 2 * CHUNK] = -val_re
        val_im = dot(lhs[half + ROWS : 2 * half], z).astype(BF16)
        cb[0:ROWS, CHUNK : 2 * CHUNK] = val_im
        cb[ROWS:half, 0:CHUNK] = val_im
        acc[...] += dot_t(ca[...], cb[...])

    pick_row = iota((8, 16), 0)
    pick_col = iota((8, 16), 1)
    xv_a = jnp.zeros((8, 128), F32)
    xv_b = jnp.zeros((8, 128), F32)
    for m in range(2):
        xv_a += dot(onehot((pick_row == m) & (pick_col == 12)), a_pays[m][:, NMU:WIDTH])
    for n in range(4):
        xv_b += dot(onehot((pick_row == n) & (pick_col == 12)), b_pays[n][:, NMU:WIDTH])
    row = iota((ROWS, 8), 0)
    col = iota((ROWS, 8), 1)
    of_a = onehot(row >> 6 == col)
    of_b = onehot((row >> 4) & 3 == col)
    row = iota((ROWS, 128), 0)
    lane = iota((ROWS, 128), 1)
    same_c = lane & 3 == (row >> 2) & 3
    same_d = lane & 3 == row & 3
    spread_a = jnp.where(same_c, dot(of_a, xv_a.astype(BF16)), 0.0).astype(BF16)
    spread_b = jnp.where(same_d, dot(of_b, xv_b.astype(BF16)), 0.0).astype(BF16)
    lane = iota((128, ROWS), 0)
    col = iota((128, ROWS), 1)
    by_w = (lane >> 2) & 3 == col & 3
    by_v = (lane >> 2) & 3 == (col >> 2) & 3
    first = lane >> 4 == 1
    second = lane >> 4 == 2
    pair = iota((ROWS, ROWS), 0) >> 4 == iota((ROWS, ROWS), 1) >> 4
    k_re = jnp.where(pair, acc[:, 0:ROWS], 0.0)
    k_im = jnp.where(pair, acc[:, ROWS:half], 0.0)
    xd_re = dot(spread_b, onehot(by_w & first))
    xd_im = dot(spread_b, onehot(by_w & second))
    xh_re = dot(spread_a, onehot(by_v & first))
    xh_im = dot(spread_a, onehot(by_v & second))
    lane = iota((ROWS, 128), 1)
    col = iota((ROWS, 128), 0)
    by_w = (lane >> 2) & 3 == col & 3
    by_v = (lane >> 2) & 3 == (col >> 2) & 3
    first = lane >> 4 == 0
    second = lane >> 4 == 1
    sum_d = dot_split(k_re * xd_re - k_im * xd_im, onehot(by_v & first)) + dot_split(
        k_re * xd_im + k_im * xd_re, onehot(by_v & second)
    )
    sum_h = dot_split(k_re * xh_re + k_im * xh_im, onehot(by_w & first)) + dot_split(
        k_re * xh_im - k_im * xh_re, onehot(by_w & second)
    )
    sum_d = jnp.where(same_c, sum_d, 0.0)
    sum_h = jnp.where(same_d, sum_h, 0.0)
    row = iota((8, ROWS), 0)
    col = iota((8, ROWS), 1)
    to_a = onehot(row == col >> 6)
    to_b = onehot(row == 4 + ((col >> 4) & 3))
    high_d, low_d = split(sum_d)
    high_h, low_h = split(sum_h)
    out_ref[...] = dot(to_a, high_d) + dot(to_a, low_d) + dot(to_b, high_h) + dot(to_b, low_h)


def exchange_kernel(y0, y1, y2, y3, c_ref, rx_ref, z_ref, out_ref, lhs):
    total = y0[...] + y1[...] + y2[...] + y3[...]
    swap = jnp.concatenate([-total[1:2], total[0:1]], 0)
    high, low = split(jnp.concatenate([total, swap], 1))
    pad = jnp.zeros((12, 2 * NMU), F32)
    lhs[...] = jnp.concatenate([high.astype(F32), low.astype(F32), pad], 0).astype(BF16)
    acc_re = jnp.zeros((16, 128), F32)
    acc_im = jnp.zeros((16, 128), F32)
    for start in range(0, NG, CHUNK):
        part = pl.ds(start, CHUNK)
        total = dot(lhs[...], z_ref[:, part])
        pot_re = (total[0:1] + total[2:3]) * c_ref[:, part]
        pot_im = (total[1:2] + total[3:4]) * c_ref[:, part]
        rx_re = rx_ref[0:16, part]
        rx_im = rx_ref[16:32, part]
        real = rx_re * pot_re + rx_im * pot_im
        imag = rx_re * pot_im - rx_im * pot_re
        for at in range(0, CHUNK, 128):
            acc_re += real[:, at : at + 128]
            acc_im += imag[:, at : at + 128]
    ones = jnp.ones((8, 128), BF16)
    out = []
    for acc in (acc_re, acc_im):
        high, low = split(acc)
        out.append((dot_t(ones, high) + dot_t(ones, low))[0:1])
    out_ref[...] = jnp.concatenate(out, 0)


def params(mib):
    return pltpu.CompilerParams(vmem_limit_bytes=mib * 1024 * 1024)


def cost(rows):
    return pl.CostEstimate(flops=2 * rows * 2 * NMU * NG, bytes_accessed=4 * NMU * NG, transcendentals=0)


def pair_call(from_core, a_near, a_pair, b_pays, weights, basis, after):
    return pl.pallas_call(
        functools.partial(pair_kernel, from_core),
        in_specs=[VMEM] * 8 + [ANY],
        out_specs=VMEM,
        out_shape=jax.ShapeDtypeStruct((8, 128), F32),
        scratch_shapes=[
            pltpu.VMEM((4 * ROWS, 2 * NMU), BF16),
            pltpu.VMEM((2, 64, NMU), F32),
            pltpu.VMEM((4, 64, NMU), F32),
            pltpu.VMEM((ROWS, 2 * ROWS), F32),
            pltpu.VMEM((ROWS, 2 * CHUNK), BF16),
            pltpu.VMEM((2 * ROWS, 2 * CHUNK), BF16),
        ],
        compiler_params=params(24),
        cost_estimate=cost(4 * ROWS),
    )(a_near, a_pair, *b_pays, weights, basis, after)


def on_device(waves, vector, energies, basis, screening, coulomb, qmap):
    basis = basis.reshape(2 * NMU, NG)
    pay = pl.pallas_call(
        pack_kernel,
        in_specs=[VMEM] * 2,
        out_specs=VMEM,
        out_shape=jax.ShapeDtypeStruct((16, WIDTH), BF16),
    )(waves.reshape(16, NMU), vector.reshape(2, NT))
    b0 = move(pay, step=1)
    a1 = move(pay, far=1)
    where = jnp.stack([lax.axis_index("grp"), lax.axis_index("kin")]).astype(jnp.int32)
    rx, far_weights, near_weights = pl.pallas_call(
        own_kernel,
        in_specs=[SMEM, SMEM, VMEM, VMEM, ANY],
        out_specs=[VMEM] * 3,
        out_shape=[
            jax.ShapeDtypeStruct((32, NG), F32),
            jax.ShapeDtypeStruct((8, NG), F32),
            jax.ShapeDtypeStruct((8, NG), F32),
        ],
        scratch_shapes=[pltpu.VMEM((32, 2 * NMU), BF16), pltpu.SemaphoreType.DMA((16,))],
        compiler_params=params(24),
        cost_estimate=cost(128),
    )(where, qmap, pay, basis, screening)
    b2 = move(b0, y=2)
    b1 = move(b0, y=1)
    b3 = move(b0, y=3)
    a23 = move(jnp.concatenate([pay, a1], 0), core=1)
    y = pl.pallas_call(
        transitions_kernel,
        in_specs=[VMEM] * 3,
        out_specs=VMEM,
        out_shape=jax.ShapeDtypeStruct((2, NMU), F32),
    )(pay, a1, a23)
    b_pays = (b0, b1, b2, b3)
    far_out = pair_call(16, a1, a23, b_pays, far_weights, basis, y)
    y = y + move(y, y=2) + move(y, y=1) + move(y, y=3)
    near_out = pair_call(0, pay, a23, b_pays, near_weights, basis, y)
    y = y + move(y, x=2) + move(y, x=1) + move(y, x=3)
    others = [move(y, z=n) for n in (2, 1, 3)]
    exchange = pl.pallas_call(
        exchange_kernel,
        in_specs=[VMEM] * 7,
        out_specs=VMEM,
        out_shape=jax.ShapeDtypeStruct((2, NT), F32),
        scratch_shapes=[pltpu.VMEM((16, 2 * NMU), BF16)],
        compiler_params=params(24),
        cost_estimate=cost(128),
    )(y, *others, coulomb.reshape(1, NG), rx, basis)

    far_sum = far_out[0:1] + move(far_out[1:2], core=1)
    herm = far_out[4:8] + near_out[4:8]
    herm = herm[0:1] + move(herm[2:3], y=2) + move(herm[1:2], y=1) + move(herm[3:4], y=3)
    terms = near_out[0:1] + move(near_out[1:2], core=1) + move(far_sum, far=1) + move(herm, step=3)
    terms = terms[:, 0:32].reshape(1, 2, NT)
    scale = jnp.float32(1.0 / 256)
    return energies[:, None, :] * vector + 2.0 * scale * exchange[None] - scale * terms


def solution(mesh):
    return jax.shard_map(
        on_device,
        mesh=mesh,
        in_specs=(
            P(("grp", "kin"), None, None, None),
            P(("grp", "kin"), None, None),
            P(("grp", "kin"), None),
            P(),
            P(),
            P(),
            P(("grp", "kin"), None),
        ),
        out_specs=P(("grp", "kin"), None, None),
        check_vma=False,
    )
```

```python
import functools

import jax
import jax.numpy as jnp
from jax import lax
from jax.experimental import pallas as pl
from jax.experimental.pallas import tpu as pltpu
from jax.sharding import PartitionSpec as P

NT = 16
NMU = 1024
NG = 1536
WIDTH = NMU + 128
CHUNK = 512
ROWS = 128
F32 = jnp.float32
BF16 = jnp.bfloat16
VMEM = pl.BlockSpec(memory_space=pltpu.VMEM)
SMEM = pl.BlockSpec(memory_space=pltpu.SMEM)
ANY = pl.BlockSpec(memory_space=pl.ANY)


def move(value, x=0, z=0, far=0, y=0, core=0, step=0):
    pairs = []
    for a in range(4):
        for b in range(4):
            for c in range(2):
                for d in range(4):
                    for e in range(2):
                        source = (a * 4 + b) * 16 + c * 8 + d * 2 + e
                        group = (((a + step) % 4) ^ x) * 4 + (b ^ z)
                        member = (c ^ far) * 8 + (d ^ y) * 2 + (e ^ core)
                        pairs.append((source, group * 16 + member))
    return lax.ppermute(value, ("grp", "kin"), pairs)


def iota(shape, dim):
    return lax.broadcasted_iota(jnp.int32, shape, dim)


def dot(left, right):
    return jnp.dot(left, right, preferred_element_type=F32)


def dot_t(left, right):
    return lax.dot_general(left, right, (((1,), (1,)), ((), ())), preferred_element_type=F32)


def split(value):
    high = value.astype(BF16)
    return high, (value - high.astype(F32)).astype(BF16)


def dot_split(left, right):
    high, low = split(left)
    return dot(high, right) + dot(low, right)


def onehot(condition):
    return jnp.where(condition, 1.0, 0.0).astype(BF16)


def spread(repeat):
    row = iota((64, 16), 0)
    col = iota((64, 16), 1)
    band = (row >> 2) & 3 if repeat else row & 3
    base = jnp.where(row < 32, 4, 0) + jnp.where((row >> 4) & 1 == 1, 8, 0)
    return onehot(col == band + base)


def conj_product(left_re, left_im, right_re, right_im):
    real = (left_re * right_re + left_im * right_im).astype(BF16)
    imag = (left_re * right_im - left_im * right_re).astype(BF16)
    return real, imag


def pack_kernel(waves_ref, vector_ref, pay_ref):
    coarse = vector_ref[...].astype(BF16).astype(F32)
    real = jnp.broadcast_to(coarse[0:1], (16, 16))
    imag = jnp.broadcast_to(coarse[1:2], (16, 16))
    row = iota((16, 16), 0)
    lane = iota((16, 16), 1)
    of_v = lane >> 2 == row & 3
    by_c = onehot(row & 3 == lane & 3)
    real_v = dot(jnp.where(of_v, real, 0.0).astype(BF16), by_c)
    imag_v = dot(jnp.where(of_v, imag, 0.0).astype(BF16), by_c)
    upper = row < 8
    first = jnp.where(upper, real_v, imag_v)
    second = jnp.where(upper, -imag_v, real_v)
    mixer = jnp.where(lane & 8 == 0, first, second)
    mixer = jnp.where((row & 4 == 0) & (lane & 4 == 4), mixer, 0.0).astype(BF16)
    line_re = jnp.where(row == 12, real, 0.0).astype(BF16)
    line_im = jnp.where(row == 12, imag, 0.0).astype(BF16)
    row = iota((16, 128), 0)
    lane = iota((16, 128), 1)
    block = dot(mixer, onehot(lane == row)) + dot(line_re, onehot(lane == row + 16)) + dot(line_im, onehot(lane == row + 32))
    pay_ref[:, 0:NMU] = waves_ref[...]
    pay_ref[:, NMU:WIDTH] = block.astype(BF16)


def fetch_kernel(where_ref, qmap_ref, basis, screening, z_ref, w_ref, sems):
    whole = pltpu.make_async_copy(basis, z_ref, sems.at[16])
    whole.start()
    own = where_ref[0]
    member = where_ref[1]
    partner = (own + 12) & 15
    steps = []
    for m, flip in enumerate((8, 9, 0, 1)):
        from_a = qmap_ref[0, own * 16 + (member ^ flip)]
        for n in range(4):
            from_b = qmap_ref[0, partner * 16 + (member ^ (2 * n))]
            index = (((from_b >> 4) - (from_a >> 4)) & 15) * 16 + ((from_b - from_a) & 15)
            at = m * 4 + n
            copy = pltpu.make_async_copy(screening.at[pl.ds(index, 1)], w_ref.at[pl.ds(at, 1)], sems.at[at])
            copy.start()
            steps.append(copy)
    for copy in steps:
        copy.wait()
    whole.wait()


def transitions_kernel(a0, a1, a2, a3, b0, b1, b2, b3, y_ref, a_ref, b_ref, sems):
    steps = []
    for n, source in enumerate((a1, a3, a0, a2, b0, b1, b2, b3)):
        target = a_ref if n < 4 else b_ref
        copy = pltpu.make_async_copy(source, target.at[pl.ds(n % 4 * 16, 16)], sems.at[n])
        copy.start()
        steps.append(copy)
    for copy in steps[:4]:
        copy.wait()
    total_re = jnp.zeros((8, NMU), F32)
    total_im = jnp.zeros((8, NMU), F32)
    for m in range(4):
        waves = a_ref[m * 16 : m * 16 + 16, 0:NMU]
        mixed = dot(a_ref[m * 16 : m * 16 + 16, NMU : NMU + 16], waves)
        waves = waves.astype(F32)
        val_re, val_im = waves[0:8], waves[8:16]
        mix_re, mix_im = mixed[0:8], mixed[8:16]
        total_re += val_re * mix_re + val_im * mix_im
        total_im += val_re * mix_im - val_im * mix_re
    total_re = jnp.sum(total_re, 0, keepdims=True)
    total_im = jnp.sum(total_im, 0, keepdims=True)
    for j in range(8):
        y_ref[j : j + 1] = total_re[:, j * 128 : j * 128 + 128]
        y_ref[8 + j : 9 + j] = total_im[:, j * 128 : j * 128 + 128]
    for copy in steps[4:]:
        copy.wait()


def pair_kernel(near, *refs):
    if near:
        a_ref, b_ref, w_ref, z_ref, far_ref, _, out_ref, rx_ref, lhs, own, xa, xb, acc, ca, cb = refs
    else:
        a_ref, b_ref, w_ref, z_ref, out_ref, lhs, xa, xb, acc, ca, cb = refs
    base = 2 * near
    a_pays = [a_ref[(base + m) * 16 : (base + m) * 16 + 16] for m in range(2)]
    b_pays = [b_ref[n * 16 : n * 16 + 16] for n in range(4)]
    half = 2 * ROWS

    def put(to, row, top, left, right, left_at, right_at):
        real, imag = conj_product(
            left[left_at : left_at + 16],
            left[left_at + 16 : left_at + 32],
            right[right_at : right_at + 16],
            right[right_at + 16 : right_at + 32],
        )
        to[row : row + 16, 0:NMU] = real
        to[row : row + 16, NMU : 2 * NMU] = -imag
        to[top + row : top + row + 16, 0:NMU] = imag
        to[top + row : top + row + 16, NMU : 2 * NMU] = real

    rep = spread(True)
    til = spread(False)
    for m in range(2):
        xa[m] = dot(rep, a_pays[m][:, 0:NMU])
    for n in range(4):
        xb[n] = dot(til, b_pays[n][:, 0:NMU])
    for m in range(2):
        for n in range(4):
            row = (m * 4 + n) * 16
            put(lhs, row, half, xa[m], xb[n], 0, 0)
            put(lhs, ROWS + row, half, xa[m], xb[n], 32, 32)
    if near:
        put(own, 0, 16, xa[0], dot(til, a_pays[0][:, 0:NMU]), 32, 0)
    acc[...] = jnp.zeros_like(acc)
    for at in range(0, NG, CHUNK):
        z = z_ref[:, at : at + CHUNK]
        con_re = dot(lhs[0:ROWS], z)
        for p in range(8):
            weight = w_ref[4 * base + p : 4 * base + p + 1, at : at + CHUNK]
            ca[p * 16 : p * 16 + 16, 0:CHUNK] = (con_re[p * 16 : p * 16 + 16] * weight).astype(BF16)
        con_im = dot(lhs[half : half + ROWS], z)
        for p in range(8):
            weight = w_ref[4 * base + p : 4 * base + p + 1, at : at + CHUNK]
            ca[p * 16 : p * 16 + 16, CHUNK : 2 * CHUNK] = (con_im[p * 16 : p * 16 + 16] * weight).astype(BF16)
        val_re = dot(lhs[ROWS:half], z).astype(BF16)
        cb[0:ROWS, 0:CHUNK] = val_re
        cb[ROWS:half, CHUNK : 2 * CHUNK] = -val_re
        val_im = dot(lhs[half + ROWS : 2 * half], z).astype(BF16)
        cb[0:ROWS, CHUNK : 2 * CHUNK] = val_im
        cb[ROWS:half, 0:CHUNK] = val_im
        acc[...] += dot_t(ca[...], cb[...])
        if near:
            rx_ref[:, at : at + CHUNK] = dot(own[...], z)

    pick_row = iota((8, 16), 0)
    pick_col = iota((8, 16), 1)
    xv_a = jnp.zeros((8, 128), F32)
    xv_b = jnp.zeros((8, 128), F32)
    for m in range(2):
        xv_a += dot(onehot((pick_row == m) & (pick_col == 12)), a_pays[m][:, NMU:WIDTH])
    for n in range(4):
        xv_b += dot(onehot((pick_row == n) & (pick_col == 12)), b_pays[n][:, NMU:WIDTH])
    row = iota((ROWS, 8), 0)
    col = iota((ROWS, 8), 1)
    of_a = onehot(row >> 6 == col)
    of_b = onehot((row >> 4) & 3 == col)
    row = iota((ROWS, 128), 0)
    lane = iota((ROWS, 128), 1)
    same_c = lane & 3 == (row >> 2) & 3
    same_d = lane & 3 == row & 3
    spread_a = jnp.where(same_c, dot(of_a, xv_a.astype(BF16)), 0.0).astype(BF16)
    spread_b = jnp.where(same_d, dot(of_b, xv_b.astype(BF16)), 0.0).astype(BF16)
    lane = iota((128, ROWS), 0)
    col = iota((128, ROWS), 1)
    by_w = (lane >> 2) & 3 == col & 3
    by_v = (lane >> 2) & 3 == (col >> 2) & 3
    first = lane >> 4 == 1
    second = lane >> 4 == 2
    pair = iota((ROWS, ROWS), 0) >> 4 == iota((ROWS, ROWS), 1) >> 4
    k_re = jnp.where(pair, acc[:, 0:ROWS], 0.0)
    k_im = jnp.where(pair, acc[:, ROWS:half], 0.0)
    xd_re = dot(spread_b, onehot(by_w & first))
    xd_im = dot(spread_b, onehot(by_w & second))
    xh_re = dot(spread_a, onehot(by_v & first))
    xh_im = dot(spread_a, onehot(by_v & second))
    lane = iota((ROWS, 128), 1)
    col = iota((ROWS, 128), 0)
    by_w = (lane >> 2) & 3 == col & 3
    by_v = (lane >> 2) & 3 == (col >> 2) & 3
    first = lane >> 4 == 0
    second = lane >> 4 == 1
    sum_d = dot_split(k_re * xd_re - k_im * xd_im, onehot(by_v & first)) + dot_split(
        k_re * xd_im + k_im * xd_re, onehot(by_v & second)
    )
    sum_h = dot_split(k_re * xh_re + k_im * xh_im, onehot(by_w & first)) + dot_split(
        k_re * xh_im - k_im * xh_re, onehot(by_w & second)
    )
    sum_d = jnp.where(same_c, sum_d, 0.0)
    sum_h = jnp.where(same_d, sum_h, 0.0)
    row = iota((8, ROWS), 0)
    col = iota((8, ROWS), 1)
    to_a = onehot(row == col >> 6)
    to_b = onehot(row == 4 + ((col >> 4) & 3))
    high_d, low_d = split(sum_d)
    high_h, low_h = split(sum_h)
    total = dot(to_a, high_d) + dot(to_a, low_d) + dot(to_b, high_h) + dot(to_b, low_h)
    if near:
        total += jnp.where(iota((8, 128), 0) >= 4, far_ref[...], 0.0)
    out_ref[...] = total


def mail_kernel(y0, y1, y2, y3, out_ref, *mails):
    total = y0[...] + y1[...] + y2[...] + y3[...]
    for n, mail in enumerate(mails):
        mail[0:16] = total
        mail[16:24] = jnp.broadcast_to(out_ref[4 + n : 5 + n], (8, 128))


def exchange_kernel(y_ref, c_ref, rx_ref, z_ref, out_ref, lhs):
    pad = jnp.zeros((12, 128), F32)
    for j in range(8):
        real = y_ref[j : j + 1]
        imag = y_ref[8 + j : 9 + j]
        for at, top, bottom in ((0, real, imag), (NMU, -imag, real)):
            high, low = split(jnp.concatenate([top, bottom], 0))
            rows = jnp.concatenate([high.astype(F32), low.astype(F32), pad], 0)
            lhs[:, at + j * 128 : at + j * 128 + 128] = rows.astype(BF16)
    acc_re = jnp.zeros((16, 128), F32)
    acc_im = jnp.zeros((16, 128), F32)
    for start in range(0, NG, CHUNK):
        part = pl.ds(start, CHUNK)
        total = dot(lhs[...], z_ref[:, part])
        pot_re = (total[0:1] + total[2:3]) * c_ref[:, part]
        pot_im = (total[1:2] + total[3:4]) * c_ref[:, part]
        rx_re = rx_ref[0:16, part]
        rx_im = rx_ref[16:32, part]
        real = rx_re * pot_re + rx_im * pot_im
        imag = rx_re * pot_im - rx_im * pot_re
        for at in range(0, CHUNK, 128):
            acc_re += real[:, at : at + 128]
            acc_im += imag[:, at : at + 128]
    ones = jnp.ones((8, 128), BF16)
    out = []
    for acc in (acc_re, acc_im):
        high, low = split(acc)
        out.append((dot_t(ones, high) + dot_t(ones, low))[0:1])
    out_ref[...] = jnp.concatenate(out, 0)


def params(mib):
    return pltpu.CompilerParams(vmem_limit_bytes=mib * 1024 * 1024)


def cost(rows):
    return pl.CostEstimate(flops=2 * rows * 2 * NMU * NG, bytes_accessed=4 * NMU * NG, transcendentals=0)


def pair_call(near, operands):
    scratch = [pltpu.VMEM((4 * ROWS, 2 * NMU), BF16)]
    out_shape = [jax.ShapeDtypeStruct((8, 128), F32)]
    if near:
        scratch.append(pltpu.VMEM((32, 2 * NMU), BF16))
        out_shape.append(pltpu.VMEM((32, NG), F32))
    return pl.pallas_call(
        functools.partial(pair_kernel, near),
        in_specs=[VMEM] * 4 + [VMEM, ANY] * near,
        out_specs=[VMEM] * len(out_shape),
        out_shape=out_shape,
        scratch_shapes=scratch
        + [
            pltpu.VMEM((2, 64, NMU), F32),
            pltpu.VMEM((4, 64, NMU), F32),
            pltpu.VMEM((ROWS, 2 * ROWS), F32),
            pltpu.VMEM((ROWS, 2 * CHUNK), BF16),
            pltpu.VMEM((2 * ROWS, 2 * CHUNK), BF16),
        ],
        compiler_params=params(24),
        cost_estimate=cost(4 * ROWS),
    )(*operands)


def on_device(waves, vector, energies, basis, screening, coulomb, qmap):
    pay = pl.pallas_call(
        pack_kernel,
        in_specs=[VMEM] * 2,
        out_specs=VMEM,
        out_shape=jax.ShapeDtypeStruct((16, WIDTH), BF16),
    )(waves.reshape(16, NMU), vector.reshape(2, NT))
    a1 = move(pay, far=1)
    b0 = move(pay, step=1)
    a2 = move(pay, core=1)
    where = jnp.stack([lax.axis_index("grp"), lax.axis_index("kin")]).astype(jnp.int32)
    z, weights = pl.pallas_call(
        fetch_kernel,
        in_specs=[SMEM, SMEM, ANY, ANY],
        out_specs=[VMEM] * 2,
        out_shape=[pltpu.VMEM((2 * NMU, NG), BF16), pltpu.VMEM((16, NG), F32)],
        scratch_shapes=[pltpu.SemaphoreType.DMA((17,))],
        compiler_params=params(50),
        cost_estimate=cost(128),
    )(where, qmap, basis.reshape(2 * NMU, NG), screening)
    b1, b2, b3 = (move(b0, y=n) for n in (1, 2, 3))
    a3 = move(a1, core=1)
    y, a_all, b_all = pl.pallas_call(
        transitions_kernel,
        in_specs=[ANY] * 8,
        out_specs=[VMEM] * 3,
        out_shape=[
            jax.ShapeDtypeStruct((16, 128), F32),
            pltpu.VMEM((64, WIDTH), BF16),
            pltpu.VMEM((64, WIDTH), BF16),
        ],
        scratch_shapes=[pltpu.SemaphoreType.DMA((8,))],
    )(pay, a1, a2, a3, b0, b1, b2, b3)
    (far_out,) = pair_call(0, (a_all, b_all, weights, z))
    far_sum = far_out[0:1] + move(far_out[1:2], core=1)
    y = y + move(y, z=2) + move(y, z=1) + move(y, z=3)
    near_out, rx = pair_call(1, (a_all, b_all, weights, z, far_out, y))
    mail = pl.pallas_call(
        mail_kernel,
        in_specs=[VMEM] * 5,
        out_specs=[VMEM] * 4,
        out_shape=[jax.ShapeDtypeStruct((24, 128), F32)] * 4,
    )(y, *(move(y, x=n) for n in (2, 1, 3)), near_out)
    mail = mail[0] + move(mail[2], y=2) + move(mail[1], y=1) + move(mail[3], y=3)
    exchange = pl.pallas_call(
        exchange_kernel,
        in_specs=[VMEM] * 4,
        out_specs=VMEM,
        out_shape=jax.ShapeDtypeStruct((2, NT), F32),
        scratch_shapes=[pltpu.VMEM((16, 2 * NMU), BF16)],
        compiler_params=params(24),
        cost_estimate=cost(128),
    )(mail, coulomb.reshape(1, NG), rx, z)

    terms = (
        near_out[0:1]
        + move(near_out[1:2], core=1)
        + move(far_sum, far=1)
        + move(mail[16:17], step=3)
    )
    terms = terms[:, 0:32].reshape(1, 2, NT)
    scale = jnp.float32(1.0 / 256)
    return energies[:, None, :] * vector + 2.0 * scale * exchange[None] - scale * terms


def solution(mesh):
    return jax.shard_map(
        on_device,
        mesh=mesh,
        in_specs=(
            P(("grp", "kin"), None, None, None),
            P(("grp", "kin"), None, None),
            P(("grp", "kin"), None),
            P(),
            P(),
            P(),
            P(("grp", "kin"), None),
        ),
        out_specs=P(("grp", "kin"), None, None),
        check_vma=False,
    )
```

```python
import functools

import jax
import jax.numpy as jnp
from jax import lax
from jax.experimental import pallas as pl
from jax.experimental.pallas import tpu as pltpu
from jax.sharding import PartitionSpec as P

NT = 16
NMU = 1024
NG = 1536
WIDTH = NMU + 128
CHUNK = 512
ROWS = 128
F32 = jnp.float32
BF16 = jnp.bfloat16
VMEM = pl.BlockSpec(memory_space=pltpu.VMEM)
SMEM = pl.BlockSpec(memory_space=pltpu.SMEM)
ANY = pl.BlockSpec(memory_space=pl.ANY)


def move(value, x=0, z=0, far=0, y=0, core=0, step=0):
    pairs = []
    for a in range(4):
        for b in range(4):
            for c in range(2):
                for d in range(4):
                    for e in range(2):
                        source = (a * 4 + b) * 16 + c * 8 + d * 2 + e
                        group = (((a + step) % 4) ^ x) * 4 + (b ^ z)
                        member = (c ^ far) * 8 + (d ^ y) * 2 + (e ^ core)
                        pairs.append((source, group * 16 + member))
    return lax.ppermute(value, ("grp", "kin"), pairs)


def iota(shape, dim):
    return lax.broadcasted_iota(jnp.int32, shape, dim)


def dot(left, right):
    return jnp.dot(left, right, preferred_element_type=F32)


def dot_t(left, right):
    return lax.dot_general(left, right, (((1,), (1,)), ((), ())), preferred_element_type=F32)


def split(value):
    high = value.astype(BF16)
    return high, (value - high.astype(F32)).astype(BF16)


def dot_split(left, right):
    high, low = split(left)
    return dot(high, right) + dot(low, right)


def onehot(condition):
    return jnp.where(condition, 1.0, 0.0).astype(BF16)


def spread(repeat):
    row = iota((64, 16), 0)
    col = iota((64, 16), 1)
    band = (row >> 2) & 3 if repeat else row & 3
    base = jnp.where(row < 32, 4, 0) + jnp.where((row >> 4) & 1 == 1, 8, 0)
    return onehot(col == band + base)


def conj_product(left_re, left_im, right_re, right_im):
    real = (left_re * right_re + left_im * right_im).astype(BF16)
    imag = (left_re * right_im - left_im * right_re).astype(BF16)
    return real, imag


def pack_kernel(waves, vector, pay_ref, vector_ref, sems):
    copies = (
        pltpu.make_async_copy(vector, vector_ref, sems.at[0]),
        pltpu.make_async_copy(waves, pay_ref.at[:, pl.ds(0, NMU)], sems.at[1]),
    )
    for copy in copies:
        copy.start()
    copies[0].wait()
    coarse = vector_ref[...].astype(BF16).astype(F32)
    real = jnp.broadcast_to(coarse[0:1], (16, 16))
    imag = jnp.broadcast_to(coarse[1:2], (16, 16))
    row = iota((16, 16), 0)
    lane = iota((16, 16), 1)
    of_v = lane >> 2 == row & 3
    by_c = onehot(row & 3 == lane & 3)
    real_v = dot(jnp.where(of_v, real, 0.0).astype(BF16), by_c)
    imag_v = dot(jnp.where(of_v, imag, 0.0).astype(BF16), by_c)
    upper = row < 8
    first = jnp.where(upper, real_v, imag_v)
    second = jnp.where(upper, -imag_v, real_v)
    mixer = jnp.where(lane & 8 == 0, first, second)
    mixer = jnp.where((row & 4 == 0) & (lane & 4 == 4), mixer, 0.0).astype(BF16)
    line_re = jnp.where(row == 12, real, 0.0).astype(BF16)
    line_im = jnp.where(row == 12, imag, 0.0).astype(BF16)
    row = iota((16, 128), 0)
    lane = iota((16, 128), 1)
    block = dot(mixer, onehot(lane == row)) + dot(line_re, onehot(lane == row + 16)) + dot(line_im, onehot(lane == row + 32))
    pay_ref[:, NMU:WIDTH] = block.astype(BF16)
    copies[1].wait()


def fetch_kernel(where_ref, qmap_ref, basis, screening, z_ref, w_ref, sems):
    whole = pltpu.make_async_copy(basis, z_ref, sems.at[16])
    whole.start()
    own = where_ref[0]
    member = where_ref[1]
    partner = (own + 12) & 15
    steps = []
    for m, flip in enumerate((8, 9, 0, 1)):
        from_a = qmap_ref[0, own * 16 + (member ^ flip)]
        for n in range(4):
            from_b = qmap_ref[0, partner * 16 + (member ^ (2 * n))]
            index = (((from_b >> 4) - (from_a >> 4)) & 15) * 16 + ((from_b - from_a) & 15)
            at = m * 4 + n
            copy = pltpu.make_async_copy(screening.at[pl.ds(index, 1)], w_ref.at[pl.ds(at, 1)], sems.at[at])
            copy.start()
            steps.append(copy)
    for copy in steps:
        copy.wait()
    whole.wait()


def transitions_kernel(a0, a1, a2, a3, y_ref):
    total_re = jnp.zeros((8, NMU), F32)
    total_im = jnp.zeros((8, NMU), F32)
    for pay in (a0, a1, a2, a3):
        waves = pay[:, 0:NMU]
        mixed = dot(pay[:, NMU : NMU + 16], waves)
        waves = waves.astype(F32)
        val_re, val_im = waves[0:8], waves[8:16]
        mix_re, mix_im = mixed[0:8], mixed[8:16]
        total_re += val_re * mix_re + val_im * mix_im
        total_im += val_re * mix_im - val_im * mix_re
    total_re = jnp.sum(total_re, 0, keepdims=True)
    total_im = jnp.sum(total_im, 0, keepdims=True)
    for j in range(8):
        y_ref[j : j + 1] = total_re[:, j * 128 : j * 128 + 128]
        y_ref[8 + j : 9 + j] = total_im[:, j * 128 : j * 128 + 128]


def pair_kernel(near, *refs):
    if near:
        w_ref, z_ref, far_ref, _, out_ref, rx_ref, lhs, own, xa, xb, acc, ca, cb = refs[6:]
    else:
        w_ref, z_ref, _, out_ref, lhs, xa, xb, acc, ca, cb = refs[6:]
    base = 2 * near
    a_pays = refs[0:2]
    b_pays = refs[2:6]
    half = 2 * ROWS

    def put(to, row, top, left, right, left_at, right_at):
        real, imag = conj_product(
            left[left_at : left_at + 16],
            left[left_at + 16 : left_at + 32],
            right[right_at : right_at + 16],
            right[right_at + 16 : right_at + 32],
        )
        to[row : row + 16, 0:NMU] = real
        to[row : row + 16, NMU : 2 * NMU] = -imag
        to[top + row : top + row + 16, 0:NMU] = imag
        to[top + row : top + row + 16, NMU : 2 * NMU] = real

    rep = spread(True)
    til = spread(False)
    for m in range(2):
        xa[m] = dot(rep, a_pays[m][:, 0:NMU])
    for n in range(4):
        xb[n] = dot(til, b_pays[n][:, 0:NMU])
    for m in range(2):
        for n in range(4):
            row = (m * 4 + n) * 16
            put(lhs, row, half, xa[m], xb[n], 0, 0)
            put(lhs, ROWS + row, half, xa[m], xb[n], 32, 32)
    if near:
        put(own, 0, 16, xa[0], dot(til, a_pays[0][:, 0:NMU]), 32, 0)
    acc[...] = jnp.zeros_like(acc)
    for at in range(0, NG, CHUNK):
        z = z_ref[:, at : at + CHUNK]
        con_re = dot(lhs[0:ROWS], z)
        for p in range(8):
            weight = w_ref[4 * base + p : 4 * base + p + 1, at : at + CHUNK]
            ca[p * 16 : p * 16 + 16, 0:CHUNK] = (con_re[p * 16 : p * 16 + 16] * weight).astype(BF16)
        con_im = dot(lhs[half : half + ROWS], z)
        for p in range(8):
            weight = w_ref[4 * base + p : 4 * base + p + 1, at : at + CHUNK]
            ca[p * 16 : p * 16 + 16, CHUNK : 2 * CHUNK] = (con_im[p * 16 : p * 16 + 16] * weight).astype(BF16)
        val_re = dot(lhs[ROWS:half], z).astype(BF16)
        cb[0:ROWS, 0:CHUNK] = val_re
        cb[ROWS:half, CHUNK : 2 * CHUNK] = -val_re
        val_im = dot(lhs[half + ROWS : 2 * half], z).astype(BF16)
        cb[0:ROWS, CHUNK : 2 * CHUNK] = val_im
        cb[ROWS:half, 0:CHUNK] = val_im
        acc[...] += dot_t(ca[...], cb[...])
        if near:
            rx_ref[:, at : at + CHUNK] = dot(own[...], z)

    pick_row = iota((8, 16), 0)
    pick_col = iota((8, 16), 1)
    xv_a = jnp.zeros((8, 128), F32)
    xv_b = jnp.zeros((8, 128), F32)
    for m in range(2):
        xv_a += dot(onehot((pick_row == m) & (pick_col == 12)), a_pays[m][:, NMU:WIDTH])
    for n in range(4):
        xv_b += dot(onehot((pick_row == n) & (pick_col == 12)), b_pays[n][:, NMU:WIDTH])
    row = iota((ROWS, 8), 0)
    col = iota((ROWS, 8), 1)
    of_a = onehot(row >> 6 == col)
    of_b = onehot((row >> 4) & 3 == col)
    row = iota((ROWS, 128), 0)
    lane = iota((ROWS, 128), 1)
    same_c = lane & 3 == (row >> 2) & 3
    same_d = lane & 3 == row & 3
    spread_a = jnp.where(same_c, dot(of_a, xv_a.astype(BF16)), 0.0).astype(BF16)
    spread_b = jnp.where(same_d, dot(of_b, xv_b.astype(BF16)), 0.0).astype(BF16)
    lane = iota((128, ROWS), 0)
    col = iota((128, ROWS), 1)
    by_w = (lane >> 2) & 3 == col & 3
    by_v = (lane >> 2) & 3 == (col >> 2) & 3
    first = lane >> 4 == 1
    second = lane >> 4 == 2
    pair = iota((ROWS, ROWS), 0) >> 4 == iota((ROWS, ROWS), 1) >> 4
    k_re = jnp.where(pair, acc[:, 0:ROWS], 0.0)
    k_im = jnp.where(pair, acc[:, ROWS:half], 0.0)
    xd_re = dot(spread_b, onehot(by_w & first))
    xd_im = dot(spread_b, onehot(by_w & second))
    xh_re = dot(spread_a, onehot(by_v & first))
    xh_im = dot(spread_a, onehot(by_v & second))
    lane = iota((ROWS, 128), 1)
    col = iota((ROWS, 128), 0)
    by_w = (lane >> 2) & 3 == col & 3
    by_v = (lane >> 2) & 3 == (col >> 2) & 3
    first = lane >> 4 == 0
    second = lane >> 4 == 1
    sum_d = dot_split(k_re * xd_re - k_im * xd_im, onehot(by_v & first)) + dot_split(
        k_re * xd_im + k_im * xd_re, onehot(by_v & second)
    )
    sum_h = dot_split(k_re * xh_re + k_im * xh_im, onehot(by_w & first)) + dot_split(
        k_re * xh_im - k_im * xh_re, onehot(by_w & second)
    )
    sum_d = jnp.where(same_c, sum_d, 0.0)
    sum_h = jnp.where(same_d, sum_h, 0.0)
    row = iota((8, ROWS), 0)
    col = iota((8, ROWS), 1)
    to_a = onehot(row == col >> 6)
    to_b = onehot(row == 4 + ((col >> 4) & 3))
    high_d, low_d = split(sum_d)
    high_h, low_h = split(sum_h)
    total = dot(to_a, high_d) + dot(to_a, low_d) + dot(to_b, high_h) + dot(to_b, low_h)
    if near:
        total += jnp.where(iota((8, 128), 0) >= 4, far_ref[...], 0.0)
    out_ref[...] = total


def mail_kernel(y0, y1, y2, y3, out_ref, *mails):
    total = y0[...] + y1[...] + y2[...] + y3[...]
    for n, mail in enumerate(mails):
        mail[0:16] = total
        mail[16:24] = jnp.broadcast_to(out_ref[4 + n : 5 + n], (8, 128))


def exchange_kernel(y_ref, c_ref, rx_ref, z_ref, out_ref, lhs):
    pad = jnp.zeros((12, 128), F32)
    for j in range(8):
        real = y_ref[j : j + 1]
        imag = y_ref[8 + j : 9 + j]
        for at, top, bottom in ((0, real, imag), (NMU, -imag, real)):
            high, low = split(jnp.concatenate([top, bottom], 0))
            rows = jnp.concatenate([high.astype(F32), low.astype(F32), pad], 0)
            lhs[:, at + j * 128 : at + j * 128 + 128] = rows.astype(BF16)
    acc_re = jnp.zeros((16, 128), F32)
    acc_im = jnp.zeros((16, 128), F32)
    for start in range(0, NG, CHUNK):
        part = pl.ds(start, CHUNK)
        total = dot(lhs[...], z_ref[:, part])
        pot_re = (total[0:1] + total[2:3]) * c_ref[:, part]
        pot_im = (total[1:2] + total[3:4]) * c_ref[:, part]
        rx_re = rx_ref[0:16, part]
        rx_im = rx_ref[16:32, part]
        real = rx_re * pot_re + rx_im * pot_im
        imag = rx_re * pot_im - rx_im * pot_re
        for at in range(0, CHUNK, 128):
            acc_re += real[:, at : at + 128]
            acc_im += imag[:, at : at + 128]
    ones = jnp.ones((8, 128), BF16)
    out = []
    for acc in (acc_re, acc_im):
        high, low = split(acc)
        out.append((dot_t(ones, high) + dot_t(ones, low))[0:1])
    out_ref[...] = jnp.concatenate(out, 0)


def final_kernel(energy_ref, vector_ref, exchange_ref, near_ref, d0, d1, d2, out_ref):
    scale = 1.0 / 256
    terms = near_ref[0:1] + d0[...] + d1[...] + d2[...]
    for part in range(2):
        term = terms[:, part * NT : part * NT + NT]
        out_ref[part : part + 1] = (
            energy_ref[...] * vector_ref[part : part + 1]
            + (2.0 * scale) * exchange_ref[part : part + 1]
            - scale * term
        )


def params(mib):
    return pltpu.CompilerParams(vmem_limit_bytes=mib * 1024 * 1024)


def cost(rows):
    return pl.CostEstimate(flops=2 * rows * 2 * NMU * NG, bytes_accessed=4 * NMU * NG, transcendentals=0)


def pair_call(near, operands):
    scratch = [pltpu.VMEM((4 * ROWS, 2 * NMU), BF16)]
    out_shape = [jax.ShapeDtypeStruct((8, 128), F32)]
    if near:
        scratch.append(pltpu.VMEM((32, 2 * NMU), BF16))
        out_shape.append(pltpu.VMEM((32, NG), F32))
    return pl.pallas_call(
        functools.partial(pair_kernel, near),
        in_specs=[VMEM] * 8 + [VMEM] * near + [ANY],
        out_specs=[VMEM] * len(out_shape),
        out_shape=out_shape,
        scratch_shapes=scratch
        + [
            pltpu.VMEM((2, 64, NMU), F32),
            pltpu.VMEM((4, 64, NMU), F32),
            pltpu.VMEM((ROWS, 2 * ROWS), F32),
            pltpu.VMEM((ROWS, 2 * CHUNK), BF16),
            pltpu.VMEM((2 * ROWS, 2 * CHUNK), BF16),
        ],
        compiler_params=params(24),
        cost_estimate=cost(4 * ROWS),
    )(*operands)


def on_device(waves, vector, energies, basis, screening, coulomb, qmap):
    pay = pl.pallas_call(
        pack_kernel,
        in_specs=[ANY] * 2,
        out_specs=VMEM,
        out_shape=pltpu.VMEM((16, WIDTH), BF16),
        scratch_shapes=[pltpu.VMEM((2, NT), F32), pltpu.SemaphoreType.DMA((2,))],
        compiler_params=params(56),
    )(waves.reshape(16, NMU), vector.reshape(2, NT))
    a1 = move(pay, far=1)
    b0 = move(pay, step=1)
    a2 = move(pay, core=1)
    where = jnp.stack([lax.axis_index("grp"), lax.axis_index("kin")]).astype(jnp.int32)
    z, weights = pl.pallas_call(
        fetch_kernel,
        in_specs=[SMEM, SMEM, ANY, ANY],
        out_specs=[VMEM] * 2,
        out_shape=[pltpu.VMEM((2 * NMU, NG), BF16), pltpu.VMEM((16, NG), F32)],
        scratch_shapes=[pltpu.SemaphoreType.DMA((17,))],
        compiler_params=params(50),
        cost_estimate=cost(128),
    )(where, qmap, basis.reshape(2 * NMU, NG), screening)
    b1, b2, b3 = (move(b0, y=n) for n in (1, 2, 3))
    a3 = move(a1, core=1)
    y = pl.pallas_call(
        transitions_kernel,
        in_specs=[VMEM] * 4,
        out_specs=VMEM,
        out_shape=jax.ShapeDtypeStruct((16, 128), F32),
        compiler_params=params(8),
    )(pay, a1, a2, a3)
    b_pays = (b0, b1, b2, b3)
    (far_out,) = pair_call(0, (a1, a3, *b_pays, weights, z, y))
    far_sum = far_out[0:1] + move(far_out[1:2], core=1)
    y = y + move(y, z=2) + move(y, z=1) + move(y, z=3)
    near_out, rx = pair_call(1, (pay, a2, *b_pays, weights, z, far_out, y))
    mail = pl.pallas_call(
        mail_kernel,
        in_specs=[VMEM] * 5,
        out_specs=[VMEM] * 4,
        out_shape=[jax.ShapeDtypeStruct((24, 128), F32)] * 4,
        compiler_params=params(4),
    )(y, *(move(y, x=n) for n in (2, 1, 3)), near_out)
    mail = mail[0] + move(mail[2], y=2) + move(mail[1], y=1) + move(mail[3], y=3)
    exchange = pl.pallas_call(
        exchange_kernel,
        in_specs=[VMEM] * 4,
        out_specs=VMEM,
        out_shape=jax.ShapeDtypeStruct((2, NT), F32),
        scratch_shapes=[pltpu.VMEM((16, 2 * NMU), BF16)],
        compiler_params=params(24),
        cost_estimate=cost(128),
    )(mail, coulomb.reshape(1, NG), rx, z)

    out = pl.pallas_call(
        final_kernel,
        in_specs=[VMEM] * 7,
        out_specs=VMEM,
        out_shape=jax.ShapeDtypeStruct((2, NT), F32),
        compiler_params=params(4),
    )(
        energies,
        vector.reshape(2, NT),
        exchange,
        near_out,
        move(near_out[1:2], core=1),
        move(far_sum, far=1),
        move(mail[16:17], step=3),
    )
    return out.reshape(1, 2, NT)


def solution(mesh):
    return jax.shard_map(
        on_device,
        mesh=mesh,
        in_specs=(
            P(("grp", "kin"), None, None, None),
            P(("grp", "kin"), None, None),
            P(("grp", "kin"), None),
            P(),
            P(),
            P(),
            P(("grp", "kin"), None),
        ),
        out_specs=P(("grp", "kin"), None, None),
        check_vma=False,
    )
```

```python
import functools

import jax
import jax.numpy as jnp
from jax import lax
from jax.experimental import pallas as pl
from jax.experimental.pallas import tpu as pltpu
from jax.sharding import PartitionSpec as P

NT = 16
NMU = 1024
NG = 1536
WIDTH = NMU + 128
PARTS = ((0, 256), (256, 512), (768, 512), (1280, 256))
CHUNK = 512
ROWS = 128
F32 = jnp.float32
BF16 = jnp.bfloat16
VMEM = pl.BlockSpec(memory_space=pltpu.VMEM)
SMEM = pl.BlockSpec(memory_space=pltpu.SMEM)
ANY = pl.BlockSpec(memory_space=pl.ANY)


def move(value, x=0, z=0, far=0, y=0, core=0, step=0):
    pairs = []
    for a in range(4):
        for b in range(4):
            for c in range(2):
                for d in range(4):
                    for e in range(2):
                        source = (a * 4 + b) * 16 + c * 8 + d * 2 + e
                        group = (((a + step) % 4) ^ x) * 4 + (b ^ z)
                        member = (c ^ far) * 8 + (d ^ y) * 2 + (e ^ core)
                        pairs.append((source, group * 16 + member))
    return lax.ppermute(value, ("grp", "kin"), pairs)


def iota(shape, dim):
    return lax.broadcasted_iota(jnp.int32, shape, dim)


def dot(left, right):
    return jnp.dot(left, right, preferred_element_type=F32)


def dot_t(left, right):
    return lax.dot_general(left, right, (((1,), (1,)), ((), ())), preferred_element_type=F32)


def split(value):
    high = value.astype(BF16)
    return high, (value - high.astype(F32)).astype(BF16)


def dot_split(left, right):
    high, low = split(left)
    return dot(high, right) + dot(low, right)


def onehot(condition):
    return jnp.where(condition, 1.0, 0.0).astype(BF16)


def spread(repeat):
    row = iota((64, 16), 0)
    col = iota((64, 16), 1)
    band = (row >> 2) & 3 if repeat else row & 3
    base = jnp.where(row < 32, 4, 0) + jnp.where((row >> 4) & 1 == 1, 8, 0)
    return onehot(col == band + base)


def conj_product(left_re, left_im, right_re, right_im):
    real = (left_re * right_re + left_im * right_im).astype(BF16)
    imag = (left_re * right_im - left_im * right_re).astype(BF16)
    return real, imag


def pack_kernel(waves, vector, pay_ref, vector_ref, sems):
    copies = (
        pltpu.make_async_copy(vector, vector_ref, sems.at[0]),
        pltpu.make_async_copy(waves, pay_ref.at[:, pl.ds(0, NMU)], sems.at[1]),
    )
    for copy in copies:
        copy.start()
    copies[0].wait()
    coarse = vector_ref[...].astype(BF16).astype(F32)
    real = jnp.broadcast_to(coarse[0:1], (16, 16))
    imag = jnp.broadcast_to(coarse[1:2], (16, 16))
    row = iota((16, 16), 0)
    lane = iota((16, 16), 1)
    of_v = lane >> 2 == row & 3
    by_c = onehot(row & 3 == lane & 3)
    real_v = dot(jnp.where(of_v, real, 0.0).astype(BF16), by_c)
    imag_v = dot(jnp.where(of_v, imag, 0.0).astype(BF16), by_c)
    upper = row < 8
    first = jnp.where(upper, real_v, imag_v)
    second = jnp.where(upper, -imag_v, real_v)
    mixer = jnp.where(lane & 8 == 0, first, second)
    mixer = jnp.where((row & 4 == 0) & (lane & 4 == 4), mixer, 0.0).astype(BF16)
    line_re = jnp.where(row == 12, real, 0.0).astype(BF16)
    line_im = jnp.where(row == 12, imag, 0.0).astype(BF16)
    row = iota((16, 128), 0)
    lane = iota((16, 128), 1)
    block = dot(mixer, onehot(lane == row)) + dot(line_re, onehot(lane == row + 16)) + dot(line_im, onehot(lane == row + 32))
    pay_ref[:, NMU:WIDTH] = block.astype(BF16)
    copies[1].wait()


def weights_kernel(where_ref, qmap_ref, screening, w_ref, sems):
    own = where_ref[0]
    member = where_ref[1]
    partner = (own + 12) & 15
    steps = []
    for m, flip in enumerate((8, 9, 0, 1)):
        from_a = qmap_ref[0, own * 16 + (member ^ flip)]
        for n in range(4):
            from_b = qmap_ref[0, partner * 16 + (member ^ (2 * n))]
            index = (((from_b >> 4) - (from_a >> 4)) & 15) * 16 + ((from_b - from_a) & 15)
            at = m * 4 + n
            copy = pltpu.make_async_copy(screening.at[pl.ds(index, 1)], w_ref.at[pl.ds(at, 1)], sems.at[at])
            copy.start()
            steps.append(copy)
    for copy in steps:
        copy.wait()


def transitions_kernel(*refs):
    y_ref = refs[8]
    for group in range(2):
        total_re = jnp.zeros((8, NMU), F32)
        total_im = jnp.zeros((8, NMU), F32)
        for pay in refs[group * 4 : group * 4 + 4]:
            waves = pay[:, 0:NMU]
            mixed = dot(pay[:, NMU : NMU + 16], waves)
            waves = waves.astype(F32)
            val_re, val_im = waves[0:8], waves[8:16]
            mix_re, mix_im = mixed[0:8], mixed[8:16]
            total_re += val_re * mix_re + val_im * mix_im
            total_im += val_re * mix_im - val_im * mix_re
        total_re = jnp.sum(total_re, 0, keepdims=True)
        total_im = jnp.sum(total_im, 0, keepdims=True)
        top = group * 16
        for j in range(8):
            y_ref[top + j : top + j + 1] = total_re[:, j * 128 : j * 128 + 128]
            y_ref[top + 8 + j : top + 9 + j] = total_im[:, j * 128 : j * 128 + 128]


def pair_kernel(near, *refs):
    if near:
        w_ref, z_ref, far_ref, _, out_ref, rx_ref, lhs, own, xa, xb, acc, ca, cb = refs[6:]
    else:
        w_ref, basis, _, out_ref, z_ref, lhs, xa, xb, acc, ca, cb, sems = refs[6:]
        copies = []
        for n, (at, width) in enumerate(PARTS):
            part = pl.ds(at, width)
            copies.append(pltpu.make_async_copy(basis.at[:, part], z_ref.at[:, part], sems.at[n]))
        for copy in copies:
            copy.start()
    base = 2 * near
    a_pays = refs[0:2]
    b_pays = refs[2:6]
    half = 2 * ROWS

    def put(to, row, top, left, right, left_at, right_at):
        real, imag = conj_product(
            left[left_at : left_at + 16],
            left[left_at + 16 : left_at + 32],
            right[right_at : right_at + 16],
            right[right_at + 16 : right_at + 32],
        )
        to[row : row + 16, 0:NMU] = real
        to[row : row + 16, NMU : 2 * NMU] = -imag
        to[top + row : top + row + 16, 0:NMU] = imag
        to[top + row : top + row + 16, NMU : 2 * NMU] = real

    rep = spread(True)
    til = spread(False)
    for m in range(2):
        xa[m] = dot(rep, a_pays[m][:, 0:NMU])
    for n in range(4):
        xb[n] = dot(til, b_pays[n][:, 0:NMU])
    for m in range(2):
        for n in range(4):
            row = (m * 4 + n) * 16
            put(lhs, row, half, xa[m], xb[n], 0, 0)
            put(lhs, ROWS + row, half, xa[m], xb[n], 32, 32)
    if near:
        put(own, 0, 16, xa[0], dot(til, a_pays[0][:, 0:NMU]), 32, 0)
    acc[...] = jnp.zeros_like(acc)
    for n, (at, width) in enumerate(PARTS):
        part = pl.ds(at, width)
        if not near:
            copies[n].wait()
        z = z_ref[:, part]
        con_re = dot(lhs[0:ROWS], z)
        for p in range(8):
            weight = w_ref[4 * base + p : 4 * base + p + 1, part]
            ca[p * 16 : p * 16 + 16, 0:width] = (con_re[p * 16 : p * 16 + 16] * weight).astype(BF16)
        con_im = dot(lhs[half : half + ROWS], z)
        for p in range(8):
            weight = w_ref[4 * base + p : 4 * base + p + 1, part]
            ca[p * 16 : p * 16 + 16, width : 2 * width] = (con_im[p * 16 : p * 16 + 16] * weight).astype(BF16)
        val_re = dot(lhs[ROWS:half], z).astype(BF16)
        cb[0:ROWS, 0:width] = val_re
        cb[ROWS:half, width : 2 * width] = -val_re
        val_im = dot(lhs[half + ROWS : 2 * half], z).astype(BF16)
        cb[0:ROWS, width : 2 * width] = val_im
        cb[ROWS:half, 0:width] = val_im
        acc[...] += dot_t(ca[:, 0 : 2 * width], cb[:, 0 : 2 * width])
        if near:
            rx_ref[:, part] = dot(own[...], z)

    pick_row = iota((8, 16), 0)
    pick_col = iota((8, 16), 1)
    xv_a = jnp.zeros((8, 128), F32)
    xv_b = jnp.zeros((8, 128), F32)
    for m in range(2):
        xv_a += dot(onehot((pick_row == m) & (pick_col == 12)), a_pays[m][:, NMU:WIDTH])
    for n in range(4):
        xv_b += dot(onehot((pick_row == n) & (pick_col == 12)), b_pays[n][:, NMU:WIDTH])
    row = iota((ROWS, 8), 0)
    col = iota((ROWS, 8), 1)
    of_a = onehot(row >> 6 == col)
    of_b = onehot((row >> 4) & 3 == col)
    row = iota((ROWS, 128), 0)
    lane = iota((ROWS, 128), 1)
    same_c = lane & 3 == (row >> 2) & 3
    same_d = lane & 3 == row & 3
    spread_a = jnp.where(same_c, dot(of_a, xv_a.astype(BF16)), 0.0).astype(BF16)
    spread_b = jnp.where(same_d, dot(of_b, xv_b.astype(BF16)), 0.0).astype(BF16)
    lane = iota((128, ROWS), 0)
    col = iota((128, ROWS), 1)
    by_w = (lane >> 2) & 3 == col & 3
    by_v = (lane >> 2) & 3 == (col >> 2) & 3
    first = lane >> 4 == 1
    second = lane >> 4 == 2
    pair = iota((ROWS, ROWS), 0) >> 4 == iota((ROWS, ROWS), 1) >> 4
    k_re = jnp.where(pair, acc[:, 0:ROWS], 0.0)
    k_im = jnp.where(pair, acc[:, ROWS:half], 0.0)
    xd_re = dot(spread_b, onehot(by_w & first))
    xd_im = dot(spread_b, onehot(by_w & second))
    xh_re = dot(spread_a, onehot(by_v & first))
    xh_im = dot(spread_a, onehot(by_v & second))
    lane = iota((ROWS, 128), 1)
    col = iota((ROWS, 128), 0)
    by_w = (lane >> 2) & 3 == col & 3
    by_v = (lane >> 2) & 3 == (col >> 2) & 3
    first = lane >> 4 == 0
    second = lane >> 4 == 1
    sum_d = dot_split(k_re * xd_re - k_im * xd_im, onehot(by_v & first)) + dot_split(
        k_re * xd_im + k_im * xd_re, onehot(by_v & second)
    )
    sum_h = dot_split(k_re * xh_re + k_im * xh_im, onehot(by_w & first)) + dot_split(
        k_re * xh_im - k_im * xh_re, onehot(by_w & second)
    )
    sum_d = jnp.where(same_c, sum_d, 0.0)
    sum_h = jnp.where(same_d, sum_h, 0.0)
    row = iota((8, ROWS), 0)
    col = iota((8, ROWS), 1)
    to_a = onehot(row == col >> 6)
    to_b = onehot(row == 4 + ((col >> 4) & 3))
    high_d, low_d = split(sum_d)
    high_h, low_h = split(sum_h)
    total = dot(to_a, high_d) + dot(to_a, low_d) + dot(to_b, high_h) + dot(to_b, low_h)
    if near:
        total += jnp.where(iota((8, 128), 0) >= 4, far_ref[...], 0.0)
    out_ref[...] = total


def mail_kernel(y0, y1, out_ref, *mails):
    total = y0[...] + y1[...]
    for n, mail in enumerate(mails):
        mail[0:16] = total[0:16] if n < 4 else total[16:32]
        row = 4 + n if n < 4 else 1
        mail[16:24] = jnp.broadcast_to(out_ref[row : row + 1], (8, 128))


def far_mail_kernel(m0, m1, d0, d1, mail):
    mail[0:16] = m0[0:16] + m1[0:16]
    mail[16:24] = jnp.broadcast_to(d0[0:1] + d1[...], (8, 128))


def exchange_kernel(y_ref, first_ref, second_ref, c_ref, rx_ref, z_ref, out_ref, lhs):
    y = y_ref[0:16] + first_ref[0:16] + second_ref[0:16]
    pad = jnp.zeros((12, 128), F32)
    for j in range(8):
        real = y[j : j + 1]
        imag = y[8 + j : 9 + j]
        for at, top, bottom in ((0, real, imag), (NMU, -imag, real)):
            high, low = split(jnp.concatenate([top, bottom], 0))
            rows = jnp.concatenate([high.astype(F32), low.astype(F32), pad], 0)
            lhs[:, at + j * 128 : at + j * 128 + 128] = rows.astype(BF16)
    acc_re = jnp.zeros((16, 128), F32)
    acc_im = jnp.zeros((16, 128), F32)
    for start in range(0, NG, CHUNK):
        part = pl.ds(start, CHUNK)
        total = dot(lhs[...], z_ref[:, part])
        pot_re = (total[0:1] + total[2:3]) * c_ref[:, part]
        pot_im = (total[1:2] + total[3:4]) * c_ref[:, part]
        rx_re = rx_ref[0:16, part]
        rx_im = rx_ref[16:32, part]
        real = rx_re * pot_re + rx_im * pot_im
        imag = rx_re * pot_im - rx_im * pot_re
        for at in range(0, CHUNK, 128):
            acc_re += real[:, at : at + 128]
            acc_im += imag[:, at : at + 128]
    ones = jnp.ones((8, 128), BF16)
    out = []
    for acc in (acc_re, acc_im):
        high, low = split(acc)
        out.append((dot_t(ones, high) + dot_t(ones, low))[0:1])
    out_ref[...] = jnp.concatenate(out, 0)


def final_kernel(energy_ref, vector_ref, exchange_ref, near_ref, core_ref, far_ref, herm_ref, out_ref):
    scale = 1.0 / 256
    terms = near_ref[0:1] + core_ref[16:17] + far_ref[16:17] + herm_ref[...]
    for part in range(2):
        term = terms[:, part * NT : part * NT + NT]
        out_ref[part : part + 1] = (
            energy_ref[...] * vector_ref[part : part + 1]
            + (2.0 * scale) * exchange_ref[part : part + 1]
            - scale * term
        )


def params(mib):
    return pltpu.CompilerParams(vmem_limit_bytes=mib * 1024 * 1024)


def cost(rows):
    return pl.CostEstimate(flops=2 * rows * 2 * NMU * NG, bytes_accessed=4 * NMU * NG, transcendentals=0)


def pair_call(near, operands):
    scratch = [pltpu.VMEM((4 * ROWS, 2 * NMU), BF16)]
    out_shape = [jax.ShapeDtypeStruct((8, 128), F32)]
    if near:
        scratch.append(pltpu.VMEM((32, 2 * NMU), BF16))
        out_shape.append(pltpu.VMEM((32, NG), F32))
    else:
        out_shape.append(pltpu.VMEM((2 * NMU, NG), BF16))
    return pl.pallas_call(
        functools.partial(pair_kernel, near),
        in_specs=[VMEM] * 7 + ([VMEM, VMEM, ANY] if near else [ANY, ANY]),
        out_specs=[VMEM] * 2,
        out_shape=out_shape,
        scratch_shapes=scratch
        + [
            pltpu.VMEM((2, 64, NMU), F32),
            pltpu.VMEM((4, 64, NMU), F32),
            pltpu.VMEM((ROWS, 2 * ROWS), F32),
            pltpu.VMEM((ROWS, 2 * CHUNK), BF16),
            pltpu.VMEM((2 * ROWS, 2 * CHUNK), BF16),
        ]
        + [pltpu.SemaphoreType.DMA((len(PARTS),))] * (1 - near),
        compiler_params=params(24 if near else 42),
        cost_estimate=cost(4 * ROWS),
    )(*operands)


def small_call(kernel, shapes, *operands):
    return pl.pallas_call(
        kernel,
        in_specs=[VMEM] * len(operands),
        out_specs=[VMEM] * len(shapes),
        out_shape=[jax.ShapeDtypeStruct(shape, F32) for shape in shapes],
        compiler_params=params(8),
    )(*operands)


def on_device(waves, vector, energies, basis, screening, coulomb, qmap):
    pay = pl.pallas_call(
        pack_kernel,
        in_specs=[ANY] * 2,
        out_specs=VMEM,
        out_shape=pltpu.VMEM((16, WIDTH), BF16),
        scratch_shapes=[pltpu.VMEM((2, NT), F32), pltpu.SemaphoreType.DMA((2,))],
        compiler_params=params(56),
    )(waves.reshape(16, NMU), vector.reshape(2, NT))
    b0 = move(pay, step=1)
    a1 = move(pay, far=1)
    a2 = move(pay, core=1)
    b1, b2, b3 = (move(b0, y=n) for n in (1, 2, 3))
    a3 = move(a1, core=1)
    where = jnp.stack([lax.axis_index("grp"), lax.axis_index("kin")]).astype(jnp.int32)
    weights = pl.pallas_call(
        weights_kernel,
        in_specs=[SMEM, SMEM, ANY],
        out_specs=VMEM,
        out_shape=pltpu.VMEM((16, NG), F32),
        scratch_shapes=[pltpu.SemaphoreType.DMA((16,))],
        compiler_params=params(56),
    )(where, qmap, screening)
    b_pays = (b0, b1, b2, b3)
    (y,) = small_call(transitions_kernel, [(32, 128)], pay, a1, a2, a3, *b_pays)
    far_out, z = pair_call(0, (a1, a3, *b_pays, weights, basis.reshape(2 * NMU, NG), y))
    y = y + move(y, z=2) + move(y, z=1) + move(y, z=3)
    near_out, rx = pair_call(1, (pay, a2, *b_pays, weights, z, far_out, y))
    mails = small_call(mail_kernel, [(24, 128)] * 5, y, move(y, x=2), near_out)
    core_mail = move(mails[4], core=1)
    (far_mail,) = small_call(
        far_mail_kernel, [(24, 128)], mails[4], core_mail, far_out, move(far_out[1:2], core=1)
    )
    far_back = move(far_mail, far=1)
    mail = mails[0] + move(mails[2], y=2) + move(mails[1], y=1) + move(mails[3], y=3)
    herm = move(mail[16:17], step=3)
    exchange = pl.pallas_call(
        exchange_kernel,
        in_specs=[VMEM] * 6,
        out_specs=VMEM,
        out_shape=jax.ShapeDtypeStruct((2, NT), F32),
        scratch_shapes=[pltpu.VMEM((16, 2 * NMU), BF16)],
        compiler_params=params(24),
        cost_estimate=cost(128),
    )(mail, far_mail, far_back, coulomb.reshape(1, NG), rx, z)
    (out,) = small_call(
        final_kernel,
        [(2, NT)],
        energies,
        vector.reshape(2, NT),
        exchange,
        near_out,
        core_mail,
        far_back,
        herm,
    )
    return out.reshape(1, 2, NT)


def solution(mesh):
    return jax.shard_map(
        on_device,
        mesh=mesh,
        in_specs=(
            P(("grp", "kin"), None, None, None),
            P(("grp", "kin"), None, None),
            P(("grp", "kin"), None),
            P(),
            P(),
            P(),
            P(("grp", "kin"), None),
        ),
        out_specs=P(("grp", "kin"), None, None),
        check_vma=False,
    )
```

```python
import functools

import jax
import jax.numpy as jnp
from jax import lax
from jax.experimental import pallas as pl
from jax.experimental.pallas import tpu as pltpu
from jax.sharding import PartitionSpec as P

NT = 16
NMU = 1024
NG = 1536
WIDTH = NMU + 128
CHUNK = 512
ROWS = 128
F32 = jnp.float32
BF16 = jnp.bfloat16
VMEM = pl.BlockSpec(memory_space=pltpu.VMEM)
SMEM = pl.BlockSpec(memory_space=pltpu.SMEM)
ANY = pl.BlockSpec(memory_space=pl.ANY)


def move(value, x=0, z=0, far=0, y=0, core=0, step=0):
    pairs = []
    for a in range(4):
        for b in range(4):
            for c in range(2):
                for d in range(4):
                    for e in range(2):
                        source = (a * 4 + b) * 16 + c * 8 + d * 2 + e
                        group = (((a + step) % 4) ^ x) * 4 + (b ^ z)
                        member = (c ^ far) * 8 + (d ^ y) * 2 + (e ^ core)
                        pairs.append((source, group * 16 + member))
    return lax.ppermute(value, ("grp", "kin"), pairs)


def iota(shape, dim):
    return lax.broadcasted_iota(jnp.int32, shape, dim)


def dot(left, right):
    return jnp.dot(left, right, preferred_element_type=F32)


def dot_t(left, right):
    return lax.dot_general(left, right, (((1,), (1,)), ((), ())), preferred_element_type=F32)


def split(value):
    high = value.astype(BF16)
    return high, (value - high.astype(F32)).astype(BF16)


def dot_split(left, right):
    high, low = split(left)
    return dot(high, right) + dot(low, right)


def onehot(condition):
    return jnp.where(condition, 1.0, 0.0).astype(BF16)


def spread(repeat):
    row = iota((64, 16), 0)
    col = iota((64, 16), 1)
    band = (row >> 2) & 3 if repeat else row & 3
    base = jnp.where(row < 32, 4, 0) + jnp.where((row >> 4) & 1 == 1, 8, 0)
    return onehot(col == band + base)


def conj_product(left_re, left_im, right_re, right_im):
    real = (left_re * right_re + left_im * right_im).astype(BF16)
    imag = (left_re * right_im - left_im * right_re).astype(BF16)
    return real, imag


def pack_kernel(waves, vector, pay_ref, vector_ref, sems):
    copies = (
        pltpu.make_async_copy(vector, vector_ref, sems.at[0]),
        pltpu.make_async_copy(waves, pay_ref.at[:, pl.ds(0, NMU)], sems.at[1]),
    )
    for copy in copies:
        copy.start()
    copies[0].wait()
    coarse = vector_ref[...].astype(BF16).astype(F32)
    real = jnp.broadcast_to(coarse[0:1], (16, 16))
    imag = jnp.broadcast_to(coarse[1:2], (16, 16))
    row = iota((16, 16), 0)
    lane = iota((16, 16), 1)
    of_v = lane >> 2 == row & 3
    by_c = onehot(row & 3 == lane & 3)
    real_v = dot(jnp.where(of_v, real, 0.0).astype(BF16), by_c)
    imag_v = dot(jnp.where(of_v, imag, 0.0).astype(BF16), by_c)
    upper = row < 8
    first = jnp.where(upper, real_v, imag_v)
    second = jnp.where(upper, -imag_v, real_v)
    mixer = jnp.where(lane & 8 == 0, first, second)
    mixer = jnp.where((row & 4 == 0) & (lane & 4 == 4), mixer, 0.0).astype(BF16)
    line_re = jnp.where(row == 12, real, 0.0).astype(BF16)
    line_im = jnp.where(row == 12, imag, 0.0).astype(BF16)
    row = iota((16, 128), 0)
    lane = iota((16, 128), 1)
    block = dot(mixer, onehot(lane == row)) + dot(line_re, onehot(lane == row + 16)) + dot(line_im, onehot(lane == row + 32))
    pay_ref[:, NMU:WIDTH] = block.astype(BF16)
    copies[1].wait()


def weights_kernel(qmap_ref, screening, w_ref, sems):
    own = lax.axis_index("grp")
    member = lax.axis_index("kin")
    partner = (own + 12) & 15
    steps = []
    for m, flip in enumerate((8, 9, 0, 1)):
        from_a = qmap_ref[0, own * 16 + (member ^ flip)]
        for n in range(4):
            from_b = qmap_ref[0, partner * 16 + (member ^ (2 * n))]
            index = (((from_b >> 4) - (from_a >> 4)) & 15) * 16 + ((from_b - from_a) & 15)
            at = m * 4 + n
            copy = pltpu.make_async_copy(screening.at[pl.ds(index, 1)], w_ref.at[pl.ds(at, 1)], sems.at[at])
            copy.start()
            steps.append(copy)
    for copy in steps:
        copy.wait()


def transitions_kernel(a0, a1, a2, a3, y_ref):
    total_re = jnp.zeros((8, NMU), F32)
    total_im = jnp.zeros((8, NMU), F32)
    for pay in (a0, a1, a2, a3):
        waves = pay[:, 0:NMU]
        mixed = dot(pay[:, NMU : NMU + 16], waves)
        waves = waves.astype(F32)
        val_re, val_im = waves[0:8], waves[8:16]
        mix_re, mix_im = mixed[0:8], mixed[8:16]
        total_re += val_re * mix_re + val_im * mix_im
        total_im += val_re * mix_im - val_im * mix_re
    total_re = jnp.sum(total_re, 0, keepdims=True)
    total_im = jnp.sum(total_im, 0, keepdims=True)
    for j in range(8):
        y_ref[j : j + 1] = total_re[:, j * 128 : j * 128 + 128]
        y_ref[8 + j : 9 + j] = total_im[:, j * 128 : j * 128 + 128]


def pair_kernel(near, *refs):
    if near:
        w_ref, z_ref, far_ref, _, out_ref, rx_ref, lhs, own, xa, xb, acc, ca, cb = refs[6:]
    else:
        w_ref, z_ref, _, out_ref, lhs, xa, xb, acc, ca, cb = refs[6:]
    base = 2 * near
    a_pays = refs[0:2]
    b_pays = refs[2:6]
    half = 2 * ROWS

    def put(to, row, top, left, right, left_at, right_at):
        real, imag = conj_product(
            left[left_at : left_at + 16],
            left[left_at + 16 : left_at + 32],
            right[right_at : right_at + 16],
            right[right_at + 16 : right_at + 32],
        )
        to[row : row + 16, 0:NMU] = real
        to[row : row + 16, NMU : 2 * NMU] = -imag
        to[top + row : top + row + 16, 0:NMU] = imag
        to[top + row : top + row + 16, NMU : 2 * NMU] = real

    rep = spread(True)
    til = spread(False)
    for m in range(2):
        xa[m] = dot(rep, a_pays[m][:, 0:NMU])
    for n in range(4):
        xb[n] = dot(til, b_pays[n][:, 0:NMU])
    for m in range(2):
        for n in range(4):
            row = (m * 4 + n) * 16
            put(lhs, row, half, xa[m], xb[n], 0, 0)
            put(lhs, ROWS + row, half, xa[m], xb[n], 32, 32)
    if near:
        put(own, 0, 16, xa[0], dot(til, a_pays[0][:, 0:NMU]), 32, 0)
    acc[...] = jnp.zeros_like(acc)
    for at in range(0, NG, CHUNK):
        z = z_ref[:, at : at + CHUNK]
        con_re = dot(lhs[0:ROWS], z)
        for p in range(8):
            weight = w_ref[4 * base + p : 4 * base + p + 1, at : at + CHUNK]
            ca[p * 16 : p * 16 + 16, 0:CHUNK] = (con_re[p * 16 : p * 16 + 16] * weight).astype(BF16)
        con_im = dot(lhs[half : half + ROWS], z)
        for p in range(8):
            weight = w_ref[4 * base + p : 4 * base + p + 1, at : at + CHUNK]
            ca[p * 16 : p * 16 + 16, CHUNK : 2 * CHUNK] = (con_im[p * 16 : p * 16 + 16] * weight).astype(BF16)
        val_re = dot(lhs[ROWS:half], z).astype(BF16)
        cb[0:ROWS, 0:CHUNK] = val_re
        cb[ROWS:half, CHUNK : 2 * CHUNK] = -val_re
        val_im = dot(lhs[half + ROWS : 2 * half], z).astype(BF16)
        cb[0:ROWS, CHUNK : 2 * CHUNK] = val_im
        cb[ROWS:half, 0:CHUNK] = val_im
        acc[...] += dot_t(ca[...], cb[...])
        if near:
            rx_ref[:, at : at + CHUNK] = dot(own[...], z)

    pick_row = iota((8, 16), 0)
    pick_col = iota((8, 16), 1)
    xv_a = jnp.zeros((8, 128), F32)
    xv_b = jnp.zeros((8, 128), F32)
    for m in range(2):
        xv_a += dot(onehot((pick_row == m) & (pick_col == 12)), a_pays[m][:, NMU:WIDTH])
    for n in range(4):
        xv_b += dot(onehot((pick_row == n) & (pick_col == 12)), b_pays[n][:, NMU:WIDTH])
    row = iota((ROWS, 8), 0)
    col = iota((ROWS, 8), 1)
    of_a = onehot(row >> 6 == col)
    of_b = onehot((row >> 4) & 3 == col)
    row = iota((ROWS, 128), 0)
    lane = iota((ROWS, 128), 1)
    same_c = lane & 3 == (row >> 2) & 3
    same_d = lane & 3 == row & 3
    spread_a = jnp.where(same_c, dot(of_a, xv_a.astype(BF16)), 0.0).astype(BF16)
    spread_b = jnp.where(same_d, dot(of_b, xv_b.astype(BF16)), 0.0).astype(BF16)
    lane = iota((128, ROWS), 0)
    col = iota((128, ROWS), 1)
    by_w = (lane >> 2) & 3 == col & 3
    by_v = (lane >> 2) & 3 == (col >> 2) & 3
    first = lane >> 4 == 1
    second = lane >> 4 == 2
    pair = iota((ROWS, ROWS), 0) >> 4 == iota((ROWS, ROWS), 1) >> 4
    k_re = jnp.where(pair, acc[:, 0:ROWS], 0.0)
    k_im = jnp.where(pair, acc[:, ROWS:half], 0.0)
    xd_re = dot(spread_b, onehot(by_w & first))
    xd_im = dot(spread_b, onehot(by_w & second))
    xh_re = dot(spread_a, onehot(by_v & first))
    xh_im = dot(spread_a, onehot(by_v & second))
    lane = iota((ROWS, 128), 1)
    col = iota((ROWS, 128), 0)
    by_w = (lane >> 2) & 3 == col & 3
    by_v = (lane >> 2) & 3 == (col >> 2) & 3
    first = lane >> 4 == 0
    second = lane >> 4 == 1
    sum_d = dot_split(k_re * xd_re - k_im * xd_im, onehot(by_v & first)) + dot_split(
        k_re * xd_im + k_im * xd_re, onehot(by_v & second)
    )
    sum_h = dot_split(k_re * xh_re + k_im * xh_im, onehot(by_w & first)) + dot_split(
        k_re * xh_im - k_im * xh_re, onehot(by_w & second)
    )
    sum_d = jnp.where(same_c, sum_d, 0.0)
    sum_h = jnp.where(same_d, sum_h, 0.0)
    row = iota((8, ROWS), 0)
    col = iota((8, ROWS), 1)
    to_a = onehot(row == col >> 6)
    to_b = onehot(row == 4 + ((col >> 4) & 3))
    high_d, low_d = split(sum_d)
    high_h, low_h = split(sum_h)
    total = dot(to_a, high_d) + dot(to_a, low_d) + dot(to_b, high_h) + dot(to_b, low_h)
    if near:
        total += jnp.where(iota((8, 128), 0) >= 4, far_ref[...], 0.0)
    out_ref[...] = total


def mail_kernel(y0, y1, y2, y3, out_ref, *mails):
    total = y0[...] + y1[...] + y2[...] + y3[...]
    for n, mail in enumerate(mails):
        mail[0:16] = total
        mail[16:24] = jnp.broadcast_to(out_ref[4 + n : 5 + n], (8, 128))


def exchange_kernel(y_ref, c_ref, rx_ref, z_ref, out_ref, lhs):
    pad = jnp.zeros((12, 128), F32)
    for j in range(8):
        real = y_ref[j : j + 1]
        imag = y_ref[8 + j : 9 + j]
        for at, top, bottom in ((0, real, imag), (NMU, -imag, real)):
            high, low = split(jnp.concatenate([top, bottom], 0))
            rows = jnp.concatenate([high.astype(F32), low.astype(F32), pad], 0)
            lhs[:, at + j * 128 : at + j * 128 + 128] = rows.astype(BF16)
    acc_re = jnp.zeros((16, 128), F32)
    acc_im = jnp.zeros((16, 128), F32)
    for start in range(0, NG, CHUNK):
        part = pl.ds(start, CHUNK)
        total = dot(lhs[...], z_ref[:, part])
        pot_re = (total[0:1] + total[2:3]) * c_ref[:, part]
        pot_im = (total[1:2] + total[3:4]) * c_ref[:, part]
        rx_re = rx_ref[0:16, part]
        rx_im = rx_ref[16:32, part]
        real = rx_re * pot_re + rx_im * pot_im
        imag = rx_re * pot_im - rx_im * pot_re
        for at in range(0, CHUNK, 128):
            acc_re += real[:, at : at + 128]
            acc_im += imag[:, at : at + 128]
    ones = jnp.ones((8, 128), BF16)
    out = []
    for acc in (acc_re, acc_im):
        high, low = split(acc)
        out.append((dot_t(ones, high) + dot_t(ones, low))[0:1])
    out_ref[...] = jnp.concatenate(out, 0)


def final_kernel(energy_ref, vector_ref, exchange_ref, near_ref, d0, d1, d2, out_ref):
    scale = 1.0 / 256
    terms = near_ref[0:1] + d0[...] + d1[...] + d2[...]
    for part in range(2):
        term = terms[:, part * NT : part * NT + NT]
        out_ref[part : part + 1] = (
            energy_ref[...] * vector_ref[part : part + 1]
            + (2.0 * scale) * exchange_ref[part : part + 1]
            - scale * term
        )


def params(mib):
    return pltpu.CompilerParams(vmem_limit_bytes=mib * 1024 * 1024)


def cost(rows):
    return pl.CostEstimate(flops=2 * rows * 2 * NMU * NG, bytes_accessed=4 * NMU * NG, transcendentals=0)


def pair_call(near, operands):
    scratch = [pltpu.VMEM((4 * ROWS, 2 * NMU), BF16)]
    out_shape = [jax.ShapeDtypeStruct((8, 128), F32)]
    if near:
        scratch.append(pltpu.VMEM((32, 2 * NMU), BF16))
        out_shape.append(pltpu.VMEM((32, NG), F32))
    return pl.pallas_call(
        functools.partial(pair_kernel, near),
        in_specs=[VMEM] * 8 + [VMEM] * near + [ANY],
        out_specs=[VMEM] * len(out_shape),
        out_shape=out_shape,
        scratch_shapes=scratch
        + [
            pltpu.VMEM((2, 64, NMU), F32),
            pltpu.VMEM((4, 64, NMU), F32),
            pltpu.VMEM((ROWS, 2 * ROWS), F32),
            pltpu.VMEM((ROWS, 2 * CHUNK), BF16),
            pltpu.VMEM((2 * ROWS, 2 * CHUNK), BF16),
        ],
        compiler_params=params(24),
        cost_estimate=cost(4 * ROWS),
    )(*operands)


def on_device(waves, vector, energies, basis, screening, coulomb, qmap):
    pay = pl.pallas_call(
        pack_kernel,
        in_specs=[ANY] * 2,
        out_specs=VMEM,
        out_shape=pltpu.VMEM((16, WIDTH), BF16),
        scratch_shapes=[pltpu.VMEM((2, NT), F32), pltpu.SemaphoreType.DMA((2,))],
        compiler_params=params(56),
    )(waves.reshape(16, NMU), vector.reshape(2, NT))
    a1 = move(pay, far=1)
    b0 = move(pay, step=1)
    a2 = move(pay, core=1)
    z = basis.reshape(2 * NMU, NG)
    weights = pl.pallas_call(
        weights_kernel,
        in_specs=[SMEM, ANY],
        out_specs=VMEM,
        out_shape=pltpu.VMEM((16, NG), F32),
        scratch_shapes=[pltpu.SemaphoreType.DMA((16,))],
        compiler_params=params(54),
        cost_estimate=pl.CostEstimate(flops=4000000000, bytes_accessed=1024, transcendentals=0),
    )(qmap, screening)
    b1, b2, b3 = (move(b0, y=n) for n in (1, 2, 3))
    a3 = move(a1, core=1)
    y = pl.pallas_call(
        transitions_kernel,
        in_specs=[VMEM] * 4,
        out_specs=VMEM,
        out_shape=jax.ShapeDtypeStruct((16, 128), F32),
        compiler_params=params(8),
    )(pay, a1, a2, a3)
    b_pays = (b0, b1, b2, b3)
    (far_out,) = pair_call(0, (a1, a3, *b_pays, weights, z, y))
    far_sum = far_out[0:1] + move(far_out[1:2], core=1)
    y = y + move(y, z=2) + move(y, z=1) + move(y, z=3)
    near_out, rx = pair_call(1, (pay, a2, *b_pays, weights, z, far_out, y))
    mail = pl.pallas_call(
        mail_kernel,
        in_specs=[VMEM] * 5,
        out_specs=[VMEM] * 4,
        out_shape=[jax.ShapeDtypeStruct((24, 128), F32)] * 4,
        compiler_params=params(4),
    )(y, *(move(y, x=n) for n in (2, 1, 3)), near_out)
    mail = mail[0] + move(mail[2], y=2) + move(mail[1], y=1) + move(mail[3], y=3)
    exchange = pl.pallas_call(
        exchange_kernel,
        in_specs=[VMEM] * 4,
        out_specs=VMEM,
        out_shape=jax.ShapeDtypeStruct((2, NT), F32),
        scratch_shapes=[pltpu.VMEM((16, 2 * NMU), BF16)],
        compiler_params=params(24),
        cost_estimate=cost(128),
    )(mail, coulomb.reshape(1, NG), rx, z)

    out = pl.pallas_call(
        final_kernel,
        in_specs=[VMEM] * 7,
        out_specs=VMEM,
        out_shape=jax.ShapeDtypeStruct((2, NT), F32),
        compiler_params=params(4),
    )(
        energies,
        vector.reshape(2, NT),
        exchange,
        near_out,
        move(near_out[1:2], core=1),
        move(far_sum, far=1),
        move(mail[16:17], step=3),
    )
    return out.reshape(1, 2, NT)


def solution(mesh):
    return jax.shard_map(
        on_device,
        mesh=mesh,
        in_specs=(
            P(("grp", "kin"), None, None, None),
            P(("grp", "kin"), None, None),
            P(("grp", "kin"), None),
            P(),
            P(),
            P(),
            P(("grp", "kin"), None),
        ),
        out_specs=P(("grp", "kin"), None, None),
        check_vma=False,
    )
```

```python
import functools

import jax
import jax.numpy as jnp
from jax import lax
from jax.experimental import pallas as pl
from jax.experimental.pallas import tpu as pltpu
from jax.sharding import PartitionSpec as P

NT = 16
NMU = 1024
NG = 1536
WIDTH = NMU + 128
CHUNK = 1536
ROWS = 128
F32 = jnp.float32
BF16 = jnp.bfloat16
VMEM = pl.BlockSpec(memory_space=pltpu.VMEM)
SMEM = pl.BlockSpec(memory_space=pltpu.SMEM)
ANY = pl.BlockSpec(memory_space=pl.ANY)


def move(value, x=0, z=0, far=0, y=0, core=0, step=0):
    pairs = []
    for a in range(4):
        for b in range(4):
            for c in range(2):
                for d in range(4):
                    for e in range(2):
                        source = (a * 4 + b) * 16 + c * 8 + d * 2 + e
                        group = (((a + step) % 4) ^ x) * 4 + (b ^ z)
                        member = (c ^ far) * 8 + (d ^ y) * 2 + (e ^ core)
                        pairs.append((source, group * 16 + member))
    return lax.ppermute(value, ("grp", "kin"), pairs)


def iota(shape, dim):
    return lax.broadcasted_iota(jnp.int32, shape, dim)


def dot(left, right):
    return jnp.dot(left, right, preferred_element_type=F32)


def dot_t(left, right):
    return lax.dot_general(left, right, (((1,), (1,)), ((), ())), preferred_element_type=F32)


def split(value):
    high = value.astype(BF16)
    return high, (value - high.astype(F32)).astype(BF16)


def dot_split(left, right):
    high, low = split(left)
    return dot(high, right) + dot(low, right)


def onehot(condition):
    return jnp.where(condition, 1.0, 0.0).astype(BF16)


def spread(repeat):
    row = iota((64, 16), 0)
    col = iota((64, 16), 1)
    band = (row >> 2) & 3 if repeat else row & 3
    base = jnp.where(row < 32, 4, 0) + jnp.where((row >> 4) & 1 == 1, 8, 0)
    return onehot(col == band + base)


def conj_product(left_re, left_im, right_re, right_im):
    real = (left_re * right_re + left_im * right_im).astype(BF16)
    imag = (left_re * right_im - left_im * right_re).astype(BF16)
    return real, imag


def pack_kernel(waves, vector, pay_ref, vector_ref, sems):
    copies = (
        pltpu.make_async_copy(vector, vector_ref, sems.at[0]),
        pltpu.make_async_copy(waves, pay_ref.at[:, pl.ds(0, NMU)], sems.at[1]),
    )
    for copy in copies:
        copy.start()
    copies[0].wait()
    coarse = vector_ref[...].astype(BF16).astype(F32)
    real = jnp.broadcast_to(coarse[0:1], (16, 16))
    imag = jnp.broadcast_to(coarse[1:2], (16, 16))
    row = iota((16, 16), 0)
    lane = iota((16, 16), 1)
    of_v = lane >> 2 == row & 3
    by_c = onehot(row & 3 == lane & 3)
    real_v = dot(jnp.where(of_v, real, 0.0).astype(BF16), by_c)
    imag_v = dot(jnp.where(of_v, imag, 0.0).astype(BF16), by_c)
    upper = row < 8
    first = jnp.where(upper, real_v, imag_v)
    second = jnp.where(upper, -imag_v, real_v)
    mixer = jnp.where(lane & 8 == 0, first, second)
    mixer = jnp.where((row & 4 == 0) & (lane & 4 == 4), mixer, 0.0).astype(BF16)
    line_re = jnp.where(row == 12, real, 0.0).astype(BF16)
    line_im = jnp.where(row == 12, imag, 0.0).astype(BF16)
    row = iota((16, 128), 0)
    lane = iota((16, 128), 1)
    block = dot(mixer, onehot(lane == row)) + dot(line_re, onehot(lane == row + 16)) + dot(line_im, onehot(lane == row + 32))
    pay_ref[:, NMU:WIDTH] = block.astype(BF16)
    copies[1].wait()


def weights_kernel(qmap_ref, screening, w_ref, sems):
    own = lax.axis_index("grp")
    member = lax.axis_index("kin")
    partner = (own + 12) & 15
    steps = []
    for m, flip in enumerate((4, 6, 0, 2)):
        from_a = qmap_ref[0, own * 16 + (member ^ flip)]
        for n, other in enumerate((0, 8, 1, 9)):
            from_b = qmap_ref[0, partner * 16 + (member ^ other)]
            index = (((from_b >> 4) - (from_a >> 4)) & 15) * 16 + ((from_b - from_a) & 15)
            at = m * 4 + n
            copy = pltpu.make_async_copy(screening.at[pl.ds(index, 1)], w_ref.at[pl.ds(at, 1)], sems.at[at])
            copy.start()
            steps.append(copy)
    for copy in steps:
        copy.wait()


def transitions_kernel(a0, a1, a2, a3, _, __, y_ref):
    total_re = jnp.zeros((8, NMU), F32)
    total_im = jnp.zeros((8, NMU), F32)
    for pay in (a0, a1, a2, a3):
        waves = pay[:, 0:NMU]
        mixed = dot(pay[:, NMU : NMU + 16], waves)
        waves = waves.astype(F32)
        val_re, val_im = waves[0:8], waves[8:16]
        mix_re, mix_im = mixed[0:8], mixed[8:16]
        total_re += val_re * mix_re + val_im * mix_im
        total_im += val_re * mix_im - val_im * mix_re
    total_re = jnp.sum(total_re, 0, keepdims=True)
    total_im = jnp.sum(total_im, 0, keepdims=True)
    for j in range(8):
        y_ref[j : j + 1] = total_re[:, j * 128 : j * 128 + 128]
        y_ref[8 + j : 9 + j] = total_im[:, j * 128 : j * 128 + 128]


def pair_kernel(near, *refs):
    if near:
        w_ref, z_ref, far_ref, _, out_ref, rx_ref, lhs, own, xa, xb, acc, ca, cb = refs[5:]
    else:
        w_ref, z_ref, _, out_ref, lhs, xa, xb, acc, ca, cb = refs[5:]
    base = 2 * near
    a_pays = [refs[0].at[pl.ds(m * 16, 16)] for m in range(2)]
    b_pays = refs[1:5]
    half = 2 * ROWS

    def put(to, row, top, left, right, left_at, right_at):
        real, imag = conj_product(
            left[left_at : left_at + 16],
            left[left_at + 16 : left_at + 32],
            right[right_at : right_at + 16],
            right[right_at + 16 : right_at + 32],
        )
        to[row : row + 16, 0:NMU] = real
        to[row : row + 16, NMU : 2 * NMU] = -imag
        to[top + row : top + row + 16, 0:NMU] = imag
        to[top + row : top + row + 16, NMU : 2 * NMU] = real

    rep = spread(True)
    til = spread(False)
    for m in range(2):
        xa[m] = dot(rep, a_pays[m][:, 0:NMU])
    for n in range(4):
        xb[n] = dot(til, b_pays[n][:, 0:NMU])
    for m in range(2):
        for n in range(4):
            row = (m * 4 + n) * 16
            put(lhs, row, half, xa[m], xb[n], 0, 0)
            put(lhs, ROWS + row, half, xa[m], xb[n], 32, 32)
    if near:
        put(own, 0, 16, xa[0], dot(til, a_pays[0][:, 0:NMU]), 32, 0)
    acc[...] = jnp.zeros_like(acc)
    for at in range(0, NG, CHUNK):
        z = z_ref[:, at : at + CHUNK]
        con_re = dot(lhs[0:ROWS], z)
        for p in range(8):
            weight = w_ref[4 * base + p : 4 * base + p + 1, at : at + CHUNK]
            ca[p * 16 : p * 16 + 16, 0:CHUNK] = (con_re[p * 16 : p * 16 + 16] * weight).astype(BF16)
        con_im = dot(lhs[half : half + ROWS], z)
        for p in range(8):
            weight = w_ref[4 * base + p : 4 * base + p + 1, at : at + CHUNK]
            ca[p * 16 : p * 16 + 16, CHUNK : 2 * CHUNK] = (con_im[p * 16 : p * 16 + 16] * weight).astype(BF16)
        val_re = dot(lhs[ROWS:half], z).astype(BF16)
        cb[0:ROWS, 0:CHUNK] = val_re
        cb[ROWS:half, CHUNK : 2 * CHUNK] = -val_re
        val_im = dot(lhs[half + ROWS : 2 * half], z).astype(BF16)
        cb[0:ROWS, CHUNK : 2 * CHUNK] = val_im
        cb[ROWS:half, 0:CHUNK] = val_im
        acc[...] += dot_t(ca[...], cb[...])
        if near:
            rx_ref[:, at : at + CHUNK] = dot(own[...], z)

    pick_row = iota((8, 16), 0)
    pick_col = iota((8, 16), 1)
    xv_a = jnp.zeros((8, 128), F32)
    xv_b = jnp.zeros((8, 128), F32)
    for m in range(2):
        xv_a += dot(onehot((pick_row == m) & (pick_col == 12)), a_pays[m][:, NMU:WIDTH])
    for n in range(4):
        xv_b += dot(onehot((pick_row == n) & (pick_col == 12)), b_pays[n][:, NMU:WIDTH])
    row = iota((ROWS, 8), 0)
    col = iota((ROWS, 8), 1)
    of_a = onehot(row >> 6 == col)
    of_b = onehot((row >> 4) & 3 == col)
    row = iota((ROWS, 128), 0)
    lane = iota((ROWS, 128), 1)
    same_c = lane & 3 == (row >> 2) & 3
    same_d = lane & 3 == row & 3
    spread_a = jnp.where(same_c, dot(of_a, xv_a.astype(BF16)), 0.0).astype(BF16)
    spread_b = jnp.where(same_d, dot(of_b, xv_b.astype(BF16)), 0.0).astype(BF16)
    lane = iota((128, ROWS), 0)
    col = iota((128, ROWS), 1)
    by_w = (lane >> 2) & 3 == col & 3
    by_v = (lane >> 2) & 3 == (col >> 2) & 3
    first = lane >> 4 == 1
    second = lane >> 4 == 2
    pair = iota((ROWS, ROWS), 0) >> 4 == iota((ROWS, ROWS), 1) >> 4
    k_re = jnp.where(pair, acc[:, 0:ROWS], 0.0)
    k_im = jnp.where(pair, acc[:, ROWS:half], 0.0)
    xd_re = dot(spread_b, onehot(by_w & first))
    xd_im = dot(spread_b, onehot(by_w & second))
    xh_re = dot(spread_a, onehot(by_v & first))
    xh_im = dot(spread_a, onehot(by_v & second))
    lane = iota((ROWS, 128), 1)
    col = iota((ROWS, 128), 0)
    by_w = (lane >> 2) & 3 == col & 3
    by_v = (lane >> 2) & 3 == (col >> 2) & 3
    first = lane >> 4 == 0
    second = lane >> 4 == 1
    sum_d = dot_split(k_re * xd_re - k_im * xd_im, onehot(by_v & first)) + dot_split(
        k_re * xd_im + k_im * xd_re, onehot(by_v & second)
    )
    sum_h = dot_split(k_re * xh_re + k_im * xh_im, onehot(by_w & first)) + dot_split(
        k_re * xh_im - k_im * xh_re, onehot(by_w & second)
    )
    sum_d = jnp.where(same_c, sum_d, 0.0)
    sum_h = jnp.where(same_d, sum_h, 0.0)
    row = iota((8, ROWS), 0)
    col = iota((8, ROWS), 1)
    to_a = onehot(row == col >> 6)
    to_b = onehot(row == 4 + ((col >> 4) & 3))
    high_d, low_d = split(sum_d)
    high_h, low_h = split(sum_h)
    total = dot(to_a, high_d) + dot(to_a, low_d) + dot(to_b, high_h) + dot(to_b, low_h)
    if near:
        total += jnp.where(iota((8, 128), 0) >= 4, far_ref[...], 0.0)
    out_ref[...] = total


def first_mail_kernel(y0, y1, y2, y3, far_ref, mail):
    mail[0:16] = y0[...] + y1[...] + y2[...] + y3[...]
    mail[16:24] = far_ref[...]


def second_mail_kernel(sent, received, near_ref, mail, herm):
    mail[0:16] = sent[0:16] + received[0:16]
    mail[16:24] = near_ref[...] + received[16:24]
    herm[...] = near_ref[...]


def row_kernel(herm, _, out_ref):
    out_ref[...] = herm[0:1]


def join_kernel(first, second, out_ref):
    out_ref[0:16] = first[...]
    out_ref[16:32] = second[...]


def exchange_kernel(sent, received, c_ref, rx_ref, z_ref, out_ref, lhs):
    y = sent[0:16] + received[0:16]
    pad = jnp.zeros((12, 128), F32)
    for j in range(8):
        real = y[j : j + 1]
        imag = y[8 + j : 9 + j]
        for at, top, bottom in ((0, real, imag), (NMU, -imag, real)):
            high, low = split(jnp.concatenate([top, bottom], 0))
            rows = jnp.concatenate([high.astype(F32), low.astype(F32), pad], 0)
            lhs[:, at + j * 128 : at + j * 128 + 128] = rows.astype(BF16)
    acc_re = jnp.zeros((16, 128), F32)
    acc_im = jnp.zeros((16, 128), F32)
    for start in range(0, NG, 512):
        part = pl.ds(start, 512)
        total = dot(lhs[...], z_ref[:, part])
        pot_re = (total[0:1] + total[2:3]) * c_ref[:, part]
        pot_im = (total[1:2] + total[3:4]) * c_ref[:, part]
        rx_re = rx_ref[0:16, part]
        rx_im = rx_ref[16:32, part]
        real = rx_re * pot_re + rx_im * pot_im
        imag = rx_re * pot_im - rx_im * pot_re
        for at in range(0, 512, 128):
            acc_re += real[:, at : at + 128]
            acc_im += imag[:, at : at + 128]
    ones = jnp.ones((8, 128), BF16)
    out = []
    for acc in (acc_re, acc_im):
        high, low = split(acc)
        out.append((dot_t(ones, high) + dot_t(ones, low))[0:1])
    out_ref[...] = jnp.concatenate(out, 0)


def final_kernel(energy_ref, vector_ref, exchange_ref, sent, received, h0, h1, out_ref):
    scale = 1.0 / 256
    terms = sent[16:17] + received[17:18] + h0[...] + h1[...]
    for part in range(2):
        term = terms[:, part * NT : part * NT + NT]
        out_ref[part : part + 1] = (
            energy_ref[...] * vector_ref[part : part + 1]
            + (2.0 * scale) * exchange_ref[part : part + 1]
            - scale * term
        )


def params(mib):
    return pltpu.CompilerParams(vmem_limit_bytes=mib * 1024 * 1024)


def cost(rows):
    return pl.CostEstimate(flops=2 * rows * 2 * NMU * NG, bytes_accessed=4 * NMU * NG, transcendentals=0)


def pair_call(near, operands):
    scratch = [pltpu.VMEM((4 * ROWS, 2 * NMU), BF16)]
    out_shape = [jax.ShapeDtypeStruct((8, 128), F32)]
    if near:
        scratch.append(pltpu.VMEM((32, 2 * NMU), BF16))
        out_shape.append(pltpu.VMEM((32, NG), F32))
    return pl.pallas_call(
        functools.partial(pair_kernel, near),
        in_specs=[VMEM] * 7 + [VMEM] * near + [ANY],
        out_specs=[VMEM] * len(out_shape),
        out_shape=out_shape,
        scratch_shapes=scratch
        + [
            pltpu.VMEM((2, 64, NMU), F32),
            pltpu.VMEM((4, 64, NMU), F32),
            pltpu.VMEM((ROWS, 2 * ROWS), F32),
            pltpu.VMEM((ROWS, 2 * CHUNK), BF16),
            pltpu.VMEM((2 * ROWS, 2 * CHUNK), BF16),
        ],
        compiler_params=params(24),
        cost_estimate=cost(4 * ROWS),
    )(*operands)


def small_call(kernel, shape, *operands, kind=F32, after=()):
    return pl.pallas_call(
        kernel,
        in_specs=[VMEM] * len(operands) + [ANY] * len(after),
        out_specs=VMEM,
        out_shape=jax.ShapeDtypeStruct(shape, kind),
        compiler_params=params(8),
    )(*operands, *after)


def on_device(waves, vector, energies, basis, screening, coulomb, qmap):
    pay = pl.pallas_call(
        pack_kernel,
        in_specs=[ANY] * 2,
        out_specs=VMEM,
        out_shape=pltpu.VMEM((16, WIDTH), BF16),
        scratch_shapes=[pltpu.VMEM((2, NT), F32), pltpu.SemaphoreType.DMA((2,))],
        compiler_params=params(56),
    )(waves.reshape(16, NMU), vector.reshape(2, NT))
    b0 = move(pay, step=1)
    b1 = move(pay, step=1, far=1)
    a1 = move(pay, y=1)
    near = small_call(join_kernel, (32, WIDTH), pay, a1, kind=BF16)
    far = move(near, y=2)
    b2 = move(b0, core=1)
    b3 = move(b1, core=1)
    weights = pl.pallas_call(
        weights_kernel,
        in_specs=[SMEM, ANY],
        out_specs=VMEM,
        out_shape=pltpu.VMEM((16, NG), F32),
        scratch_shapes=[pltpu.SemaphoreType.DMA((16,))],
        compiler_params=params(54),
        cost_estimate=pl.CostEstimate(flops=4000000000, bytes_accessed=1024, transcendentals=0),
    )(qmap, screening)
    z = basis.reshape(2 * NMU, NG)
    b_pays = (b0, b1, b2, b3)
    y = small_call(transitions_kernel, (16, 128), *b_pays, after=(near, weights))
    (far_out,) = pair_call(0, (far, *b_pays, weights, z, y))
    y = y + move(y, z=2) + move(y, z=1) + move(y, z=3)
    first = small_call(first_mail_kernel, (24, 128), y, *(move(y, x=n) for n in (2, 1, 3)), far_out)
    near_out, rx = pair_call(1, (near, *b_pays, weights, z, far_out, first))
    second, herm = pl.pallas_call(
        second_mail_kernel,
        in_specs=[VMEM] * 3,
        out_specs=[VMEM] * 2,
        out_shape=[jax.ShapeDtypeStruct((24, 128), F32), jax.ShapeDtypeStruct((8, 128), F32)],
        compiler_params=params(8),
    )(first, move(first, y=2), near_out)
    received = move(second, y=1)
    herm = herm[4:6] + move(herm[6:8], core=1)
    far_herm = move(herm[1:2], step=3, far=1)
    near_herm = move(small_call(row_kernel, (1, 128), herm, after=(received,)), step=3)
    exchange = pl.pallas_call(
        exchange_kernel,
        in_specs=[VMEM] * 5,
        out_specs=VMEM,
        out_shape=jax.ShapeDtypeStruct((2, NT), F32),
        scratch_shapes=[pltpu.VMEM((16, 2 * NMU), BF16)],
        compiler_params=params(24),
        cost_estimate=cost(128),
    )(second, received, coulomb.reshape(1, NG), rx, z)
    out = small_call(
        final_kernel,
        (2, NT),
        energies,
        vector.reshape(2, NT),
        exchange,
        second,
        received,
        near_herm,
        far_herm,
    )
    return out.reshape(1, 2, NT)


def solution(mesh):
    return jax.shard_map(
        on_device,
        mesh=mesh,
        in_specs=(
            P(("grp", "kin"), None, None, None),
            P(("grp", "kin"), None, None),
            P(("grp", "kin"), None),
            P(),
            P(),
            P(),
            P(("grp", "kin"), None),
        ),
        out_specs=P(("grp", "kin"), None, None),
        check_vma=False,
    )
```

```python
import functools

import jax
import jax.numpy as jnp
from jax import lax
from jax.experimental import pallas as pl
from jax.experimental.pallas import tpu as pltpu
from jax.sharding import PartitionSpec as P

NT = 16
NMU = 1024
NG = 1536
WIDTH = NMU + 128
CHUNK = 1536
ROWS = 128
F32 = jnp.float32
BF16 = jnp.bfloat16
VMEM = pl.BlockSpec(memory_space=pltpu.VMEM)
SMEM = pl.BlockSpec(memory_space=pltpu.SMEM)
ANY = pl.BlockSpec(memory_space=pl.ANY)


def move(value, x=0, z=0, far=0, y=0, core=0, step=0):
    pairs = []
    for a in range(4):
        for b in range(4):
            for c in range(2):
                for d in range(4):
                    for e in range(2):
                        source = (a * 4 + b) * 16 + c * 8 + d * 2 + e
                        group = (((a + step) % 4) ^ x) * 4 + (b ^ z)
                        member = (c ^ far) * 8 + (d ^ y) * 2 + (e ^ core)
                        pairs.append((source, group * 16 + member))
    return lax.ppermute(value, ("grp", "kin"), pairs)


def iota(shape, dim):
    return lax.broadcasted_iota(jnp.int32, shape, dim)


def dot(left, right):
    return jnp.dot(left, right, preferred_element_type=F32)


def dot_t(left, right):
    return lax.dot_general(left, right, (((1,), (1,)), ((), ())), preferred_element_type=F32)


def split(value):
    high = value.astype(BF16)
    return high, (value - high.astype(F32)).astype(BF16)


def dot_split(left, right):
    high, low = split(left)
    return dot(high, right) + dot(low, right)


def onehot(condition):
    return jnp.where(condition, 1.0, 0.0).astype(BF16)


def spread(repeat):
    row = iota((64, 16), 0)
    col = iota((64, 16), 1)
    band = (row >> 2) & 3 if repeat else row & 3
    base = jnp.where(row < 32, 4, 0) + jnp.where((row >> 4) & 1 == 1, 8, 0)
    return onehot(col == band + base)


def conj_product(left_re, left_im, right_re, right_im):
    real = (left_re * right_re + left_im * right_im).astype(BF16)
    imag = (left_re * right_im - left_im * right_re).astype(BF16)
    return real, imag


def pack_kernel(waves, vector, pay_ref, vector_ref, sems):
    copies = (
        pltpu.make_async_copy(vector, vector_ref, sems.at[0]),
        pltpu.make_async_copy(waves, pay_ref.at[:, pl.ds(0, NMU)], sems.at[1]),
    )
    for copy in copies:
        copy.start()
    copies[0].wait()
    coarse = vector_ref[...].astype(BF16).astype(F32)
    real = jnp.broadcast_to(coarse[0:1], (16, 16))
    imag = jnp.broadcast_to(coarse[1:2], (16, 16))
    row = iota((16, 16), 0)
    lane = iota((16, 16), 1)
    of_v = lane >> 2 == row & 3
    by_c = onehot(row & 3 == lane & 3)
    real_v = dot(jnp.where(of_v, real, 0.0).astype(BF16), by_c)
    imag_v = dot(jnp.where(of_v, imag, 0.0).astype(BF16), by_c)
    upper = row < 8
    first = jnp.where(upper, real_v, imag_v)
    second = jnp.where(upper, -imag_v, real_v)
    mixer = jnp.where(lane & 8 == 0, first, second)
    mixer = jnp.where((row & 4 == 0) & (lane & 4 == 4), mixer, 0.0).astype(BF16)
    line_re = jnp.where(row == 12, real, 0.0).astype(BF16)
    line_im = jnp.where(row == 12, imag, 0.0).astype(BF16)
    row = iota((16, 128), 0)
    lane = iota((16, 128), 1)
    block = dot(mixer, onehot(lane == row)) + dot(line_re, onehot(lane == row + 16)) + dot(line_im, onehot(lane == row + 32))
    pay_ref[:, NMU:WIDTH] = block.astype(BF16)
    copies[1].wait()


def weights_kernel(qmap_ref, screening, w_ref, sems):
    own = lax.axis_index("grp")
    member = lax.axis_index("kin")
    partner = (own + 12) & 15
    steps = []
    for m, flip in enumerate((8, 9, 0, 1)):
        from_a = qmap_ref[0, own * 16 + (member ^ flip)]
        for n in range(4):
            from_b = qmap_ref[0, partner * 16 + (member ^ (2 * n))]
            index = (((from_b >> 4) - (from_a >> 4)) & 15) * 16 + ((from_b - from_a) & 15)
            at = m * 4 + n
            copy = pltpu.make_async_copy(screening.at[pl.ds(index, 1)], w_ref.at[pl.ds(at, 1)], sems.at[at])
            copy.start()
            steps.append(copy)
    for copy in steps:
        copy.wait()


def transitions_kernel(a0, a1, a2, a3, y_ref):
    total_re = jnp.zeros((8, NMU), F32)
    total_im = jnp.zeros((8, NMU), F32)
    for pay in (a0, a1, a2, a3):
        waves = pay[:, 0:NMU]
        mixed = dot(pay[:, NMU : NMU + 16], waves)
        waves = waves.astype(F32)
        val_re, val_im = waves[0:8], waves[8:16]
        mix_re, mix_im = mixed[0:8], mixed[8:16]
        total_re += val_re * mix_re + val_im * mix_im
        total_im += val_re * mix_im - val_im * mix_re
    total_re = jnp.sum(total_re, 0, keepdims=True)
    total_im = jnp.sum(total_im, 0, keepdims=True)
    for j in range(8):
        y_ref[j : j + 1] = total_re[:, j * 128 : j * 128 + 128]
        y_ref[8 + j : 9 + j] = total_im[:, j * 128 : j * 128 + 128]


def pair_kernel(near, *refs):
    if near:
        w_ref, z_ref, far_ref, _, out_ref, rx_ref, lhs, xa, xb, acc, ca, cb = refs[6:]
    else:
        w_ref, z_ref, _, out_ref, lhs, xa, xb, acc, ca, cb = refs[6:]
    base = 2 * near
    a_pays = refs[0:2]
    b_pays = refs[2:6]
    val = ROWS + 16 * near
    half = ROWS + val

    def put(row, left, right, left_at, right_at):
        real, imag = conj_product(
            left[left_at : left_at + 16],
            left[left_at + 16 : left_at + 32],
            right[right_at : right_at + 16],
            right[right_at + 16 : right_at + 32],
        )
        lhs[row : row + 16, 0:NMU] = real
        lhs[row : row + 16, NMU : 2 * NMU] = -imag
        lhs[half + row : half + row + 16, 0:NMU] = imag
        lhs[half + row : half + row + 16, NMU : 2 * NMU] = real

    rep = spread(True)
    til = spread(False)
    for m in range(2):
        xa[m] = dot(rep, a_pays[m][:, 0:NMU])
    for n in range(4):
        xb[n] = dot(til, b_pays[n][:, 0:NMU])
    for m in range(2):
        for n in range(4):
            row = (m * 4 + n) * 16
            put(row, xa[m], xb[n], 0, 0)
            put(ROWS + row, xa[m], xb[n], 32, 32)
    if near:
        put(2 * ROWS, xa[0], dot(til, a_pays[0][:, 0:NMU]), 32, 0)
    acc[...] = jnp.zeros_like(acc)
    for at in range(0, NG, CHUNK):
        part = pl.ds(at, CHUNK)
        z = z_ref[:, part]
        for side in range(2):
            con = dot(lhs[side * half : side * half + ROWS], z)
            for p in range(8):
                weight = w_ref[4 * base + p : 4 * base + p + 1, part]
                row = side * ROWS + p * 16
                ca[row : row + 16] = (con[p * 16 : p * 16 + 16] * weight).astype(BF16)
            dens = dot(lhs[side * half + ROWS : side * half + half], z)
            cb[side * ROWS : side * ROWS + ROWS] = dens[0:ROWS].astype(BF16)
            if near:
                rx_ref[side * 16 : side * 16 + 16, part] = dens[ROWS:val]
        acc[...] += dot_t(ca[...], cb[...])

    pick_row = iota((8, 16), 0)
    pick_col = iota((8, 16), 1)
    xv_a = jnp.zeros((8, 128), F32)
    xv_b = jnp.zeros((8, 128), F32)
    for m in range(2):
        xv_a += dot(onehot((pick_row == m) & (pick_col == 12)), a_pays[m][:, NMU:WIDTH])
    for n in range(4):
        xv_b += dot(onehot((pick_row == n) & (pick_col == 12)), b_pays[n][:, NMU:WIDTH])
    row = iota((ROWS, 8), 0)
    col = iota((ROWS, 8), 1)
    of_a = onehot(row >> 6 == col)
    of_b = onehot((row >> 4) & 3 == col)
    row = iota((ROWS, 128), 0)
    lane = iota((ROWS, 128), 1)
    same_c = lane & 3 == (row >> 2) & 3
    same_d = lane & 3 == row & 3
    spread_a = jnp.where(same_c, dot(of_a, xv_a.astype(BF16)), 0.0).astype(BF16)
    spread_b = jnp.where(same_d, dot(of_b, xv_b.astype(BF16)), 0.0).astype(BF16)
    lane = iota((128, ROWS), 0)
    col = iota((128, ROWS), 1)
    by_w = (lane >> 2) & 3 == col & 3
    by_v = (lane >> 2) & 3 == (col >> 2) & 3
    first = lane >> 4 == 1
    second = lane >> 4 == 2
    pair = iota((ROWS, ROWS), 0) >> 4 == iota((ROWS, ROWS), 1) >> 4
    k_re = jnp.where(pair, acc[0:ROWS, 0:ROWS] + acc[ROWS:, ROWS:], 0.0)
    k_im = jnp.where(pair, acc[0:ROWS, ROWS:] - acc[ROWS:, 0:ROWS], 0.0)
    xd_re = dot(spread_b, onehot(by_w & first))
    xd_im = dot(spread_b, onehot(by_w & second))
    xh_re = dot(spread_a, onehot(by_v & first))
    xh_im = dot(spread_a, onehot(by_v & second))
    lane = iota((ROWS, 128), 1)
    col = iota((ROWS, 128), 0)
    by_w = (lane >> 2) & 3 == col & 3
    by_v = (lane >> 2) & 3 == (col >> 2) & 3
    first = lane >> 4 == 0
    second = lane >> 4 == 1
    sum_d = dot_split(k_re * xd_re - k_im * xd_im, onehot(by_v & first)) + dot_split(
        k_re * xd_im + k_im * xd_re, onehot(by_v & second)
    )
    sum_h = dot_split(k_re * xh_re + k_im * xh_im, onehot(by_w & first)) + dot_split(
        k_re * xh_im - k_im * xh_re, onehot(by_w & second)
    )
    sum_d = jnp.where(same_c, sum_d, 0.0)
    sum_h = jnp.where(same_d, sum_h, 0.0)
    row = iota((8, ROWS), 0)
    col = iota((8, ROWS), 1)
    to_a = onehot(row == col >> 6)
    to_b = onehot(row == 4 + ((col >> 4) & 3))
    high_d, low_d = split(sum_d)
    high_h, low_h = split(sum_h)
    total = dot(to_a, high_d) + dot(to_a, low_d) + dot(to_b, high_h) + dot(to_b, low_h)
    if near:
        total += jnp.where(iota((8, 128), 0) >= 4, far_ref[...], 0.0)
    out_ref[...] = total


def mail_kernel(y0, y1, y2, y3, out_ref, *mails):
    total = y0[...] + y1[...] + y2[...] + y3[...]
    for n, mail in enumerate(mails):
        mail[0:16] = total
        mail[16:24] = jnp.broadcast_to(out_ref[4 + n : 5 + n], (8, 128))


def exchange_kernel(y_ref, c_ref, rx_ref, z_ref, out_ref, lhs):
    pad = jnp.zeros((12, 128), F32)
    for j in range(8):
        real = y_ref[j : j + 1]
        imag = y_ref[8 + j : 9 + j]
        for at, top, bottom in ((0, real, imag), (NMU, -imag, real)):
            high, low = split(jnp.concatenate([top, bottom], 0))
            rows = jnp.concatenate([high.astype(F32), low.astype(F32), pad], 0)
            lhs[:, at + j * 128 : at + j * 128 + 128] = rows.astype(BF16)
    acc_re = jnp.zeros((16, 128), F32)
    acc_im = jnp.zeros((16, 128), F32)
    for start in range(0, NG, 512):
        part = pl.ds(start, 512)
        total = dot(lhs[...], z_ref[:, part])
        pot_re = (total[0:1] + total[2:3]) * c_ref[:, part]
        pot_im = (total[1:2] + total[3:4]) * c_ref[:, part]
        rx_re = rx_ref[0:16, part]
        rx_im = rx_ref[16:32, part]
        real = rx_re * pot_re + rx_im * pot_im
        imag = rx_re * pot_im - rx_im * pot_re
        for at in range(0, 512, 128):
            acc_re += real[:, at : at + 128]
            acc_im += imag[:, at : at + 128]
    ones = jnp.ones((8, 128), BF16)
    out = []
    for acc in (acc_re, acc_im):
        high, low = split(acc)
        out.append((dot_t(ones, high) + dot_t(ones, low))[0:1])
    out_ref[...] = jnp.concatenate(out, 0)


def final_kernel(energy_ref, vector_ref, exchange_ref, near_ref, d0, d1, d2, out_ref):
    scale = 1.0 / 256
    terms = near_ref[0:1] + d0[...] + d1[...] + d2[...]
    for part in range(2):
        term = terms[:, part * NT : part * NT + NT]
        out_ref[part : part + 1] = (
            energy_ref[...] * vector_ref[part : part + 1]
            + (2.0 * scale) * exchange_ref[part : part + 1]
            - scale * term
        )


def params(mib):
    return pltpu.CompilerParams(vmem_limit_bytes=mib * 1024 * 1024)


def cost(rows):
    return pl.CostEstimate(flops=2 * rows * 2 * NMU * NG, bytes_accessed=4 * NMU * NG, transcendentals=0)


def pair_call(near, operands):
    out_shape = [jax.ShapeDtypeStruct((8, 128), F32)]
    if near:
        out_shape.append(pltpu.VMEM((32, NG), F32))
    return pl.pallas_call(
        functools.partial(pair_kernel, near),
        in_specs=[VMEM] * 8 + [VMEM] * near + [ANY],
        out_specs=[VMEM] * len(out_shape),
        out_shape=out_shape,
        scratch_shapes=[
            pltpu.VMEM((4 * ROWS + 32 * near, 2 * NMU), BF16),
            pltpu.VMEM((2, 64, NMU), F32),
            pltpu.VMEM((4, 64, NMU), F32),
            pltpu.VMEM((2 * ROWS, 2 * ROWS), F32),
            pltpu.VMEM((2 * ROWS, CHUNK), BF16),
            pltpu.VMEM((2 * ROWS, CHUNK), BF16),
        ],
        compiler_params=params(24),
        cost_estimate=cost(4 * ROWS),
    )(*operands)


def on_device(waves, vector, energies, basis, screening, coulomb, qmap):
    pay = pl.pallas_call(
        pack_kernel,
        in_specs=[ANY] * 2,
        out_specs=VMEM,
        out_shape=pltpu.VMEM((16, WIDTH), BF16),
        scratch_shapes=[pltpu.VMEM((2, NT), F32), pltpu.SemaphoreType.DMA((2,))],
        compiler_params=params(56),
    )(waves.reshape(16, NMU), vector.reshape(2, NT))
    a1 = move(pay, far=1)
    b0 = move(pay, step=1)
    a2 = move(pay, core=1)
    z = basis.reshape(2 * NMU, NG)
    weights = pl.pallas_call(
        weights_kernel,
        in_specs=[SMEM, ANY],
        out_specs=VMEM,
        out_shape=pltpu.VMEM((16, NG), F32),
        scratch_shapes=[pltpu.SemaphoreType.DMA((16,))],
        compiler_params=params(54),
        cost_estimate=pl.CostEstimate(flops=4000000000, bytes_accessed=1024, transcendentals=0),
    )(qmap, screening)
    b1, b2, b3 = (move(b0, y=n) for n in (1, 2, 3))
    a3 = move(a1, core=1)
    y = pl.pallas_call(
        transitions_kernel,
        in_specs=[VMEM] * 4,
        out_specs=VMEM,
        out_shape=jax.ShapeDtypeStruct((16, 128), F32),
        compiler_params=params(8),
    )(pay, a1, a2, a3)
    b_pays = (b0, b1, b2, b3)
    (far_out,) = pair_call(0, (a1, a3, *b_pays, weights, z, y))
    far_sum = far_out[0:1] + move(far_out[1:2], core=1)
    y = y + move(y, z=2) + move(y, z=1) + move(y, z=3)
    near_out, rx = pair_call(1, (pay, a2, *b_pays, weights, z, far_out, y))
    mail = pl.pallas_call(
        mail_kernel,
        in_specs=[VMEM] * 5,
        out_specs=[VMEM] * 4,
        out_shape=[jax.ShapeDtypeStruct((24, 128), F32)] * 4,
        compiler_params=params(4),
    )(y, *(move(y, x=n) for n in (2, 1, 3)), near_out)
    mail = mail[0] + move(mail[2], y=2) + move(mail[1], y=1) + move(mail[3], y=3)
    exchange = pl.pallas_call(
        exchange_kernel,
        in_specs=[VMEM] * 4,
        out_specs=VMEM,
        out_shape=jax.ShapeDtypeStruct((2, NT), F32),
        scratch_shapes=[pltpu.VMEM((16, 2 * NMU), BF16)],
        compiler_params=params(24),
        cost_estimate=cost(128),
    )(mail, coulomb.reshape(1, NG), rx, z)

    out = pl.pallas_call(
        final_kernel,
        in_specs=[VMEM] * 7,
        out_specs=VMEM,
        out_shape=jax.ShapeDtypeStruct((2, NT), F32),
        compiler_params=params(4),
    )(
        energies,
        vector.reshape(2, NT),
        exchange,
        near_out,
        move(near_out[1:2], core=1),
        move(far_sum, far=1),
        move(mail[16:17], step=3),
    )
    return out.reshape(1, 2, NT)


def solution(mesh):
    return jax.shard_map(
        on_device,
        mesh=mesh,
        in_specs=(
            P(("grp", "kin"), None, None, None),
            P(("grp", "kin"), None, None),
            P(("grp", "kin"), None),
            P(),
            P(),
            P(),
            P(("grp", "kin"), None),
        ),
        out_specs=P(("grp", "kin"), None, None),
        check_vma=False,
    )
```

```python
import functools

import jax
import jax.numpy as jnp
from jax import lax
from jax.experimental import pallas as pl
from jax.experimental.pallas import tpu as pltpu
from jax.sharding import PartitionSpec as P

NT = 16
NMU = 1024
NG = 1536
WIDTH = NMU + 128
CHUNK = 1536
ROWS = 128
F32 = jnp.float32
BF16 = jnp.bfloat16
VMEM = pl.BlockSpec(memory_space=pltpu.VMEM)
SMEM = pl.BlockSpec(memory_space=pltpu.SMEM)
ANY = pl.BlockSpec(memory_space=pl.ANY)


def move(value, x=0, z=0, far=0, y=0, core=0, step=0, z_other=None):
    pairs = []
    for a in range(4):
        for b in range(4):
            for c in range(2):
                for d in range(4):
                    for e in range(2):
                        source = (a * 4 + b) * 16 + c * 8 + d * 2 + e
                        turn = z_other if e and z_other is not None else z
                        group = (((a + step) % 4) ^ x) * 4 + (b ^ turn)
                        member = (c ^ far) * 8 + (d ^ y) * 2 + (e ^ core)
                        pairs.append((source, group * 16 + member))
    return lax.ppermute(value, ("grp", "kin"), pairs)


def iota(shape, dim):
    return lax.broadcasted_iota(jnp.int32, shape, dim)


def dot(left, right):
    return jnp.dot(left, right, preferred_element_type=F32)


def dot_t(left, right):
    return lax.dot_general(left, right, (((1,), (1,)), ((), ())), preferred_element_type=F32)


def split(value):
    high = value.astype(BF16)
    return high, (value - high.astype(F32)).astype(BF16)


def dot_split(left, right):
    high, low = split(left)
    return dot(high, right) + dot(low, right)


def onehot(condition):
    return jnp.where(condition, 1.0, 0.0).astype(BF16)


def spread(repeat):
    row = iota((64, 16), 0)
    col = iota((64, 16), 1)
    band = (row >> 2) & 3 if repeat else row & 3
    base = jnp.where(row < 32, 4, 0) + jnp.where((row >> 4) & 1 == 1, 8, 0)
    return onehot(col == band + base)


def conj_product(left_re, left_im, right_re, right_im):
    real = (left_re * right_re + left_im * right_im).astype(BF16)
    imag = (left_re * right_im - left_im * right_re).astype(BF16)
    return real, imag


def pack_kernel(waves, vector, pay_ref, vector_ref, sems):
    copies = (
        pltpu.make_async_copy(vector, vector_ref, sems.at[0]),
        pltpu.make_async_copy(waves, pay_ref.at[:, pl.ds(0, NMU)], sems.at[1]),
    )
    for copy in copies:
        copy.start()
    copies[0].wait()
    coarse = vector_ref[...].astype(BF16).astype(F32)
    real = jnp.broadcast_to(coarse[0:1], (16, 16))
    imag = jnp.broadcast_to(coarse[1:2], (16, 16))
    row = iota((16, 16), 0)
    lane = iota((16, 16), 1)
    of_v = lane >> 2 == row & 3
    by_c = onehot(row & 3 == lane & 3)
    real_v = dot(jnp.where(of_v, real, 0.0).astype(BF16), by_c)
    imag_v = dot(jnp.where(of_v, imag, 0.0).astype(BF16), by_c)
    upper = row < 8
    first = jnp.where(upper, real_v, imag_v)
    second = jnp.where(upper, -imag_v, real_v)
    mixer = jnp.where(lane & 8 == 0, first, second)
    mixer = jnp.where((row & 4 == 0) & (lane & 4 == 4), mixer, 0.0).astype(BF16)
    line_re = jnp.where(row == 12, real, 0.0).astype(BF16)
    line_im = jnp.where(row == 12, imag, 0.0).astype(BF16)
    row = iota((16, 128), 0)
    lane = iota((16, 128), 1)
    block = dot(mixer, onehot(lane == row)) + dot(line_re, onehot(lane == row + 16)) + dot(line_im, onehot(lane == row + 32))
    pay_ref[:, NMU:WIDTH] = block.astype(BF16)
    copies[1].wait()


def weights_kernel(qmap_ref, screening, w_ref, sems):
    own = lax.axis_index("grp")
    member = lax.axis_index("kin")
    partner = (own + 12) & 15
    steps = []
    for m, flip in enumerate((8, 9, 0, 1)):
        from_a = qmap_ref[0, own * 16 + (member ^ flip)]
        for n in range(4):
            from_b = qmap_ref[0, partner * 16 + (member ^ (2 * n))]
            index = (((from_b >> 4) - (from_a >> 4)) & 15) * 16 + ((from_b - from_a) & 15)
            at = m * 4 + n
            copy = pltpu.make_async_copy(screening.at[pl.ds(index, 1)], w_ref.at[pl.ds(at, 1)], sems.at[at])
            copy.start()
            steps.append(copy)
    for copy in steps:
        copy.wait()


def transitions_kernel(a0, a1, a2, a3, y_ref):
    total_re = jnp.zeros((8, NMU), F32)
    total_im = jnp.zeros((8, NMU), F32)
    for pay in (a0, a1, a2, a3):
        waves = pay[:, 0:NMU]
        mixed = dot(pay[:, NMU : NMU + 16], waves)
        waves = waves.astype(F32)
        val_re, val_im = waves[0:8], waves[8:16]
        mix_re, mix_im = mixed[0:8], mixed[8:16]
        total_re += val_re * mix_re + val_im * mix_im
        total_im += val_re * mix_im - val_im * mix_re
    total_re = jnp.sum(total_re, 0, keepdims=True)
    total_im = jnp.sum(total_im, 0, keepdims=True)
    for j in range(8):
        y_ref[j : j + 1] = total_re[:, j * 128 : j * 128 + 128]
        y_ref[8 + j : 9 + j] = total_im[:, j * 128 : j * 128 + 128]


def pair_kernel(near, *refs):
    if near:
        w_ref, z_ref, _, __, acc_ref, rx_ref, lhs, xa, xb, ca, cb = refs[6:]
    else:
        w_ref, z_ref, _, acc_ref, lhs, xa, xb, ca, cb = refs[6:]
    base = 2 * near
    a_pays = refs[0:2]
    b_pays = refs[2:6]
    val = ROWS + 16 * near
    half = ROWS + val

    def put(row, left, right, left_at, right_at):
        real, imag = conj_product(
            left[left_at : left_at + 16],
            left[left_at + 16 : left_at + 32],
            right[right_at : right_at + 16],
            right[right_at + 16 : right_at + 32],
        )
        lhs[row : row + 16, 0:NMU] = real
        lhs[row : row + 16, NMU : 2 * NMU] = -imag
        lhs[half + row : half + row + 16, 0:NMU] = imag
        lhs[half + row : half + row + 16, NMU : 2 * NMU] = real

    rep = spread(True)
    til = spread(False)
    for m in range(2):
        xa[m] = dot(rep, a_pays[m][:, 0:NMU])
    for n in range(4):
        xb[n] = dot(til, b_pays[n][:, 0:NMU])
    for m in range(2):
        for n in range(4):
            row = (m * 4 + n) * 16
            put(row, xa[m], xb[n], 0, 0)
            put(ROWS + row, xa[m], xb[n], 32, 32)
    if near:
        put(2 * ROWS, xa[0], dot(til, a_pays[0][:, 0:NMU]), 32, 0)
    for at in range(0, NG, CHUNK):
        part = pl.ds(at, CHUNK)
        z = z_ref[:, part]
        for side in range(2):
            con = dot(lhs[side * half : side * half + ROWS], z)
            for p in range(8):
                weight = w_ref[4 * base + p : 4 * base + p + 1, part]
                row = side * ROWS + p * 16
                ca[row : row + 16] = (con[p * 16 : p * 16 + 16] * weight).astype(BF16)
            dens = dot(lhs[side * half + ROWS : side * half + half], z)
            cb[side * ROWS : side * ROWS + ROWS] = dens[0:ROWS].astype(BF16)
            if near:
                rx_ref[side * 16 : side * 16 + 16, part] = dens[ROWS:val]
        acc_ref[...] = dot_t(ca[...], cb[...])


def rows_kernel(far_ref, near_ref, *refs):
    a_pays, b_pays, out_ref = refs[0:4], refs[4:8], refs[8]
    half = 2 * ROWS
    pick_row = iota((8, 16), 0)
    pick_col = iota((8, 16), 1)

    def lines(pays):
        total = jnp.zeros((8, 128), F32)
        for n, pay in enumerate(pays):
            total += dot(onehot((pick_row == n) & (pick_col == 12)), pay[:, NMU:WIDTH])
        return total.astype(BF16)

    row = iota((ROWS, 8), 0)
    col = iota((ROWS, 8), 1)
    of_a = onehot(row >> 6 == col)
    of_b = onehot((row >> 4) & 3 == col)
    row = iota((ROWS, 128), 0)
    lane = iota((ROWS, 128), 1)
    same_c = lane & 3 == (row >> 2) & 3
    same_d = lane & 3 == row & 3
    lane = iota((128, ROWS), 0)
    col = iota((128, ROWS), 1)
    by_w = (lane >> 2) & 3 == col & 3
    by_v = (lane >> 2) & 3 == (col >> 2) & 3
    first = lane >> 4 == 1
    second = lane >> 4 == 2
    spread_b = jnp.where(same_d, dot(of_b, lines(b_pays)), 0.0).astype(BF16)
    xd_re = dot(spread_b, onehot(by_w & first))
    xd_im = dot(spread_b, onehot(by_w & second))
    to_re = onehot(by_v & first)
    to_im = onehot(by_v & second)
    pair = iota((ROWS, ROWS), 0) >> 4 == iota((ROWS, ROWS), 1) >> 4
    lane = iota((ROWS, 128), 1)
    col = iota((ROWS, 128), 0)
    by_w = (lane >> 2) & 3 == col & 3
    by_v = (lane >> 2) & 3 == (col >> 2) & 3
    first = lane >> 4 == 0
    second = lane >> 4 == 1
    d_re, d_im = onehot(by_v & first), onehot(by_v & second)
    h_re, h_im = onehot(by_w & first), onehot(by_w & second)
    row = iota((16, ROWS), 0)
    col = iota((16, ROWS), 1)
    to_b = onehot(row == 8 + ((col >> 4) & 3))
    total = jnp.zeros((16, 128), F32)
    for side, acc in enumerate((far_ref, near_ref)):
        spread_a = dot(of_a, lines(a_pays[2 * side : 2 * side + 2]))
        spread_a = jnp.where(same_c, spread_a, 0.0).astype(BF16)
        xh_re = dot(spread_a, to_re)
        xh_im = dot(spread_a, to_im)
        k_re = jnp.where(pair, acc[0:ROWS, 0:ROWS] + acc[ROWS:half, ROWS:half], 0.0)
        k_im = jnp.where(pair, acc[0:ROWS, ROWS:half] - acc[ROWS:half, 0:ROWS], 0.0)
        sum_d = dot_split(k_re * xd_re - k_im * xd_im, d_re) + dot_split(k_re * xd_im + k_im * xd_re, d_im)
        sum_h = dot_split(k_re * xh_re + k_im * xh_im, h_re) + dot_split(k_re * xh_im - k_im * xh_re, h_im)
        high_d, low_d = split(jnp.where(same_c, sum_d, 0.0))
        high_h, low_h = split(jnp.where(same_d, sum_h, 0.0))
        to_a = onehot(row == side + 2 * (col >> 6))
        total += dot(to_a, high_d) + dot(to_a, low_d) + dot(to_b, high_h) + dot(to_b, low_h)
    out_ref[...] = total


def sum_kernel(y0, y1, y2, y3, _, out_ref):
    out_ref[...] = y0[...] + y1[...] + y2[...] + y3[...]


def mail_kernel(y0, y1, rows_ref, *mails):
    total = y0[...] + y1[...]
    for n, mail in enumerate(mails):
        mail[0:16] = total
        mail[16:24] = jnp.broadcast_to(rows_ref[8 + n : 9 + n], (8, 128))


def exchange_kernel(y_ref, c_ref, rx_ref, z_ref, out_ref, lhs):
    pad = jnp.zeros((12, 128), F32)
    for j in range(8):
        real = y_ref[j : j + 1]
        imag = y_ref[8 + j : 9 + j]
        for at, top, bottom in ((0, real, imag), (NMU, -imag, real)):
            high, low = split(jnp.concatenate([top, bottom], 0))
            rows = jnp.concatenate([high.astype(F32), low.astype(F32), pad], 0)
            lhs[:, at + j * 128 : at + j * 128 + 128] = rows.astype(BF16)
    acc_re = jnp.zeros((16, 128), F32)
    acc_im = jnp.zeros((16, 128), F32)
    for start in range(0, NG, 512):
        part = pl.ds(start, 512)
        total = dot(lhs[...], z_ref[:, part])
        pot_re = (total[0:1] + total[2:3]) * c_ref[:, part]
        pot_im = (total[1:2] + total[3:4]) * c_ref[:, part]
        rx_re = rx_ref[0:16, part]
        rx_im = rx_ref[16:32, part]
        real = rx_re * pot_re + rx_im * pot_im
        imag = rx_re * pot_im - rx_im * pot_re
        for at in range(0, 512, 128):
            acc_re += real[:, at : at + 128]
            acc_im += imag[:, at : at + 128]
    ones = jnp.ones((8, 128), BF16)
    out = []
    for acc in (acc_re, acc_im):
        high, low = split(acc)
        out.append((dot_t(ones, high) + dot_t(ones, low))[0:1])
    out_ref[...] = jnp.concatenate(out, 0)


def final_kernel(energy_ref, vector_ref, exchange_ref, near_ref, d_ref, h_ref, out_ref):
    scale = 1.0 / 256
    terms = near_ref[1:2] + d_ref[...] + h_ref[...]
    for part in range(2):
        term = terms[:, part * NT : part * NT + NT]
        out_ref[part : part + 1] = (
            energy_ref[...] * vector_ref[part : part + 1]
            + (2.0 * scale) * exchange_ref[part : part + 1]
            - scale * term
        )


def params(mib):
    return pltpu.CompilerParams(vmem_limit_bytes=mib * 1024 * 1024)


def cost(rows):
    return pl.CostEstimate(flops=2 * rows * 2 * NMU * NG, bytes_accessed=4 * NMU * NG, transcendentals=0)


def pair_call(near, operands):
    out_shape = [pltpu.VMEM((2 * ROWS, 2 * ROWS), F32)]
    if near:
        out_shape.append(pltpu.VMEM((32, NG), F32))
    return pl.pallas_call(
        functools.partial(pair_kernel, near),
        in_specs=[VMEM] * 8 + [ANY] * (1 + near),
        out_specs=[VMEM] * len(out_shape),
        out_shape=out_shape,
        scratch_shapes=[
            pltpu.VMEM((4 * ROWS + 32 * near, 2 * NMU), BF16),
            pltpu.VMEM((2, 64, NMU), F32),
            pltpu.VMEM((4, 64, NMU), F32),
            pltpu.VMEM((2 * ROWS, CHUNK), BF16),
            pltpu.VMEM((2 * ROWS, CHUNK), BF16),
        ],
        compiler_params=params(24),
        cost_estimate=cost(4 * ROWS),
    )(*operands)


def small_call(kernel, shapes, *operands, after=()):
    return pl.pallas_call(
        kernel,
        in_specs=[VMEM] * len(operands) + [ANY] * len(after),
        out_specs=[VMEM] * len(shapes),
        out_shape=[jax.ShapeDtypeStruct(shape, F32) for shape in shapes],
        compiler_params=params(8),
    )(*operands, *after)


def on_device(waves, vector, energies, basis, screening, coulomb, qmap):
    pay = pl.pallas_call(
        pack_kernel,
        in_specs=[ANY] * 2,
        out_specs=VMEM,
        out_shape=pltpu.VMEM((16, WIDTH), BF16),
        scratch_shapes=[pltpu.VMEM((2, NT), F32), pltpu.SemaphoreType.DMA((2,))],
        compiler_params=params(56),
    )(waves.reshape(16, NMU), vector.reshape(2, NT))
    a1 = move(pay, far=1)
    b0 = move(pay, step=1)
    a2 = move(pay, core=1)
    z = basis.reshape(2 * NMU, NG)
    weights = pl.pallas_call(
        weights_kernel,
        in_specs=[SMEM, ANY],
        out_specs=VMEM,
        out_shape=pltpu.VMEM((16, NG), F32),
        scratch_shapes=[pltpu.SemaphoreType.DMA((16,))],
        compiler_params=params(54),
        cost_estimate=pl.CostEstimate(flops=4000000000, bytes_accessed=1024, transcendentals=0),
    )(qmap, screening)
    b1, b2, b3 = (move(b0, y=n) for n in (1, 2, 3))
    a3 = move(a1, core=1)
    y = pl.pallas_call(
        transitions_kernel,
        in_specs=[VMEM] * 4,
        out_specs=VMEM,
        out_shape=jax.ShapeDtypeStruct((16, 128), F32),
        compiler_params=params(8),
    )(pay, a1, a2, a3)
    b_pays = (b0, b1, b2, b3)
    (far_acc,) = pair_call(0, (a1, a3, *b_pays, weights, z, y))
    y = 0.5 * (y + move(y, z=1)) + move(y, z=3, z_other=2)
    near_acc, rx = pair_call(1, (pay, a2, *b_pays, weights, z, far_acc, y))
    (y,) = small_call(sum_kernel, [(16, 128)], y, *(move(y, x=n) for n in (2, 1, 3)), after=(near_acc,))
    other = move(y, core=1)
    (rows,) = small_call(rows_kernel, [(16, 128)], far_acc, near_acc, a1, a3, pay, a2, *b_pays)
    mails = small_call(mail_kernel, [(24, 128)] * 4, y, other, rows)
    mail = mails[0] + move(mails[2], y=2) + move(mails[1], y=1) + move(mails[3], y=3)
    rows = rows[0:2] + move(rows[2:4], core=1)
    exchange = pl.pallas_call(
        exchange_kernel,
        in_specs=[VMEM] * 4,
        out_specs=VMEM,
        out_shape=jax.ShapeDtypeStruct((2, NT), F32),
        scratch_shapes=[pltpu.VMEM((16, 2 * NMU), BF16)],
        compiler_params=params(24),
        cost_estimate=cost(128),
    )(mail, coulomb.reshape(1, NG), rx, z)

    (out,) = small_call(
        final_kernel,
        [(2, NT)],
        energies,
        vector.reshape(2, NT),
        exchange,
        rows,
        move(rows[0:1], far=1),
        move(mail[16:17], step=3),
    )
    return out.reshape(1, 2, NT)


def solution(mesh):
    return jax.shard_map(
        on_device,
        mesh=mesh,
        in_specs=(
            P(("grp", "kin"), None, None, None),
            P(("grp", "kin"), None, None),
            P(("grp", "kin"), None),
            P(),
            P(),
            P(),
            P(("grp", "kin"), None),
        ),
        out_specs=P(("grp", "kin"), None, None),
        check_vma=False,
    )
```

```python
import functools

import jax
import jax.numpy as jnp
from jax import lax
from jax.experimental import pallas as pl
from jax.experimental.pallas import tpu as pltpu
from jax.sharding import PartitionSpec as P

NT = 16
NMU = 1024
NG = 1536
WIDTH = NMU + 128
CHUNK = 1536
ROWS = 128
F32 = jnp.float32
BF16 = jnp.bfloat16
VMEM = pl.BlockSpec(memory_space=pltpu.VMEM)
SMEM = pl.BlockSpec(memory_space=pltpu.SMEM)
ANY = pl.BlockSpec(memory_space=pl.ANY)


def move(value, x=0, z=0, far=0, y=0, core=0, step=0, other=(0, 0)):
    pairs = []
    for a in range(4):
        for b in range(4):
            for c in range(2):
                for d in range(4):
                    for e in range(2):
                        source = (a * 4 + b) * 16 + c * 8 + d * 2 + e
                        to_x, to_z = other if e and any(other) else (x, z)
                        group = (((a + step) % 4) ^ to_x) * 4 + (b ^ to_z)
                        member = (c ^ far) * 8 + (d ^ y) * 2 + (e ^ core)
                        pairs.append((source, group * 16 + member))
    return lax.ppermute(value, ("grp", "kin"), pairs)


def iota(shape, dim):
    return lax.broadcasted_iota(jnp.int32, shape, dim)


def dot(left, right):
    return jnp.dot(left, right, preferred_element_type=F32)


def dot_t(left, right):
    return lax.dot_general(left, right, (((1,), (1,)), ((), ())), preferred_element_type=F32)


def split(value):
    high = value.astype(BF16)
    return high, (value - high.astype(F32)).astype(BF16)


def dot_split(left, right):
    high, low = split(left)
    return dot(high, right) + dot(low, right)


def onehot(condition):
    return jnp.where(condition, 1.0, 0.0).astype(BF16)


def spread(repeat):
    row = iota((64, 16), 0)
    col = iota((64, 16), 1)
    band = (row >> 2) & 3 if repeat else row & 3
    base = jnp.where(row < 32, 4, 0) + jnp.where((row >> 4) & 1 == 1, 8, 0)
    return onehot(col == band + base)


def conj_product(left_re, left_im, right_re, right_im):
    real = (left_re * right_re + left_im * right_im).astype(BF16)
    imag = (left_re * right_im - left_im * right_re).astype(BF16)
    return real, imag


def pack_kernel(waves, vector, pay_ref, vector_ref, sems):
    copies = (
        pltpu.make_async_copy(vector, vector_ref, sems.at[0]),
        pltpu.make_async_copy(waves, pay_ref.at[:, pl.ds(0, NMU)], sems.at[1]),
    )
    for copy in copies:
        copy.start()
    copies[0].wait()
    coarse = vector_ref[...].astype(BF16).astype(F32)
    real = jnp.broadcast_to(coarse[0:1], (16, 16))
    imag = jnp.broadcast_to(coarse[1:2], (16, 16))
    row = iota((16, 16), 0)
    lane = iota((16, 16), 1)
    of_v = lane >> 2 == row & 3
    by_c = onehot(row & 3 == lane & 3)
    real_v = dot(jnp.where(of_v, real, 0.0).astype(BF16), by_c)
    imag_v = dot(jnp.where(of_v, imag, 0.0).astype(BF16), by_c)
    upper = row < 8
    first = jnp.where(upper, real_v, imag_v)
    second = jnp.where(upper, -imag_v, real_v)
    mixer = jnp.where(lane & 8 == 0, first, second)
    mixer = jnp.where((row & 4 == 0) & (lane & 4 == 4), mixer, 0.0).astype(BF16)
    line_re = jnp.where(row == 12, real, 0.0).astype(BF16)
    line_im = jnp.where(row == 12, imag, 0.0).astype(BF16)
    row = iota((16, 128), 0)
    lane = iota((16, 128), 1)
    block = dot(mixer, onehot(lane == row)) + dot(line_re, onehot(lane == row + 16)) + dot(line_im, onehot(lane == row + 32))
    pay_ref[:, NMU:WIDTH] = block.astype(BF16)
    copies[1].wait()


def weights_kernel(qmap_ref, screening, w_ref, sems):
    own = lax.axis_index("grp")
    member = lax.axis_index("kin")
    partner = (own + 12) & 15
    steps = []
    for m, flip in enumerate((8, 9, 0, 1)):
        from_a = qmap_ref[0, own * 16 + (member ^ flip)]
        for n in range(4):
            from_b = qmap_ref[0, partner * 16 + (member ^ (2 * n))]
            index = (((from_b >> 4) - (from_a >> 4)) & 15) * 16 + ((from_b - from_a) & 15)
            at = m * 4 + n
            copy = pltpu.make_async_copy(screening.at[pl.ds(index, 1)], w_ref.at[pl.ds(at, 1)], sems.at[at])
            copy.start()
            steps.append(copy)
    for copy in steps:
        copy.wait()


def transitions_kernel(a0, a1, a2, a3, y_ref):
    total_re = jnp.zeros((8, NMU), F32)
    total_im = jnp.zeros((8, NMU), F32)
    for pay in (a0, a1, a2, a3):
        waves = pay[:, 0:NMU]
        mixed = dot(pay[:, NMU : NMU + 16], waves)
        waves = waves.astype(F32)
        val_re, val_im = waves[0:8], waves[8:16]
        mix_re, mix_im = mixed[0:8], mixed[8:16]
        total_re += val_re * mix_re + val_im * mix_im
        total_im += val_re * mix_im - val_im * mix_re
    total_re = jnp.sum(total_re, 0, keepdims=True)
    total_im = jnp.sum(total_im, 0, keepdims=True)
    for j in range(8):
        y_ref[j : j + 1] = total_re[:, j * 128 : j * 128 + 128]
        y_ref[8 + j : 9 + j] = total_im[:, j * 128 : j * 128 + 128]


def pair_kernel(near, *refs):
    if near:
        w_ref, z_ref, _, __, acc_ref, rx_ref, lhs, xa, xb, ca, cb = refs[6:]
    else:
        w_ref, z_ref, _, acc_ref, lhs, xa, xb, ca, cb = refs[6:]
    base = 2 * near
    a_pays = refs[0:2]
    b_pays = refs[2:6]
    val = ROWS + 16 * near
    half = ROWS + val

    def put(row, left, right, left_at, right_at):
        real, imag = conj_product(
            left[left_at : left_at + 16],
            left[left_at + 16 : left_at + 32],
            right[right_at : right_at + 16],
            right[right_at + 16 : right_at + 32],
        )
        lhs[row : row + 16, 0:NMU] = real
        lhs[row : row + 16, NMU : 2 * NMU] = -imag
        lhs[half + row : half + row + 16, 0:NMU] = imag
        lhs[half + row : half + row + 16, NMU : 2 * NMU] = real

    rep = spread(True)
    til = spread(False)
    for m in range(2):
        xa[m] = dot(rep, a_pays[m][:, 0:NMU])
    for n in range(4):
        xb[n] = dot(til, b_pays[n][:, 0:NMU])
    for m in range(2):
        for n in range(4):
            row = (m * 4 + n) * 16
            put(row, xa[m], xb[n], 0, 0)
            put(ROWS + row, xa[m], xb[n], 32, 32)
    if near:
        put(2 * ROWS, xa[0], dot(til, a_pays[0][:, 0:NMU]), 32, 0)
    for at in range(0, NG, CHUNK):
        part = pl.ds(at, CHUNK)
        z = z_ref[:, part]
        for side in range(2):
            con = dot(lhs[side * half : side * half + ROWS], z)
            for p in range(8):
                weight = w_ref[4 * base + p : 4 * base + p + 1, part]
                row = side * ROWS + p * 16
                ca[row : row + 16] = (con[p * 16 : p * 16 + 16] * weight).astype(BF16)
            dens = dot(lhs[side * half + ROWS : side * half + half], z)
            cb[side * ROWS : side * ROWS + ROWS] = dens[0:ROWS].astype(BF16)
            if near:
                rx_ref[side * 16 : side * 16 + 16, part] = dens[ROWS:val]
        acc_ref[...] = dot_t(ca[...], cb[...])


def rows_kernel(side, acc, *refs):
    a_pays, b_pays, out_ref = refs[0:2], refs[2:6], refs[-1]
    half = 2 * ROWS

    def line(pay):
        return pay[:, NMU:WIDTH].astype(F32)[12:13]

    from_a = jnp.concatenate([jnp.broadcast_to(line(pay), (64, 128)) for pay in a_pays], 0)
    from_b = jnp.concatenate([jnp.broadcast_to(line(pay), (16, 128)) for pay in b_pays] * 2, 0)
    row = iota((ROWS, 128), 0)
    lane = iota((ROWS, 128), 1)
    same_c = lane & 3 == (row >> 2) & 3
    same_d = lane & 3 == row & 3
    from_a = jnp.where(same_c, from_a, 0.0).astype(BF16)
    from_b = jnp.where(same_d, from_b, 0.0).astype(BF16)
    lane = iota((128, half), 0)
    col = iota((128, half), 1)
    part = lane >> 4 == 1 + (col >> 7)
    x_d = dot(from_b, onehot(part & ((lane >> 2) & 3 == col & 3)))
    x_h = dot(from_a, onehot(part & ((lane >> 2) & 3 == (col >> 2) & 3)))
    pair = iota((ROWS, ROWS), 0) >> 4 == iota((ROWS, ROWS), 1) >> 4
    k_re = jnp.where(pair, acc[0:ROWS, 0:ROWS] + acc[ROWS:half, ROWS:half], 0.0)
    k_im = jnp.where(pair, acc[0:ROWS, ROWS:half] - acc[ROWS:half, 0:ROWS], 0.0)
    row = iota((half, 128), 0)
    lane = iota((half, 128), 1)
    part = lane >> 4 == row >> 7

    def fold(real, imag, picked, kept):
        high, low = split(jnp.concatenate([real, imag], 1))
        both = dot(jnp.concatenate([high, low], 0), onehot(part & picked))
        return split(jnp.where(kept, both[0:ROWS] + both[ROWS:half], 0.0))

    re, im = x_d[:, 0:ROWS], x_d[:, ROWS:half]
    terms = fold(k_re * re - k_im * im, k_re * im + k_im * re, (lane >> 2) & 3 == (row >> 2) & 3, same_c)
    re, im = x_h[:, 0:ROWS], x_h[:, ROWS:half]
    terms += fold(k_re * re + k_im * im, k_re * im - k_im * re, (lane >> 2) & 3 == row & 3, same_d)
    row = iota((16, 4 * ROWS), 0)
    col = iota((16, 4 * ROWS), 1)
    to_a = (col < half) & (row == side + 2 * ((col >> 6) & 1))
    to_b = (col >= half) & (row == 8 + ((col >> 4) & 3))
    total = dot(onehot(to_a | to_b), jnp.concatenate(terms, 0))
    if side:
        total += refs[6][...]
    out_ref[...] = total


def join_kernel(y0, y1, _, out_ref):
    out_ref[...] = y0[...] + y1[...]


def half_kernel(y0, y1, y2, _, out_ref):
    out_ref[...] = 0.5 * (y0[...] + y1[...]) + y2[...]


def mail_kernel(y0, y1, rows_ref, *mails):
    total = y0[...] + y1[...]
    for n, mail in enumerate(mails):
        mail[0:16] = total
        mail[16:24] = jnp.broadcast_to(rows_ref[8 + n : 9 + n], (8, 128))


def exchange_kernel(y_ref, c_ref, rx_ref, z_ref, out_ref, lhs):
    pad = jnp.zeros((12, 128), F32)
    for j in range(8):
        real = y_ref[j : j + 1]
        imag = y_ref[8 + j : 9 + j]
        for at, top, bottom in ((0, real, imag), (NMU, -imag, real)):
            high, low = split(jnp.concatenate([top, bottom], 0))
            rows = jnp.concatenate([high.astype(F32), low.astype(F32), pad], 0)
            lhs[:, at + j * 128 : at + j * 128 + 128] = rows.astype(BF16)
    acc_re = jnp.zeros((16, 128), F32)
    acc_im = jnp.zeros((16, 128), F32)
    for start in range(0, NG, 512):
        part = pl.ds(start, 512)
        total = dot(lhs[...], z_ref[:, part])
        pot_re = (total[0:1] + total[2:3]) * c_ref[:, part]
        pot_im = (total[1:2] + total[3:4]) * c_ref[:, part]
        rx_re = rx_ref[0:16, part]
        rx_im = rx_ref[16:32, part]
        real = rx_re * pot_re + rx_im * pot_im
        imag = rx_re * pot_im - rx_im * pot_re
        for at in range(0, 512, 128):
            acc_re += real[:, at : at + 128]
            acc_im += imag[:, at : at + 128]
    ones = jnp.ones((8, 128), BF16)
    out = []
    for acc in (acc_re, acc_im):
        high, low = split(acc)
        out.append((dot_t(ones, high) + dot_t(ones, low))[0:1])
    out_ref[...] = jnp.concatenate(out, 0)


def final_kernel(energy_ref, vector_ref, exchange_ref, near_ref, d_ref, h_ref, out_ref):
    scale = 1.0 / 256
    terms = near_ref[1:2] + d_ref[...] + h_ref[...]
    for part in range(2):
        term = terms[:, part * NT : part * NT + NT]
        out_ref[part : part + 1] = (
            energy_ref[...] * vector_ref[part : part + 1]
            + (2.0 * scale) * exchange_ref[part : part + 1]
            - scale * term
        )


def params(mib):
    return pltpu.CompilerParams(vmem_limit_bytes=mib * 1024 * 1024)


def cost(rows):
    return pl.CostEstimate(flops=2 * rows * 2 * NMU * NG, bytes_accessed=4 * NMU * NG, transcendentals=0)


def pair_call(near, operands):
    out_shape = [pltpu.VMEM((2 * ROWS, 2 * ROWS), F32)]
    if near:
        out_shape.append(pltpu.VMEM((32, NG), F32))
    return pl.pallas_call(
        functools.partial(pair_kernel, near),
        in_specs=[VMEM] * 8 + [ANY] * (1 + near),
        out_specs=[VMEM] * len(out_shape),
        out_shape=out_shape,
        scratch_shapes=[
            pltpu.VMEM((4 * ROWS + 32 * near, 2 * NMU), BF16),
            pltpu.VMEM((2, 64, NMU), F32),
            pltpu.VMEM((4, 64, NMU), F32),
            pltpu.VMEM((2 * ROWS, CHUNK), BF16),
            pltpu.VMEM((2 * ROWS, CHUNK), BF16),
        ],
        compiler_params=params(24),
        cost_estimate=cost(4 * ROWS),
    )(*operands)


def small_call(kernel, shapes, *operands, after=()):
    return pl.pallas_call(
        kernel,
        in_specs=[VMEM] * len(operands) + [ANY] * len(after),
        out_specs=[VMEM] * len(shapes),
        out_shape=[jax.ShapeDtypeStruct(shape, F32) for shape in shapes],
        compiler_params=params(8),
    )(*operands, *after)


def on_device(waves, vector, energies, basis, screening, coulomb, qmap):
    pay = pl.pallas_call(
        pack_kernel,
        in_specs=[ANY] * 2,
        out_specs=VMEM,
        out_shape=pltpu.VMEM((16, WIDTH), BF16),
        scratch_shapes=[pltpu.VMEM((2, NT), F32), pltpu.SemaphoreType.DMA((2,))],
        compiler_params=params(56),
    )(waves.reshape(16, NMU), vector.reshape(2, NT))
    a1 = move(pay, far=1)
    b0 = move(pay, step=1)
    a2 = move(pay, core=1)
    z = basis.reshape(2 * NMU, NG)
    weights = pl.pallas_call(
        weights_kernel,
        in_specs=[SMEM, ANY],
        out_specs=VMEM,
        out_shape=pltpu.VMEM((16, NG), F32),
        scratch_shapes=[pltpu.SemaphoreType.DMA((16,))],
        compiler_params=params(54),
        cost_estimate=pl.CostEstimate(flops=4000000000, bytes_accessed=1024, transcendentals=0),
    )(qmap, screening)
    b1, b2, b3 = (move(b0, y=n) for n in (1, 2, 3))
    a3 = move(a1, core=1)
    y = pl.pallas_call(
        transitions_kernel,
        in_specs=[VMEM] * 4,
        out_specs=VMEM,
        out_shape=jax.ShapeDtypeStruct((16, 128), F32),
        compiler_params=params(8),
    )(pay, a1, a2, a3)
    b_pays = (b0, b1, b2, b3)
    (far_acc,) = pair_call(0, (a1, a3, *b_pays, weights, z, y))
    (y,) = small_call(half_kernel, [(16, 128)], y, move(y, z=1), move(y, z=3, other=(0, 2)), after=(far_acc,))
    swapped = move(y, core=1)
    (far_rows,) = small_call(functools.partial(rows_kernel, 0), [(16, 128)], far_acc, a1, a3, *b_pays)
    (y,) = small_call(join_kernel, [(16, 128)], y, swapped, after=(far_rows,))
    near_acc, rx = pair_call(1, (pay, a2, *b_pays, weights, z, far_rows, y))
    (y,) = small_call(half_kernel, [(16, 128)], y, move(y, x=1), move(y, x=3, other=(2, 0)), after=(near_acc,))
    swapped = move(y, core=1)
    (rows,) = small_call(functools.partial(rows_kernel, 1), [(16, 128)], near_acc, pay, a2, *b_pays, far_rows)
    mails = small_call(mail_kernel, [(24, 128)] * 4, y, swapped, rows)
    mail = mails[0] + move(mails[2], y=2) + move(mails[1], y=1) + move(mails[3], y=3)
    rows = rows[0:2] + move(rows[2:4], core=1)
    exchange = pl.pallas_call(
        exchange_kernel,
        in_specs=[VMEM] * 4,
        out_specs=VMEM,
        out_shape=jax.ShapeDtypeStruct((2, NT), F32),
        scratch_shapes=[pltpu.VMEM((16, 2 * NMU), BF16)],
        compiler_params=params(24),
        cost_estimate=cost(128),
    )(mail, coulomb.reshape(1, NG), rx, z)

    (out,) = small_call(
        final_kernel,
        [(2, NT)],
        energies,
        vector.reshape(2, NT),
        exchange,
        rows,
        move(rows[0:1], far=1),
        move(mail[16:17], step=3),
    )
    return out.reshape(1, 2, NT)


def solution(mesh):
    return jax.shard_map(
        on_device,
        mesh=mesh,
        in_specs=(
            P(("grp", "kin"), None, None, None),
            P(("grp", "kin"), None, None),
            P(("grp", "kin"), None),
            P(),
            P(),
            P(),
            P(("grp", "kin"), None),
        ),
        out_specs=P(("grp", "kin"), None, None),
        check_vma=False,
    )
```

```python
import functools

import jax
import jax.numpy as jnp
from jax import lax
from jax.experimental import pallas as pl
from jax.experimental.pallas import tpu as pltpu
from jax.sharding import PartitionSpec as P

NT = 16
NMU = 1024
NG = 1536
WIDTH = NMU + 128
ROWS = 128
F32 = jnp.float32
BF16 = jnp.bfloat16
VMEM = pl.BlockSpec(memory_space=pltpu.VMEM)
SMEM = pl.BlockSpec(memory_space=pltpu.SMEM)
ANY = pl.BlockSpec(memory_space=pl.ANY)


def move(value, x=0, z=0, far=0, y=0, core=0, step=0, other=(0, 0)):
    pairs = []
    for a in range(4):
        for b in range(4):
            for c in range(2):
                for d in range(4):
                    for e in range(2):
                        source = (a * 4 + b) * 16 + c * 8 + d * 2 + e
                        to_x, to_z = other if e and any(other) else (x, z)
                        group = (((a + step) % 4) ^ to_x) * 4 + (b ^ to_z)
                        member = (c ^ far) * 8 + (d ^ y) * 2 + (e ^ core)
                        pairs.append((source, group * 16 + member))
    return lax.ppermute(value, ("grp", "kin"), pairs)


def iota(shape, dim):
    return lax.broadcasted_iota(jnp.int32, shape, dim)


def dot(left, right):
    return jnp.dot(left, right, preferred_element_type=F32)


def dot_t(left, right):
    return lax.dot_general(left, right, (((1,), (1,)), ((), ())), preferred_element_type=F32)


def split(value):
    high = value.astype(BF16)
    return high, (value - high.astype(F32)).astype(BF16)


def dot_split(left, right):
    high, low = split(left)
    return dot(high, right) + dot(low, right)


def onehot(condition):
    return jnp.where(condition, 1.0, 0.0).astype(BF16)


def spread(repeat):
    row = iota((64, 16), 0)
    col = iota((64, 16), 1)
    band = (row >> 2) & 3 if repeat else row & 3
    base = jnp.where(row < 32, 4, 0) + jnp.where((row >> 4) & 1 == 1, 8, 0)
    return onehot(col == band + base)


def conj_product(left_re, left_im, right_re, right_im):
    real = (left_re * right_re + left_im * right_im).astype(BF16)
    imag = (left_re * right_im - left_im * right_re).astype(BF16)
    return real, imag


def pack_kernel(waves, vector, pay_ref, vector_ref, sems):
    copies = (
        pltpu.make_async_copy(vector, vector_ref, sems.at[0]),
        pltpu.make_async_copy(waves, pay_ref.at[:, pl.ds(0, NMU)], sems.at[1]),
    )
    for copy in copies:
        copy.start()
    copies[0].wait()
    coarse = vector_ref[...].astype(BF16).astype(F32)
    real = jnp.broadcast_to(coarse[0:1], (16, 16))
    imag = jnp.broadcast_to(coarse[1:2], (16, 16))
    row = iota((16, 16), 0)
    lane = iota((16, 16), 1)
    of_v = lane >> 2 == row & 3
    by_c = onehot(row & 3 == lane & 3)
    real_v = dot(jnp.where(of_v, real, 0.0).astype(BF16), by_c)
    imag_v = dot(jnp.where(of_v, imag, 0.0).astype(BF16), by_c)
    upper = row < 8
    first = jnp.where(upper, real_v, imag_v)
    second = jnp.where(upper, -imag_v, real_v)
    mixer = jnp.where(lane & 8 == 0, first, second)
    mixer = jnp.where((row & 4 == 0) & (lane & 4 == 4), mixer, 0.0).astype(BF16)
    line_re = jnp.where(row == 12, real, 0.0).astype(BF16)
    line_im = jnp.where(row == 12, imag, 0.0).astype(BF16)
    row = iota((16, 128), 0)
    lane = iota((16, 128), 1)
    block = dot(mixer, onehot(lane == row)) + dot(line_re, onehot(lane == row + 16)) + dot(line_im, onehot(lane == row + 32))
    pay_ref[:, NMU:WIDTH] = block.astype(BF16)
    copies[1].wait()


def weights_kernel(qmap_ref, screening, w_ref, sems):
    own = lax.axis_index("grp")
    member = lax.axis_index("kin")
    partner = (own + 12) & 15
    steps = []
    for m, flip in enumerate((8, 9, 0, 1)):
        from_a = qmap_ref[0, own * 16 + (member ^ flip)]
        for n in range(4):
            from_b = qmap_ref[0, partner * 16 + (member ^ (2 * n))]
            index = (((from_b >> 4) - (from_a >> 4)) & 15) * 16 + ((from_b - from_a) & 15)
            at = m * 4 + n
            copy = pltpu.make_async_copy(screening.at[pl.ds(index, 1)], w_ref.at[pl.ds(at, 1)], sems.at[at])
            copy.start()
            steps.append(copy)
    for copy in steps:
        copy.wait()


def transitions_kernel(a0, a1, a2, a3, y_ref):
    total_re = jnp.zeros((8, NMU), F32)
    total_im = jnp.zeros((8, NMU), F32)
    for pay in (a0, a1, a2, a3):
        waves = pay[:, 0:NMU]
        mixed = dot(pay[:, NMU : NMU + 16], waves)
        waves = waves.astype(F32)
        val_re, val_im = waves[0:8], waves[8:16]
        mix_re, mix_im = mixed[0:8], mixed[8:16]
        total_re += val_re * mix_re + val_im * mix_im
        total_im += val_re * mix_im - val_im * mix_re
    total_re = jnp.sum(total_re, 0, keepdims=True)
    total_im = jnp.sum(total_im, 0, keepdims=True)
    for j in range(8):
        y_ref[j : j + 1] = total_re[:, j * 128 : j * 128 + 128]
        y_ref[8 + j : 9 + j] = total_im[:, j * 128 : j * 128 + 128]


def build_kernel(near, a_near, a_pair, b0, b1, b2, b3, *refs):
    lhs, xa, xb = refs[-3:]
    a_pays = (a_near, a_pair)
    half = lhs.shape[0] // 2

    def put(row, left, right, left_at, right_at):
        real, imag = conj_product(
            left[left_at : left_at + 16],
            left[left_at + 16 : left_at + 32],
            right[right_at : right_at + 16],
            right[right_at + 16 : right_at + 32],
        )
        lhs[row : row + 16, 0:NMU] = real
        lhs[row : row + 16, NMU : 2 * NMU] = -imag
        lhs[half + row : half + row + 16, 0:NMU] = imag
        lhs[half + row : half + row + 16, NMU : 2 * NMU] = real

    rep = spread(True)
    til = spread(False)
    for m in range(2):
        xa[m] = dot(rep, a_pays[m][:, 0:NMU])
    for n, pay in enumerate((b0, b1, b2, b3)):
        xb[n] = dot(til, pay[:, 0:NMU])
    for m in range(2):
        for n in range(4):
            row = (m * 4 + n) * 16
            put(row, xa[m], xb[n], 0, 0)
            put(ROWS + row, xa[m], xb[n], 32, 32)
    if near:
        put(2 * ROWS, xa[0], dot(til, a_pays[0][:, 0:NMU]), 32, 0)


def product_kernel(near, lhs, w_ref, z_ref, acc_ref, rx_ref, ca, cb):
    half = lhs.shape[0] // 2
    z = z_ref[...]
    for side in range(2):
        con = dot(lhs[side * half : side * half + ROWS], z)
        for p in range(8):
            weight = w_ref[8 * near + p : 8 * near + p + 1]
            row = side * ROWS + p * 16
            ca[row : row + 16] = (con[p * 16 : p * 16 + 16] * weight).astype(BF16)
        dens = dot(lhs[side * half + ROWS : side * half + half], z)
        cb[side * ROWS : side * ROWS + ROWS] = dens[0:ROWS].astype(BF16)
        if near:
            rx_ref[side * 16 : side * 16 + 16] = dens[ROWS : ROWS + 16]
    acc_ref[...] = dot_t(ca[...], cb[...])


def far_kernel(a_near, a_pair, b0, b1, b2, b3, w_ref, z_ref, _, acc_ref, lhs, xa, xb, ca, cb):
    build_kernel(0, a_near, a_pair, b0, b1, b2, b3, lhs, xa, xb)
    product_kernel(0, lhs, w_ref, z_ref, acc_ref, None, ca, cb)


def near_kernel(lhs, w_ref, z_ref, _, acc_ref, rx_ref, ca, cb):
    product_kernel(1, lhs, w_ref, z_ref, acc_ref, rx_ref, ca, cb)


def rows_kernel(side, acc, *refs):
    a_pays, b_pays, out_ref = refs[0:2], refs[2:6], refs[-1]
    half = 2 * ROWS

    def line(pay):
        return pay[:, NMU:WIDTH].astype(F32)[12:13]

    from_a = jnp.concatenate([jnp.broadcast_to(line(pay), (64, 128)) for pay in a_pays], 0)
    from_b = jnp.concatenate([jnp.broadcast_to(line(pay), (16, 128)) for pay in b_pays] * 2, 0)
    row = iota((ROWS, 128), 0)
    lane = iota((ROWS, 128), 1)
    same_c = lane & 3 == (row >> 2) & 3
    same_d = lane & 3 == row & 3
    from_a = jnp.where(same_c, from_a, 0.0).astype(BF16)
    from_b = jnp.where(same_d, from_b, 0.0).astype(BF16)
    lane = iota((128, half), 0)
    col = iota((128, half), 1)
    part = lane >> 4 == 1 + (col >> 7)
    x_d = dot(from_b, onehot(part & ((lane >> 2) & 3 == col & 3)))
    x_h = dot(from_a, onehot(part & ((lane >> 2) & 3 == (col >> 2) & 3)))
    pair = iota((ROWS, ROWS), 0) >> 4 == iota((ROWS, ROWS), 1) >> 4
    k_re = jnp.where(pair, acc[0:ROWS, 0:ROWS] + acc[ROWS:half, ROWS:half], 0.0)
    k_im = jnp.where(pair, acc[0:ROWS, ROWS:half] - acc[ROWS:half, 0:ROWS], 0.0)
    row = iota((half, 128), 0)
    lane = iota((half, 128), 1)
    part = lane >> 4 == row >> 7

    def fold(real, imag, picked, kept):
        high, low = split(jnp.concatenate([real, imag], 1))
        both = dot(jnp.concatenate([high, low], 0), onehot(part & picked))
        return split(jnp.where(kept, both[0:ROWS] + both[ROWS:half], 0.0))

    re, im = x_d[:, 0:ROWS], x_d[:, ROWS:half]
    terms = fold(k_re * re - k_im * im, k_re * im + k_im * re, (lane >> 2) & 3 == (row >> 2) & 3, same_c)
    re, im = x_h[:, 0:ROWS], x_h[:, ROWS:half]
    terms += fold(k_re * re + k_im * im, k_re * im - k_im * re, (lane >> 2) & 3 == row & 3, same_d)
    row = iota((16, 4 * ROWS), 0)
    col = iota((16, 4 * ROWS), 1)
    to_a = (col < half) & (row == side + 2 * ((col >> 6) & 1))
    to_b = (col >= half) & (row == 8 + ((col >> 4) & 3))
    total = dot(onehot(to_a | to_b), jnp.concatenate(terms, 0))
    if side:
        total += refs[6][...]
    out_ref[...] = total


def join_kernel(y0, y1, _, __, out_ref):
    out_ref[...] = y0[...] + y1[...]


def half_kernel(y0, y1, y2, _, out_ref):
    out_ref[...] = 0.5 * (y0[...] + y1[...]) + y2[...]


def mail_kernel(y0, y1, rows_ref, *mails):
    total = y0[...] + y1[...]
    for n, mail in enumerate(mails):
        mail[0:16] = total
        mail[16:24] = jnp.broadcast_to(rows_ref[8 + n : 9 + n], (8, 128))


def exchange_kernel(y_ref, c_ref, rx_ref, z_ref, out_ref, lhs):
    pad = jnp.zeros((12, 128), F32)
    for j in range(8):
        real = y_ref[j : j + 1]
        imag = y_ref[8 + j : 9 + j]
        for at, top, bottom in ((0, real, imag), (NMU, -imag, real)):
            high, low = split(jnp.concatenate([top, bottom], 0))
            rows = jnp.concatenate([high.astype(F32), low.astype(F32), pad], 0)
            lhs[:, at + j * 128 : at + j * 128 + 128] = rows.astype(BF16)
    acc_re = jnp.zeros((16, 128), F32)
    acc_im = jnp.zeros((16, 128), F32)
    for start in range(0, NG, 512):
        part = pl.ds(start, 512)
        total = dot(lhs[...], z_ref[:, part])
        pot_re = (total[0:1] + total[2:3]) * c_ref[:, part]
        pot_im = (total[1:2] + total[3:4]) * c_ref[:, part]
        rx_re = rx_ref[0:16, part]
        rx_im = rx_ref[16:32, part]
        real = rx_re * pot_re + rx_im * pot_im
        imag = rx_re * pot_im - rx_im * pot_re
        for at in range(0, 512, 128):
            acc_re += real[:, at : at + 128]
            acc_im += imag[:, at : at + 128]
    ones = jnp.ones((8, 128), BF16)
    out = []
    for acc in (acc_re, acc_im):
        high, low = split(acc)
        out.append((dot_t(ones, high) + dot_t(ones, low))[0:1])
    out_ref[...] = jnp.concatenate(out, 0)


def final_kernel(energy_ref, vector_ref, exchange_ref, near_ref, d_ref, h_ref, out_ref):
    scale = 1.0 / 256
    terms = near_ref[1:2] + d_ref[...] + h_ref[...]
    for part in range(2):
        term = terms[:, part * NT : part * NT + NT]
        out_ref[part : part + 1] = (
            energy_ref[...] * vector_ref[part : part + 1]
            + (2.0 * scale) * exchange_ref[part : part + 1]
            - scale * term
        )


def params(mib):
    return pltpu.CompilerParams(vmem_limit_bytes=mib * 1024 * 1024)


def cost(rows):
    return pl.CostEstimate(flops=2 * rows * 2 * NMU * NG, bytes_accessed=4 * NMU * NG, transcendentals=0)


def spreads():
    return [pltpu.VMEM((2, 64, NMU), F32), pltpu.VMEM((4, 64, NMU), F32)]


def far_call(*operands):
    return pl.pallas_call(
        far_kernel,
        in_specs=[VMEM] * 8 + [ANY],
        out_specs=VMEM,
        out_shape=pltpu.VMEM((2 * ROWS, 2 * ROWS), F32),
        scratch_shapes=[pltpu.VMEM((4 * ROWS, 2 * NMU), BF16)] + spreads() + [pltpu.VMEM((2 * ROWS, NG), BF16)] * 2,
        compiler_params=params(24),
        cost_estimate=cost(4 * ROWS),
    )(*operands)


def build_call(*operands):
    return pl.pallas_call(
        functools.partial(build_kernel, 1),
        in_specs=[VMEM] * 6 + [ANY],
        out_specs=VMEM,
        out_shape=pltpu.VMEM((4 * ROWS + 32, 2 * NMU), BF16),
        scratch_shapes=spreads(),
        compiler_params=params(12),
    )(*operands)


def near_call(*operands):
    return pl.pallas_call(
        near_kernel,
        in_specs=[VMEM] * 3 + [ANY],
        out_specs=[VMEM] * 2,
        out_shape=[pltpu.VMEM((2 * ROWS, 2 * ROWS), F32), pltpu.VMEM((32, NG), F32)],
        scratch_shapes=[pltpu.VMEM((2 * ROWS, NG), BF16)] * 2,
        compiler_params=params(24),
        cost_estimate=cost(4 * ROWS),
    )(*operands)


def small_call(kernel, shapes, *operands, after=()):
    return pl.pallas_call(
        kernel,
        in_specs=[VMEM] * len(operands) + [ANY] * len(after),
        out_specs=[VMEM] * len(shapes),
        out_shape=[jax.ShapeDtypeStruct(shape, F32) for shape in shapes],
        compiler_params=params(8),
    )(*operands, *after)


def on_device(waves, vector, energies, basis, screening, coulomb, qmap):
    pay = pl.pallas_call(
        pack_kernel,
        in_specs=[ANY] * 2,
        out_specs=VMEM,
        out_shape=pltpu.VMEM((16, WIDTH), BF16),
        scratch_shapes=[pltpu.VMEM((2, NT), F32), pltpu.SemaphoreType.DMA((2,))],
        compiler_params=params(56),
    )(waves.reshape(16, NMU), vector.reshape(2, NT))
    a1 = move(pay, far=1)
    b0 = move(pay, step=1)
    a2 = move(pay, core=1)
    z = basis.reshape(2 * NMU, NG)
    weights = pl.pallas_call(
        weights_kernel,
        in_specs=[SMEM, ANY],
        out_specs=VMEM,
        out_shape=pltpu.VMEM((16, NG), F32),
        scratch_shapes=[pltpu.SemaphoreType.DMA((16,))],
        compiler_params=params(54),
        cost_estimate=pl.CostEstimate(flops=4000000000, bytes_accessed=1024, transcendentals=0),
    )(qmap, screening)
    b1, b2, b3 = (move(b0, y=n) for n in (1, 2, 3))
    a3 = move(a1, core=1)
    y = pl.pallas_call(
        transitions_kernel,
        in_specs=[VMEM] * 4,
        out_specs=VMEM,
        out_shape=jax.ShapeDtypeStruct((16, 128), F32),
        compiler_params=params(8),
    )(pay, a1, a2, a3)
    b_pays = (b0, b1, b2, b3)
    far_acc = far_call(a1, a3, *b_pays, weights, z, y)
    (y,) = small_call(half_kernel, [(16, 128)], y, move(y, z=1), move(y, z=3, other=(0, 2)), after=(far_acc,))
    swapped = move(y, core=1)
    (far_rows,) = small_call(functools.partial(rows_kernel, 0), [(16, 128)], far_acc, a1, a3, *b_pays)
    lhs = build_call(pay, a2, *b_pays, far_acc)
    (y,) = small_call(join_kernel, [(16, 128)], y, swapped, after=(far_rows, lhs))
    near_acc, rx = near_call(lhs, weights, z, y)
    (y,) = small_call(half_kernel, [(16, 128)], y, move(y, x=1), move(y, x=3, other=(2, 0)), after=(near_acc,))
    swapped = move(y, core=1)
    (rows,) = small_call(functools.partial(rows_kernel, 1), [(16, 128)], near_acc, pay, a2, *b_pays, far_rows)
    mails = small_call(mail_kernel, [(24, 128)] * 4, y, swapped, rows)
    mail = mails[0] + move(mails[2], y=2) + move(mails[1], y=1) + move(mails[3], y=3)
    rows = rows[0:2] + move(rows[2:4], core=1)
    exchange = pl.pallas_call(
        exchange_kernel,
        in_specs=[VMEM] * 4,
        out_specs=VMEM,
        out_shape=jax.ShapeDtypeStruct((2, NT), F32),
        scratch_shapes=[pltpu.VMEM((16, 2 * NMU), BF16)],
        compiler_params=params(24),
        cost_estimate=cost(128),
    )(mail, coulomb.reshape(1, NG), rx, z)

    (out,) = small_call(
        final_kernel,
        [(2, NT)],
        energies,
        vector.reshape(2, NT),
        exchange,
        rows,
        move(rows[0:1], far=1),
        move(mail[16:17], step=3),
    )
    return out.reshape(1, 2, NT)


def solution(mesh):
    return jax.shard_map(
        on_device,
        mesh=mesh,
        in_specs=(
            P(("grp", "kin"), None, None, None),
            P(("grp", "kin"), None, None),
            P(("grp", "kin"), None),
            P(),
            P(),
            P(),
            P(("grp", "kin"), None),
        ),
        out_specs=P(("grp", "kin"), None, None),
        check_vma=False,
    )
```

```python
import functools

import jax
import jax.numpy as jnp
from jax import lax
from jax.experimental import pallas as pl
from jax.experimental.pallas import tpu as pltpu
from jax.sharding import PartitionSpec as P

NT = 16
NMU = 1024
NG = 1536
WIDTH = NMU + 128
ROWS = 128
F32 = jnp.float32
BF16 = jnp.bfloat16
VMEM = pl.BlockSpec(memory_space=pltpu.VMEM)
SMEM = pl.BlockSpec(memory_space=pltpu.SMEM)
ANY = pl.BlockSpec(memory_space=pl.ANY)


def move(value, x=0, z=0, far=0, y=0, core=0, step=0, other=(0, 0)):
    pairs = []
    for a in range(4):
        for b in range(4):
            for c in range(2):
                for d in range(4):
                    for e in range(2):
                        source = (a * 4 + b) * 16 + c * 8 + d * 2 + e
                        to_x, to_z = other if e and any(other) else (x, z)
                        group = (((a + step) % 4) ^ to_x) * 4 + (b ^ to_z)
                        member = (c ^ far) * 8 + (d ^ y) * 2 + (e ^ core)
                        pairs.append((source, group * 16 + member))
    return lax.ppermute(value, ("grp", "kin"), pairs)


def iota(shape, dim):
    return lax.broadcasted_iota(jnp.int32, shape, dim)


def dot(left, right):
    return jnp.dot(left, right, preferred_element_type=F32)


def dot_t(left, right):
    return lax.dot_general(left, right, (((1,), (1,)), ((), ())), preferred_element_type=F32)


def split(value):
    high = value.astype(BF16)
    return high, (value - high.astype(F32)).astype(BF16)


def dot_split(left, right):
    high, low = split(left)
    return dot(high, right) + dot(low, right)


def onehot(condition):
    return jnp.where(condition, 1.0, 0.0).astype(BF16)


def spread(repeat):
    row = iota((64, 16), 0)
    col = iota((64, 16), 1)
    band = (row >> 2) & 3 if repeat else row & 3
    base = jnp.where(row < 32, 4, 0) + jnp.where((row >> 4) & 1 == 1, 8, 0)
    return onehot(col == band + base)


def conj_product(left_re, left_im, right_re, right_im):
    real = (left_re * right_re + left_im * right_im).astype(BF16)
    imag = (left_re * right_im - left_im * right_re).astype(BF16)
    return real, imag


def pack_kernel(waves, vector, pay_ref, vector_ref, sems):
    copies = (
        pltpu.make_async_copy(vector, vector_ref, sems.at[0]),
        pltpu.make_async_copy(waves, pay_ref.at[:, pl.ds(0, NMU)], sems.at[1]),
    )
    for copy in copies:
        copy.start()
    copies[0].wait()
    coarse = vector_ref[...].astype(BF16).astype(F32)
    real = jnp.broadcast_to(coarse[0:1], (16, 16))
    imag = jnp.broadcast_to(coarse[1:2], (16, 16))
    row = iota((16, 16), 0)
    lane = iota((16, 16), 1)
    of_v = lane >> 2 == row & 3
    by_c = onehot(row & 3 == lane & 3)
    real_v = dot(jnp.where(of_v, real, 0.0).astype(BF16), by_c)
    imag_v = dot(jnp.where(of_v, imag, 0.0).astype(BF16), by_c)
    upper = row < 8
    first = jnp.where(upper, real_v, imag_v)
    second = jnp.where(upper, -imag_v, real_v)
    mixer = jnp.where(lane & 8 == 0, first, second)
    mixer = jnp.where((row & 4 == 0) & (lane & 4 == 4), mixer, 0.0).astype(BF16)
    line_re = jnp.where(row == 12, real, 0.0).astype(BF16)
    line_im = jnp.where(row == 12, imag, 0.0).astype(BF16)
    row = iota((16, 128), 0)
    lane = iota((16, 128), 1)
    block = dot(mixer, onehot(lane == row)) + dot(line_re, onehot(lane == row + 16)) + dot(line_im, onehot(lane == row + 32))
    pay_ref[:, NMU:WIDTH] = block.astype(BF16)
    copies[1].wait()


def fetch_rows(qmap_ref, screening, w_ref, sems):
    own = lax.axis_index("grp")
    member = lax.axis_index("kin")
    partner = (own + 12) & 15
    copies = []
    for m, flip in enumerate((8, 9, 0, 1)):
        from_a = qmap_ref[0, own * 16 + (member ^ flip)]
        for n in range(4):
            from_b = qmap_ref[0, partner * 16 + (member ^ (2 * n))]
            index = (((from_b >> 4) - (from_a >> 4)) & 15) * 16 + ((from_b - from_a) & 15)
            at = m * 4 + n
            copy = pltpu.make_async_copy(screening.at[pl.ds(index, 1)], w_ref.at[pl.ds(at, 1)], sems.at[at])
            copy.start()
            copies.append(copy)
    return copies


def place_kernel(source, out_ref):
    out_ref[...] = jnp.broadcast_to(source[:, 0:128], (8, 128))


def transitions_kernel(a0, a1, a2, a3, y_ref):
    total_re = jnp.zeros((8, NMU), F32)
    total_im = jnp.zeros((8, NMU), F32)
    for pay in (a0, a1, a2, a3):
        waves = pay[:, 0:NMU]
        mixed = dot(pay[:, NMU : NMU + 16], waves)
        waves = waves.astype(F32)
        val_re, val_im = waves[0:8], waves[8:16]
        mix_re, mix_im = mixed[0:8], mixed[8:16]
        total_re += val_re * mix_re + val_im * mix_im
        total_im += val_re * mix_im - val_im * mix_re
    total_re = jnp.sum(total_re, 0, keepdims=True)
    total_im = jnp.sum(total_im, 0, keepdims=True)
    for j in range(8):
        y_ref[j : j + 1] = total_re[:, j * 128 : j * 128 + 128]
        y_ref[8 + j : 9 + j] = total_im[:, j * 128 : j * 128 + 128]


def build_kernel(near, a_near, a_pair, b0, b1, b2, b3, *refs):
    lhs, xa, xb = refs[-3:]
    a_pays = (a_near, a_pair)
    half = lhs.shape[0] // 2

    def put(row, left, right, left_at, right_at):
        real, imag = conj_product(
            left[left_at : left_at + 16],
            left[left_at + 16 : left_at + 32],
            right[right_at : right_at + 16],
            right[right_at + 16 : right_at + 32],
        )
        lhs[row : row + 16, 0:NMU] = real
        lhs[row : row + 16, NMU : 2 * NMU] = -imag
        lhs[half + row : half + row + 16, 0:NMU] = imag
        lhs[half + row : half + row + 16, NMU : 2 * NMU] = real

    rep = spread(True)
    til = spread(False)
    for m in range(2):
        xa[m] = dot(rep, a_pays[m][:, 0:NMU])
    for n, pay in enumerate((b0, b1, b2, b3)):
        xb[n] = dot(til, pay[:, 0:NMU])
    for m in range(2):
        for n in range(4):
            row = (m * 4 + n) * 16
            put(row, xa[m], xb[n], 0, 0)
            put(ROWS + row, xa[m], xb[n], 32, 32)
    if near:
        put(2 * ROWS, xa[0], dot(til, a_pays[0][:, 0:NMU]), 32, 0)


def product_kernel(near, lhs, w_ref, z_ref, acc_ref, rx_ref, ca, cb, copies=()):
    half = lhs.shape[0] // 2
    z = z_ref[...]
    for side in range(2):
        con = dot(lhs[side * half : side * half + ROWS], z)
        if side == 0:
            for copy in copies:
                copy.wait()
        for p in range(8):
            weight = w_ref[8 * near + p : 8 * near + p + 1]
            row = side * ROWS + p * 16
            ca[row : row + 16] = (con[p * 16 : p * 16 + 16] * weight).astype(BF16)
        dens = dot(lhs[side * half + ROWS : side * half + half], z)
        cb[side * ROWS : side * ROWS + ROWS] = dens[0:ROWS].astype(BF16)
        if near:
            rx_ref[side * 16 : side * 16 + 16] = dens[ROWS : ROWS + 16]
    acc_ref[...] = dot_t(ca[...], cb[...])


def far_kernel(a_near, a_pair, b0, b1, b2, b3, z_ref, qmap, screening, _, __, acc_ref, w_ref, lhs, xa, xb, ca, cb, qmap_ref, sems):
    table = pltpu.make_async_copy(qmap, qmap_ref, sems.at[16])
    table.start()
    build_kernel(0, a_near, a_pair, b0, b1, b2, b3, lhs, xa, xb)
    table.wait()
    copies = fetch_rows(qmap_ref, screening, w_ref, sems)
    product_kernel(0, lhs, w_ref, z_ref, acc_ref, None, ca, cb, copies)


def near_kernel(lhs, w_ref, z_ref, _, acc_ref, rx_ref, ca, cb):
    product_kernel(1, lhs, w_ref, z_ref, acc_ref, rx_ref, ca, cb)


def rows_kernel(side, acc, *refs):
    a_pays, b_pays, out_ref = refs[0:2], refs[2:6], refs[-1]
    half = 2 * ROWS

    def line(pay):
        return pay[:, NMU:WIDTH].astype(F32)[12:13]

    from_a = jnp.concatenate([jnp.broadcast_to(line(pay), (64, 128)) for pay in a_pays], 0)
    from_b = jnp.concatenate([jnp.broadcast_to(line(pay), (16, 128)) for pay in b_pays] * 2, 0)
    row = iota((ROWS, 128), 0)
    lane = iota((ROWS, 128), 1)
    same_c = lane & 3 == (row >> 2) & 3
    same_d = lane & 3 == row & 3
    from_a = jnp.where(same_c, from_a, 0.0).astype(BF16)
    from_b = jnp.where(same_d, from_b, 0.0).astype(BF16)
    lane = iota((128, half), 0)
    col = iota((128, half), 1)
    part = lane >> 4 == 1 + (col >> 7)
    x_d = dot(from_b, onehot(part & ((lane >> 2) & 3 == col & 3)))
    x_h = dot(from_a, onehot(part & ((lane >> 2) & 3 == (col >> 2) & 3)))
    pair = iota((ROWS, ROWS), 0) >> 4 == iota((ROWS, ROWS), 1) >> 4
    k_re = jnp.where(pair, acc[0:ROWS, 0:ROWS] + acc[ROWS:half, ROWS:half], 0.0)
    k_im = jnp.where(pair, acc[0:ROWS, ROWS:half] - acc[ROWS:half, 0:ROWS], 0.0)
    row = iota((half, 128), 0)
    lane = iota((half, 128), 1)
    part = lane >> 4 == row >> 7

    def fold(real, imag, picked, kept):
        high, low = split(jnp.concatenate([real, imag], 1))
        both = dot(jnp.concatenate([high, low], 0), onehot(part & picked))
        return split(jnp.where(kept, both[0:ROWS] + both[ROWS:half], 0.0))

    re, im = x_d[:, 0:ROWS], x_d[:, ROWS:half]
    terms = fold(k_re * re - k_im * im, k_re * im + k_im * re, (lane >> 2) & 3 == (row >> 2) & 3, same_c)
    re, im = x_h[:, 0:ROWS], x_h[:, ROWS:half]
    terms += fold(k_re * re + k_im * im, k_re * im - k_im * re, (lane >> 2) & 3 == row & 3, same_d)
    row = iota((16, 4 * ROWS), 0)
    col = iota((16, 4 * ROWS), 1)
    to_a = (col < half) & (row == side + 2 * ((col >> 6) & 1))
    to_b = (col >= half) & (row == 8 + ((col >> 4) & 3))
    total = dot(onehot(to_a | to_b), jnp.concatenate(terms, 0))
    if side:
        total += refs[6][...]
    out_ref[...] = total


def join_kernel(y0, y1, _, __, out_ref):
    out_ref[...] = y0[...] + y1[...]


def half_kernel(y0, y1, y2, _, out_ref):
    out_ref[...] = 0.5 * (y0[...] + y1[...]) + y2[...]


def mail_kernel(y0, y1, rows_ref, *mails):
    total = y0[...] + y1[...]
    for n, mail in enumerate(mails):
        mail[0:16] = total
        mail[16:24] = jnp.broadcast_to(rows_ref[8 + n : 9 + n], (8, 128))


def exchange_kernel(y_ref, c_ref, rx_ref, z_ref, out_ref, lhs):
    pad = jnp.zeros((12, 128), F32)
    for j in range(8):
        real = y_ref[j : j + 1]
        imag = y_ref[8 + j : 9 + j]
        for at, top, bottom in ((0, real, imag), (NMU, -imag, real)):
            high, low = split(jnp.concatenate([top, bottom], 0))
            rows = jnp.concatenate([high.astype(F32), low.astype(F32), pad], 0)
            lhs[:, at + j * 128 : at + j * 128 + 128] = rows.astype(BF16)
    acc_re = jnp.zeros((16, 128), F32)
    acc_im = jnp.zeros((16, 128), F32)
    for start in range(0, NG, 512):
        part = pl.ds(start, 512)
        total = dot(lhs[...], z_ref[:, part])
        pot_re = (total[0:1] + total[2:3]) * c_ref[:, part]
        pot_im = (total[1:2] + total[3:4]) * c_ref[:, part]
        rx_re = rx_ref[0:16, part]
        rx_im = rx_ref[16:32, part]
        real = rx_re * pot_re + rx_im * pot_im
        imag = rx_re * pot_im - rx_im * pot_re
        for at in range(0, 512, 128):
            acc_re += real[:, at : at + 128]
            acc_im += imag[:, at : at + 128]
    ones = jnp.ones((8, 128), BF16)
    out = []
    for acc in (acc_re, acc_im):
        high, low = split(acc)
        out.append((dot_t(ones, high) + dot_t(ones, low))[0:1])
    out_ref[...] = jnp.concatenate(out, 0)


def final_kernel(energy_ref, vector_ref, exchange_ref, near_ref, d_ref, h_ref, out_ref):
    scale = 1.0 / 256
    terms = near_ref[1:2] + d_ref[...] + h_ref[...]
    for part in range(2):
        term = terms[:, part * NT : part * NT + NT]
        out_ref[part : part + 1] = (
            energy_ref[...] * vector_ref[part : part + 1]
            + (2.0 * scale) * exchange_ref[part : part + 1]
            - scale * term
        )


def params(mib):
    return pltpu.CompilerParams(vmem_limit_bytes=mib * 1024 * 1024)


def cost(rows):
    return pl.CostEstimate(flops=2 * rows * 2 * NMU * NG, bytes_accessed=4 * NMU * NG, transcendentals=0)


def spreads():
    return [pltpu.VMEM((2, 64, NMU), F32), pltpu.VMEM((4, 64, NMU), F32)]


def far_call(*operands):
    return pl.pallas_call(
        far_kernel,
        in_specs=[VMEM] * 7 + [ANY] * 4,
        out_specs=[VMEM] * 2,
        out_shape=[pltpu.VMEM((2 * ROWS, 2 * ROWS), F32), pltpu.VMEM((16, NG), F32)],
        scratch_shapes=[pltpu.VMEM((4 * ROWS, 2 * NMU), BF16)]
        + spreads()
        + [pltpu.VMEM((2 * ROWS, NG), BF16)] * 2
        + [pltpu.SMEM((1, 256), jnp.int32), pltpu.SemaphoreType.DMA((17,))],
        compiler_params=params(30),
        cost_estimate=cost(4 * ROWS),
    )(*operands)


def build_call(*operands):
    return pl.pallas_call(
        functools.partial(build_kernel, 1),
        in_specs=[VMEM] * 6 + [ANY],
        out_specs=VMEM,
        out_shape=pltpu.VMEM((4 * ROWS + 32, 2 * NMU), BF16),
        scratch_shapes=spreads(),
        compiler_params=params(12),
    )(*operands)


def near_call(*operands):
    return pl.pallas_call(
        near_kernel,
        in_specs=[VMEM] * 3 + [ANY],
        out_specs=[VMEM] * 2,
        out_shape=[pltpu.VMEM((2 * ROWS, 2 * ROWS), F32), pltpu.VMEM((32, NG), F32)],
        scratch_shapes=[pltpu.VMEM((2 * ROWS, NG), BF16)] * 2,
        compiler_params=params(24),
        cost_estimate=cost(4 * ROWS),
    )(*operands)


def small_call(kernel, shapes, *operands, after=()):
    return pl.pallas_call(
        kernel,
        in_specs=[VMEM] * len(operands) + [ANY] * len(after),
        out_specs=[VMEM] * len(shapes),
        out_shape=[jax.ShapeDtypeStruct(shape, F32) for shape in shapes],
        compiler_params=params(8),
    )(*operands, *after)


def on_device(waves, vector, energies, basis, screening, coulomb, qmap):
    pay = pl.pallas_call(
        pack_kernel,
        in_specs=[ANY] * 2,
        out_specs=VMEM,
        out_shape=pltpu.VMEM((16, WIDTH), BF16),
        scratch_shapes=[pltpu.VMEM((2, NT), F32), pltpu.SemaphoreType.DMA((2,))],
        compiler_params=params(56),
    )(waves.reshape(16, NMU), vector.reshape(2, NT))
    a1 = move(pay, far=1)
    b0 = move(pay, step=1)
    a2 = move(pay, core=1)
    z = basis.reshape(2 * NMU, NG)
    coulomb = coulomb.reshape(1, NG)
    place = pl.pallas_call(
        place_kernel,
        in_specs=[VMEM],
        out_specs=VMEM,
        out_shape=jax.ShapeDtypeStruct((8, 128), F32),
        compiler_params=params(24),
        cost_estimate=pl.CostEstimate(flops=4000000000, bytes_accessed=1024, transcendentals=0),
    )(coulomb)
    b1, b2, b3 = (move(b0, y=n) for n in (1, 2, 3))
    a3 = move(a1, core=1)
    y = pl.pallas_call(
        transitions_kernel,
        in_specs=[VMEM] * 4,
        out_specs=VMEM,
        out_shape=jax.ShapeDtypeStruct((16, 128), F32),
        compiler_params=params(8),
    )(pay, a1, a2, a3)
    b_pays = (b0, b1, b2, b3)
    far_acc, weights = far_call(a1, a3, *b_pays, z, qmap, screening, place, y)
    (y,) = small_call(half_kernel, [(16, 128)], y, move(y, z=1), move(y, z=3, other=(0, 2)), after=(far_acc,))
    swapped = move(y, core=1)
    (far_rows,) = small_call(functools.partial(rows_kernel, 0), [(16, 128)], far_acc, a1, a3, *b_pays)
    lhs = build_call(pay, a2, *b_pays, far_acc)
    (y,) = small_call(join_kernel, [(16, 128)], y, swapped, after=(far_rows, lhs))
    near_acc, rx = near_call(lhs, weights, z, y)
    (y,) = small_call(half_kernel, [(16, 128)], y, move(y, x=1), move(y, x=3, other=(2, 0)), after=(near_acc,))
    swapped = move(y, core=1)
    (rows,) = small_call(functools.partial(rows_kernel, 1), [(16, 128)], near_acc, pay, a2, *b_pays, far_rows)
    mails = small_call(mail_kernel, [(24, 128)] * 4, y, swapped, rows)
    mail = mails[0] + move(mails[2], y=2) + move(mails[1], y=1) + move(mails[3], y=3)
    rows = rows[0:2] + move(rows[2:4], core=1)
    exchange = pl.pallas_call(
        exchange_kernel,
        in_specs=[VMEM] * 4,
        out_specs=VMEM,
        out_shape=jax.ShapeDtypeStruct((2, NT), F32),
        scratch_shapes=[pltpu.VMEM((16, 2 * NMU), BF16)],
        compiler_params=params(24),
        cost_estimate=cost(128),
    )(mail, coulomb, rx, z)

    (out,) = small_call(
        final_kernel,
        [(2, NT)],
        energies,
        vector.reshape(2, NT),
        exchange,
        rows,
        move(rows[0:1], far=1),
        move(mail[16:17], step=3),
    )
    return out.reshape(1, 2, NT)


def solution(mesh):
    return jax.shard_map(
        on_device,
        mesh=mesh,
        in_specs=(
            P(("grp", "kin"), None, None, None),
            P(("grp", "kin"), None, None),
            P(("grp", "kin"), None),
            P(),
            P(),
            P(),
            P(("grp", "kin"), None),
        ),
        out_specs=P(("grp", "kin"), None, None),
        check_vma=False,
    )
```

```python
import functools

import jax
import jax.numpy as jnp
from jax import lax
from jax.experimental import pallas as pl
from jax.experimental.pallas import tpu as pltpu
from jax.sharding import PartitionSpec as P

NT = 16
NMU = 1024
NG = 1536
WIDTH = NMU + 128
ROWS = 128
F32 = jnp.float32
BF16 = jnp.bfloat16
VMEM = pl.BlockSpec(memory_space=pltpu.VMEM)
SMEM = pl.BlockSpec(memory_space=pltpu.SMEM)
ANY = pl.BlockSpec(memory_space=pl.ANY)


def move(value, x=0, z=0, far=0, y=0, core=0, step=0, other=(0, 0)):
    pairs = []
    for a in range(4):
        for b in range(4):
            for c in range(2):
                for d in range(4):
                    for e in range(2):
                        source = (a * 4 + b) * 16 + c * 8 + d * 2 + e
                        to_x, to_z = other if e and any(other) else (x, z)
                        group = (((a + step) % 4) ^ to_x) * 4 + (b ^ to_z)
                        member = (c ^ far) * 8 + (d ^ y) * 2 + (e ^ core)
                        pairs.append((source, group * 16 + member))
    return lax.ppermute(value, ("grp", "kin"), pairs)


def iota(shape, dim):
    return lax.broadcasted_iota(jnp.int32, shape, dim)


def dot(left, right):
    return jnp.dot(left, right, preferred_element_type=F32)


def dot_t(left, right):
    return lax.dot_general(left, right, (((1,), (1,)), ((), ())), preferred_element_type=F32)


def split(value):
    high = value.astype(BF16)
    return high, (value - high.astype(F32)).astype(BF16)


def dot_split(left, right):
    high, low = split(left)
    return dot(high, right) + dot(low, right)


def onehot(condition):
    return jnp.where(condition, 1.0, 0.0).astype(BF16)


def spread(repeat):
    row = iota((64, 16), 0)
    col = iota((64, 16), 1)
    band = (row >> 2) & 3 if repeat else row & 3
    base = jnp.where(row < 32, 4, 0) + jnp.where((row >> 4) & 1 == 1, 8, 0)
    return onehot(col == band + base)


def conj_product(left_re, left_im, right_re, right_im):
    real = (left_re * right_re + left_im * right_im).astype(BF16)
    imag = (left_re * right_im - left_im * right_re).astype(BF16)
    return real, imag


def pack_kernel(waves, vector, pay_ref, vector_ref, sems):
    copies = (
        pltpu.make_async_copy(vector, vector_ref, sems.at[0]),
        pltpu.make_async_copy(waves, pay_ref.at[:, pl.ds(0, NMU)], sems.at[1]),
    )
    for copy in copies:
        copy.start()
    copies[0].wait()
    coarse = vector_ref[...].astype(BF16).astype(F32)
    real = jnp.broadcast_to(coarse[0:1], (16, 16))
    imag = jnp.broadcast_to(coarse[1:2], (16, 16))
    row = iota((16, 16), 0)
    lane = iota((16, 16), 1)
    of_v = lane >> 2 == row & 3
    by_c = onehot(row & 3 == lane & 3)
    real_v = dot(jnp.where(of_v, real, 0.0).astype(BF16), by_c)
    imag_v = dot(jnp.where(of_v, imag, 0.0).astype(BF16), by_c)
    upper = row < 8
    first = jnp.where(upper, real_v, imag_v)
    second = jnp.where(upper, -imag_v, real_v)
    mixer = jnp.where(lane & 8 == 0, first, second)
    mixer = jnp.where((row & 4 == 0) & (lane & 4 == 4), mixer, 0.0).astype(BF16)
    line_re = jnp.where(row == 12, real, 0.0).astype(BF16)
    line_im = jnp.where(row == 12, imag, 0.0).astype(BF16)
    row = iota((16, 128), 0)
    lane = iota((16, 128), 1)
    block = dot(mixer, onehot(lane == row)) + dot(line_re, onehot(lane == row + 16)) + dot(line_im, onehot(lane == row + 32))
    pay_ref[:, NMU:WIDTH] = block.astype(BF16)
    copies[1].wait()


def place_kernel(_, out_ref):
    out_ref[...] = jnp.zeros((8, 128), F32)


def weights_kernel(qmap_ref, screening, _, w_ref, sems):
    own = lax.axis_index("grp")
    member = lax.axis_index("kin")
    partner = (own + 12) & 15
    steps = []
    for m, flip in enumerate((8, 9, 0, 1)):
        from_a = qmap_ref[0, own * 16 + (member ^ flip)]
        for n in range(4):
            from_b = qmap_ref[0, partner * 16 + (member ^ (2 * n))]
            index = (((from_b >> 4) - (from_a >> 4)) & 15) * 16 + ((from_b - from_a) & 15)
            at = m * 4 + n
            copy = pltpu.make_async_copy(screening.at[pl.ds(index, 1)], w_ref.at[pl.ds(at, 1)], sems.at[at])
            copy.start()
            steps.append(copy)
    for copy in steps:
        copy.wait()


def transitions_kernel(a0, a1, a2, a3, y_ref):
    total_re = jnp.zeros((8, NMU), F32)
    total_im = jnp.zeros((8, NMU), F32)
    for pay in (a0, a1, a2, a3):
        waves = pay[:, 0:NMU]
        mixed = dot(pay[:, NMU : NMU + 16], waves)
        waves = waves.astype(F32)
        val_re, val_im = waves[0:8], waves[8:16]
        mix_re, mix_im = mixed[0:8], mixed[8:16]
        total_re += val_re * mix_re + val_im * mix_im
        total_im += val_re * mix_im - val_im * mix_re
    total_re = jnp.sum(total_re, 0, keepdims=True)
    total_im = jnp.sum(total_im, 0, keepdims=True)
    for j in range(8):
        y_ref[j : j + 1] = total_re[:, j * 128 : j * 128 + 128]
        y_ref[8 + j : 9 + j] = total_im[:, j * 128 : j * 128 + 128]


def build_kernel(near, a_near, a_pair, b0, b1, b2, b3, *refs):
    lhs, xa, xb = refs[-3:]
    a_pays = (a_near, a_pair)
    half = lhs.shape[0] // 2

    def put(row, left, right, left_at, right_at):
        real, imag = conj_product(
            left[left_at : left_at + 16],
            left[left_at + 16 : left_at + 32],
            right[right_at : right_at + 16],
            right[right_at + 16 : right_at + 32],
        )
        lhs[row : row + 16, 0:NMU] = real
        lhs[row : row + 16, NMU : 2 * NMU] = -imag
        lhs[half + row : half + row + 16, 0:NMU] = imag
        lhs[half + row : half + row + 16, NMU : 2 * NMU] = real

    rep = spread(True)
    til = spread(False)
    for m in range(2):
        xa[m] = dot(rep, a_pays[m][:, 0:NMU])
    for n, pay in enumerate((b0, b1, b2, b3)):
        xb[n] = dot(til, pay[:, 0:NMU])
    for m in range(2):
        for n in range(4):
            row = (m * 4 + n) * 16
            put(row, xa[m], xb[n], 0, 0)
            put(ROWS + row, xa[m], xb[n], 32, 32)
    if near:
        put(2 * ROWS, xa[0], dot(til, a_pays[0][:, 0:NMU]), 32, 0)


def product_kernel(near, lhs, w_ref, z_ref, acc_ref, rx_ref, ca, cb):
    half = lhs.shape[0] // 2
    z = z_ref[...]
    for side in range(2):
        con = dot(lhs[side * half : side * half + ROWS], z)
        for p in range(8):
            weight = w_ref[8 * near + p : 8 * near + p + 1]
            row = side * ROWS + p * 16
            ca[row : row + 16] = (con[p * 16 : p * 16 + 16] * weight).astype(BF16)
        dens = dot(lhs[side * half + ROWS : side * half + half], z)
        cb[side * ROWS : side * ROWS + ROWS] = dens[0:ROWS].astype(BF16)
        if near:
            rx_ref[side * 16 : side * 16 + 16] = dens[ROWS : ROWS + 16]
    acc_ref[...] = dot_t(ca[...], cb[...])


def far_kernel(a_near, a_pair, b0, b1, b2, b3, w_ref, z_ref, _, acc_ref, lhs, xa, xb, ca, cb):
    build_kernel(0, a_near, a_pair, b0, b1, b2, b3, lhs, xa, xb)
    product_kernel(0, lhs, w_ref, z_ref, acc_ref, None, ca, cb)


def near_kernel(lhs, w_ref, z_ref, _, acc_ref, rx_ref, ca, cb):
    product_kernel(1, lhs, w_ref, z_ref, acc_ref, rx_ref, ca, cb)


def rows_kernel(side, acc, *refs):
    a_pays, b_pays, out_ref = refs[0:2], refs[2:6], refs[-1]
    half = 2 * ROWS

    def line(pay):
        return pay[:, NMU:WIDTH].astype(F32)[12:13]

    from_a = jnp.concatenate([jnp.broadcast_to(line(pay), (64, 128)) for pay in a_pays], 0)
    from_b = jnp.concatenate([jnp.broadcast_to(line(pay), (16, 128)) for pay in b_pays] * 2, 0)
    row = iota((ROWS, 128), 0)
    lane = iota((ROWS, 128), 1)
    same_c = lane & 3 == (row >> 2) & 3
    same_d = lane & 3 == row & 3
    from_a = jnp.where(same_c, from_a, 0.0).astype(BF16)
    from_b = jnp.where(same_d, from_b, 0.0).astype(BF16)
    lane = iota((128, half), 0)
    col = iota((128, half), 1)
    part = lane >> 4 == 1 + (col >> 7)
    x_d = dot(from_b, onehot(part & ((lane >> 2) & 3 == col & 3)))
    x_h = dot(from_a, onehot(part & ((lane >> 2) & 3 == (col >> 2) & 3)))
    pair = iota((ROWS, ROWS), 0) >> 4 == iota((ROWS, ROWS), 1) >> 4
    k_re = jnp.where(pair, acc[0:ROWS, 0:ROWS] + acc[ROWS:half, ROWS:half], 0.0)
    k_im = jnp.where(pair, acc[0:ROWS, ROWS:half] - acc[ROWS:half, 0:ROWS], 0.0)
    row = iota((half, 128), 0)
    lane = iota((half, 128), 1)
    part = lane >> 4 == row >> 7

    def fold(real, imag, picked, kept):
        high, low = split(jnp.concatenate([real, imag], 1))
        both = dot(jnp.concatenate([high, low], 0), onehot(part & picked))
        return split(jnp.where(kept, both[0:ROWS] + both[ROWS:half], 0.0))

    re, im = x_d[:, 0:ROWS], x_d[:, ROWS:half]
    terms = fold(k_re * re - k_im * im, k_re * im + k_im * re, (lane >> 2) & 3 == (row >> 2) & 3, same_c)
    re, im = x_h[:, 0:ROWS], x_h[:, ROWS:half]
    terms += fold(k_re * re + k_im * im, k_re * im - k_im * re, (lane >> 2) & 3 == row & 3, same_d)
    row = iota((16, 4 * ROWS), 0)
    col = iota((16, 4 * ROWS), 1)
    to_a = (col < half) & (row == side + 2 * ((col >> 6) & 1))
    to_b = (col >= half) & (row == 8 + ((col >> 4) & 3))
    total = dot(onehot(to_a | to_b), jnp.concatenate(terms, 0))
    if side:
        total += refs[6][...]
    out_ref[...] = total


def join_kernel(y0, y1, _, __, out_ref):
    out_ref[...] = y0[...] + y1[...]


def half_kernel(y0, y1, y2, _, out_ref):
    out_ref[...] = 0.5 * (y0[...] + y1[...]) + y2[...]


def mail_kernel(y0, y1, rows_ref, *mails):
    total = y0[...] + y1[...]
    for n, mail in enumerate(mails):
        mail[0:16] = total
        mail[16:24] = jnp.broadcast_to(rows_ref[8 + n : 9 + n], (8, 128))


def exchange_kernel(y_ref, c_ref, rx_ref, z_ref, out_ref, lhs):
    pad = jnp.zeros((12, 128), F32)
    for j in range(8):
        real = y_ref[j : j + 1]
        imag = y_ref[8 + j : 9 + j]
        for at, top, bottom in ((0, real, imag), (NMU, -imag, real)):
            high, low = split(jnp.concatenate([top, bottom], 0))
            rows = jnp.concatenate([high.astype(F32), low.astype(F32), pad], 0)
            lhs[:, at + j * 128 : at + j * 128 + 128] = rows.astype(BF16)
    acc_re = jnp.zeros((16, 128), F32)
    acc_im = jnp.zeros((16, 128), F32)
    for start in range(0, NG, 512):
        part = pl.ds(start, 512)
        total = dot(lhs[...], z_ref[:, part])
        pot_re = (total[0:1] + total[2:3]) * c_ref[:, part]
        pot_im = (total[1:2] + total[3:4]) * c_ref[:, part]
        rx_re = rx_ref[0:16, part]
        rx_im = rx_ref[16:32, part]
        real = rx_re * pot_re + rx_im * pot_im
        imag = rx_re * pot_im - rx_im * pot_re
        for at in range(0, 512, 128):
            acc_re += real[:, at : at + 128]
            acc_im += imag[:, at : at + 128]
    ones = jnp.ones((8, 128), BF16)
    out = []
    for acc in (acc_re, acc_im):
        high, low = split(acc)
        out.append((dot_t(ones, high) + dot_t(ones, low))[0:1])
    out_ref[...] = jnp.concatenate(out, 0)


def final_kernel(energy_ref, vector_ref, exchange_ref, near_ref, d_ref, h_ref, out_ref):
    scale = 1.0 / 256
    terms = near_ref[1:2] + d_ref[...] + h_ref[...]
    for part in range(2):
        term = terms[:, part * NT : part * NT + NT]
        out_ref[part : part + 1] = (
            energy_ref[...] * vector_ref[part : part + 1]
            + (2.0 * scale) * exchange_ref[part : part + 1]
            - scale * term
        )


def params(mib):
    return pltpu.CompilerParams(vmem_limit_bytes=mib * 1024 * 1024)


def cost(rows):
    return pl.CostEstimate(flops=2 * rows * 2 * NMU * NG, bytes_accessed=4 * NMU * NG, transcendentals=0)


def spreads():
    return [pltpu.VMEM((2, 64, NMU), F32), pltpu.VMEM((4, 64, NMU), F32)]


def far_call(*operands):
    return pl.pallas_call(
        far_kernel,
        in_specs=[VMEM] * 8 + [ANY],
        out_specs=VMEM,
        out_shape=pltpu.VMEM((2 * ROWS, 2 * ROWS), F32),
        scratch_shapes=[pltpu.VMEM((4 * ROWS, 2 * NMU), BF16)] + spreads() + [pltpu.VMEM((2 * ROWS, NG), BF16)] * 2,
        compiler_params=params(24),
        cost_estimate=cost(4 * ROWS),
    )(*operands)


def build_call(*operands):
    return pl.pallas_call(
        functools.partial(build_kernel, 1),
        in_specs=[VMEM] * 6 + [ANY],
        out_specs=VMEM,
        out_shape=pltpu.VMEM((4 * ROWS + 32, 2 * NMU), BF16),
        scratch_shapes=spreads(),
        compiler_params=params(12),
    )(*operands)


def near_call(*operands):
    return pl.pallas_call(
        near_kernel,
        in_specs=[VMEM] * 3 + [ANY],
        out_specs=[VMEM] * 2,
        out_shape=[pltpu.VMEM((2 * ROWS, 2 * ROWS), F32), pltpu.VMEM((32, NG), F32)],
        scratch_shapes=[pltpu.VMEM((2 * ROWS, NG), BF16)] * 2,
        compiler_params=params(24),
        cost_estimate=cost(4 * ROWS),
    )(*operands)


def small_call(kernel, shapes, *operands, after=()):
    return pl.pallas_call(
        kernel,
        in_specs=[VMEM] * len(operands) + [ANY] * len(after),
        out_specs=[VMEM] * len(shapes),
        out_shape=[jax.ShapeDtypeStruct(shape, F32) for shape in shapes],
        compiler_params=params(8),
    )(*operands, *after)


def on_device(waves, vector, energies, basis, screening, coulomb, qmap):
    pay = pl.pallas_call(
        pack_kernel,
        in_specs=[ANY] * 2,
        out_specs=VMEM,
        out_shape=pltpu.VMEM((16, WIDTH), BF16),
        scratch_shapes=[pltpu.VMEM((2, NT), F32), pltpu.SemaphoreType.DMA((2,))],
        compiler_params=params(56),
    )(waves.reshape(16, NMU), vector.reshape(2, NT))
    a1 = move(pay, far=1)
    b0 = move(pay, step=1)
    a2 = move(pay, core=1)
    z = basis.reshape(2 * NMU, NG)
    place = pl.pallas_call(
        place_kernel,
        in_specs=[ANY],
        out_specs=VMEM,
        out_shape=jax.ShapeDtypeStruct((8, 128), F32),
        compiler_params=params(8),
        cost_estimate=pl.CostEstimate(flops=4000000000, bytes_accessed=1024, transcendentals=0),
    )(b0)
    weights = pl.pallas_call(
        weights_kernel,
        in_specs=[SMEM, ANY, ANY],
        out_specs=VMEM,
        out_shape=pltpu.VMEM((16, NG), F32),
        scratch_shapes=[pltpu.SemaphoreType.DMA((16,))],
        compiler_params=params(16),
        cost_estimate=pl.CostEstimate(flops=4000000000, bytes_accessed=1024, transcendentals=0),
    )(qmap, screening, place)
    b1, b2, b3 = (move(b0, y=n) for n in (1, 2, 3))
    a3 = move(a1, core=1)
    y = pl.pallas_call(
        transitions_kernel,
        in_specs=[VMEM] * 4,
        out_specs=VMEM,
        out_shape=jax.ShapeDtypeStruct((16, 128), F32),
        compiler_params=params(8),
    )(pay, a1, a2, a3)
    b_pays = (b0, b1, b2, b3)
    far_acc = far_call(a1, a3, *b_pays, weights, z, y)
    (y,) = small_call(half_kernel, [(16, 128)], y, move(y, z=1), move(y, z=3, other=(0, 2)), after=(far_acc,))
    swapped = move(y, core=1)
    (far_rows,) = small_call(functools.partial(rows_kernel, 0), [(16, 128)], far_acc, a1, a3, *b_pays)
    lhs = build_call(pay, a2, *b_pays, far_acc)
    (y,) = small_call(join_kernel, [(16, 128)], y, swapped, after=(far_rows, lhs))
    near_acc, rx = near_call(lhs, weights, z, y)
    (y,) = small_call(half_kernel, [(16, 128)], y, move(y, x=1), move(y, x=3, other=(2, 0)), after=(near_acc,))
    swapped = move(y, core=1)
    (rows,) = small_call(functools.partial(rows_kernel, 1), [(16, 128)], near_acc, pay, a2, *b_pays, far_rows)
    mails = small_call(mail_kernel, [(24, 128)] * 4, y, swapped, rows)
    mail = mails[0] + move(mails[2], y=2) + move(mails[1], y=1) + move(mails[3], y=3)
    rows = rows[0:2] + move(rows[2:4], core=1)
    exchange = pl.pallas_call(
        exchange_kernel,
        in_specs=[VMEM] * 4,
        out_specs=VMEM,
        out_shape=jax.ShapeDtypeStruct((2, NT), F32),
        scratch_shapes=[pltpu.VMEM((16, 2 * NMU), BF16)],
        compiler_params=params(24),
        cost_estimate=cost(128),
    )(mail, coulomb.reshape(1, NG), rx, z)

    (out,) = small_call(
        final_kernel,
        [(2, NT)],
        energies,
        vector.reshape(2, NT),
        exchange,
        rows,
        move(rows[0:1], far=1),
        move(mail[16:17], step=3),
    )
    return out.reshape(1, 2, NT)


def solution(mesh):
    return jax.shard_map(
        on_device,
        mesh=mesh,
        in_specs=(
            P(("grp", "kin"), None, None, None),
            P(("grp", "kin"), None, None),
            P(("grp", "kin"), None),
            P(),
            P(),
            P(),
            P(("grp", "kin"), None),
        ),
        out_specs=P(("grp", "kin"), None, None),
        check_vma=False,
    )
```

```python
import functools

import jax
import jax.numpy as jnp
from jax import lax
from jax.experimental import pallas as pl
from jax.experimental.pallas import tpu as pltpu
from jax.sharding import PartitionSpec as P

NT = 16
NMU = 1024
NG = 1536
WIDTH = NMU + 128
ROWS = 128
F32 = jnp.float32
BF16 = jnp.bfloat16
VMEM = pl.BlockSpec(memory_space=pltpu.VMEM)
SMEM = pl.BlockSpec(memory_space=pltpu.SMEM)
ANY = pl.BlockSpec(memory_space=pl.ANY)


def move(value, x=0, z=0, far=0, y=0, core=0, step=0, other=(0, 0)):
    pairs = []
    for a in range(4):
        for b in range(4):
            for c in range(2):
                for d in range(4):
                    for e in range(2):
                        source = (a * 4 + b) * 16 + c * 8 + d * 2 + e
                        to_x, to_z = other if e and any(other) else (x, z)
                        group = (((a + step) % 4) ^ to_x) * 4 + (b ^ to_z)
                        member = (c ^ far) * 8 + (d ^ y) * 2 + (e ^ core)
                        pairs.append((source, group * 16 + member))
    return lax.ppermute(value, ("grp", "kin"), pairs)


def iota(shape, dim):
    return lax.broadcasted_iota(jnp.int32, shape, dim)


def dot(left, right):
    return jnp.dot(left, right, preferred_element_type=F32)


def dot_t(left, right):
    return lax.dot_general(left, right, (((1,), (1,)), ((), ())), preferred_element_type=F32)


def split(value):
    high = value.astype(BF16)
    return high, (value - high.astype(F32)).astype(BF16)


def dot_split(left, right):
    high, low = split(left)
    return dot(high, right) + dot(low, right)


def onehot(condition):
    return jnp.where(condition, 1.0, 0.0).astype(BF16)


def spread(repeat):
    row = iota((64, 16), 0)
    col = iota((64, 16), 1)
    band = (row >> 2) & 3 if repeat else row & 3
    base = jnp.where(row < 32, 4, 0) + jnp.where((row >> 4) & 1 == 1, 8, 0)
    return onehot(col == band + base)


def conj_product(left_re, left_im, right_re, right_im):
    real = (left_re * right_re + left_im * right_im).astype(BF16)
    imag = (left_re * right_im - left_im * right_re).astype(BF16)
    return real, imag


def pack_kernel(waves, vector, pay_ref, vector_ref, sems):
    copies = (
        pltpu.make_async_copy(vector, vector_ref, sems.at[0]),
        pltpu.make_async_copy(waves, pay_ref.at[:, pl.ds(0, NMU)], sems.at[1]),
    )
    for copy in copies:
        copy.start()
    copies[0].wait()
    coarse = vector_ref[...].astype(BF16).astype(F32)
    real = jnp.broadcast_to(coarse[0:1], (16, 16))
    imag = jnp.broadcast_to(coarse[1:2], (16, 16))
    row = iota((16, 16), 0)
    lane = iota((16, 16), 1)
    of_v = lane >> 2 == row & 3
    by_c = onehot(row & 3 == lane & 3)
    real_v = dot(jnp.where(of_v, real, 0.0).astype(BF16), by_c)
    imag_v = dot(jnp.where(of_v, imag, 0.0).astype(BF16), by_c)
    upper = row < 8
    first = jnp.where(upper, real_v, imag_v)
    second = jnp.where(upper, -imag_v, real_v)
    mixer = jnp.where(lane & 8 == 0, first, second)
    mixer = jnp.where((row & 4 == 0) & (lane & 4 == 4), mixer, 0.0).astype(BF16)
    line_re = jnp.where(row == 12, real, 0.0).astype(BF16)
    line_im = jnp.where(row == 12, imag, 0.0).astype(BF16)
    row = iota((16, 128), 0)
    lane = iota((16, 128), 1)
    block = dot(mixer, onehot(lane == row)) + dot(line_re, onehot(lane == row + 16)) + dot(line_im, onehot(lane == row + 32))
    pay_ref[:, NMU:WIDTH] = block.astype(BF16)
    copies[1].wait()


def place_kernel(_, out_ref):
    out_ref[...] = jnp.zeros((8, 128), F32)


def weights_kernel(qmap_ref, screening, _, w_ref, sems):
    own = lax.axis_index("grp")
    member = lax.axis_index("kin")
    partner = (own + 12) & 15
    steps = []
    for m, flip in enumerate((8, 9, 0, 1)):
        from_a = qmap_ref[0, own * 16 + (member ^ flip)]
        for n in range(4):
            from_b = qmap_ref[0, partner * 16 + (member ^ (2 * n))]
            index = (((from_b >> 4) - (from_a >> 4)) & 15) * 16 + ((from_b - from_a) & 15)
            at = m * 4 + n
            copy = pltpu.make_async_copy(screening.at[pl.ds(index, 1)], w_ref.at[pl.ds(at, 1)], sems.at[at])
            copy.start()
            steps.append(copy)
    for copy in steps:
        copy.wait()


def transitions_kernel(a0, a1, a2, a3, y_ref):
    total_re = jnp.zeros((8, NMU), F32)
    total_im = jnp.zeros((8, NMU), F32)
    for pay in (a0, a1, a2, a3):
        waves = pay[:, 0:NMU]
        mixed = dot(pay[:, NMU : NMU + 16], waves)
        waves = waves.astype(F32)
        val_re, val_im = waves[0:8], waves[8:16]
        mix_re, mix_im = mixed[0:8], mixed[8:16]
        total_re += val_re * mix_re + val_im * mix_im
        total_im += val_re * mix_im - val_im * mix_re
    total_re = jnp.sum(total_re, 0, keepdims=True)
    total_im = jnp.sum(total_im, 0, keepdims=True)
    for j in range(8):
        y_ref[j : j + 1] = total_re[:, j * 128 : j * 128 + 128]
        y_ref[8 + j : 9 + j] = total_im[:, j * 128 : j * 128 + 128]


def build_kernel(near, a_near, a_pair, b0, b1, b2, b3, *refs):
    lhs, xa, xb = refs[-3:]
    a_pays = (a_near, a_pair)
    half = lhs.shape[0] // 2

    def put(row, left, right, left_at, right_at):
        real, imag = conj_product(
            left[left_at : left_at + 16],
            left[left_at + 16 : left_at + 32],
            right[right_at : right_at + 16],
            right[right_at + 16 : right_at + 32],
        )
        lhs[row : row + 16, 0:NMU] = real
        lhs[row : row + 16, NMU : 2 * NMU] = -imag
        lhs[half + row : half + row + 16, 0:NMU] = imag
        lhs[half + row : half + row + 16, NMU : 2 * NMU] = real

    rep = spread(True)
    til = spread(False)
    for m in range(2):
        xa[m] = dot(rep, a_pays[m][:, 0:NMU])
    for n, pay in enumerate((b0, b1, b2, b3)):
        xb[n] = dot(til, pay[:, 0:NMU])
    for m in range(2):
        for n in range(4):
            row = (m * 4 + n) * 16
            put(row, xa[m], xb[n], 0, 0)
            put(ROWS + row, xa[m], xb[n], 32, 32)
    if near:
        put(2 * ROWS, xa[0], dot(til, a_pays[0][:, 0:NMU]), 32, 0)


def product_kernel(near, lhs, w_ref, z_ref, acc_ref, rx_ref, ca, cb):
    half = lhs.shape[0] // 2
    z = z_ref[...]
    for side in range(2):
        con = dot(lhs[side * half : side * half + ROWS], z)
        for p in range(8):
            weight = w_ref[8 * near + p : 8 * near + p + 1]
            row = side * ROWS + p * 16
            ca[row : row + 16] = (con[p * 16 : p * 16 + 16] * weight).astype(BF16)
        dens = dot(lhs[side * half + ROWS : side * half + half], z)
        cb[side * ROWS : side * ROWS + ROWS] = dens[0:ROWS].astype(BF16)
        if near:
            rx_ref[side * 16 : side * 16 + 16] = dens[ROWS : ROWS + 16]
    acc_ref[...] = dot_t(ca[...], cb[...])


def far_kernel(a_near, a_pair, b0, b1, b2, b3, w_ref, z_ref, _, acc_ref, lhs, xa, xb, ca, cb):
    build_kernel(0, a_near, a_pair, b0, b1, b2, b3, lhs, xa, xb)
    product_kernel(0, lhs, w_ref, z_ref, acc_ref, None, ca, cb)


def near_kernel(lhs, w_ref, z_ref, _, acc_ref, rx_ref, ca, cb):
    product_kernel(1, lhs, w_ref, z_ref, acc_ref, rx_ref, ca, cb)


def rows_kernel(side, acc, *refs):
    a_pays, b_pays, out_ref = refs[0:2], refs[2:6], refs[-1]
    half = 2 * ROWS

    def line(pay):
        return pay[:, NMU:WIDTH].astype(F32)[12:13]

    from_a = jnp.concatenate([jnp.broadcast_to(line(pay), (64, 128)) for pay in a_pays], 0)
    from_b = jnp.concatenate([jnp.broadcast_to(line(pay), (16, 128)) for pay in b_pays] * 2, 0)
    row = iota((ROWS, 128), 0)
    lane = iota((ROWS, 128), 1)
    same_c = lane & 3 == (row >> 2) & 3
    same_d = lane & 3 == row & 3
    from_a = jnp.where(same_c, from_a, 0.0).astype(BF16)
    from_b = jnp.where(same_d, from_b, 0.0).astype(BF16)
    lane = iota((128, half), 0)
    col = iota((128, half), 1)
    part = lane >> 4 == 1 + (col >> 7)
    x_d = dot(from_b, onehot(part & ((lane >> 2) & 3 == col & 3)))
    x_h = dot(from_a, onehot(part & ((lane >> 2) & 3 == (col >> 2) & 3)))
    pair = iota((ROWS, ROWS), 0) >> 4 == iota((ROWS, ROWS), 1) >> 4
    k_re = jnp.where(pair, acc[0:ROWS, 0:ROWS] + acc[ROWS:half, ROWS:half], 0.0)
    k_im = jnp.where(pair, acc[0:ROWS, ROWS:half] - acc[ROWS:half, 0:ROWS], 0.0)
    row = iota((half, 128), 0)
    lane = iota((half, 128), 1)
    part = lane >> 4 == row >> 7

    def fold(real, imag, picked, kept):
        high, low = split(jnp.concatenate([real, imag], 1))
        both = dot(jnp.concatenate([high, low], 0), onehot(part & picked))
        return split(jnp.where(kept, both[0:ROWS] + both[ROWS:half], 0.0))

    re, im = x_d[:, 0:ROWS], x_d[:, ROWS:half]
    terms = fold(k_re * re - k_im * im, k_re * im + k_im * re, (lane >> 2) & 3 == (row >> 2) & 3, same_c)
    re, im = x_h[:, 0:ROWS], x_h[:, ROWS:half]
    terms += fold(k_re * re + k_im * im, k_re * im - k_im * re, (lane >> 2) & 3 == row & 3, same_d)
    row = iota((16, 4 * ROWS), 0)
    col = iota((16, 4 * ROWS), 1)
    to_a = (col < half) & (row == side + 2 * ((col >> 6) & 1))
    to_b = (col >= half) & (row == 8 + ((col >> 4) & 3))
    total = dot(onehot(to_a | to_b), jnp.concatenate(terms, 0))
    if side:
        total += refs[6][...]
    out_ref[...] = total


def relay_kernel(source, _, __, target):
    target[...] = source[...]


def join_kernel(y0, y1, _, __, out_ref):
    out_ref[...] = y0[...] + y1[...]


def half_kernel(y0, y1, y2, _, out_ref):
    out_ref[...] = 0.5 * (y0[...] + y1[...]) + y2[...]


def mail_kernel(y0, y1, rows_ref, *mails):
    total = y0[...] + y1[...]
    for n, mail in enumerate(mails):
        mail[0:16] = total
        mail[16:24] = jnp.broadcast_to(rows_ref[8 + n : 9 + n], (8, 128))


def exchange_kernel(y_ref, c_ref, rx_ref, z_ref, out_ref, lhs):
    pad = jnp.zeros((12, 128), F32)
    for j in range(8):
        real = y_ref[j : j + 1]
        imag = y_ref[8 + j : 9 + j]
        for at, top, bottom in ((0, real, imag), (NMU, -imag, real)):
            high, low = split(jnp.concatenate([top, bottom], 0))
            rows = jnp.concatenate([high.astype(F32), low.astype(F32), pad], 0)
            lhs[:, at + j * 128 : at + j * 128 + 128] = rows.astype(BF16)
    acc_re = jnp.zeros((16, 128), F32)
    acc_im = jnp.zeros((16, 128), F32)
    for start in range(0, NG, 512):
        part = pl.ds(start, 512)
        total = dot(lhs[...], z_ref[:, part])
        pot_re = (total[0:1] + total[2:3]) * c_ref[:, part]
        pot_im = (total[1:2] + total[3:4]) * c_ref[:, part]
        rx_re = rx_ref[0:16, part]
        rx_im = rx_ref[16:32, part]
        real = rx_re * pot_re + rx_im * pot_im
        imag = rx_re * pot_im - rx_im * pot_re
        for at in range(0, 512, 128):
            acc_re += real[:, at : at + 128]
            acc_im += imag[:, at : at + 128]
    ones = jnp.ones((8, 128), BF16)
    out = []
    for acc in (acc_re, acc_im):
        high, low = split(acc)
        out.append((dot_t(ones, high) + dot_t(ones, low))[0:1])
    out_ref[...] = jnp.concatenate(out, 0)


def final_kernel(energy_ref, vector_ref, exchange_ref, near_ref, d_ref, h_ref, out_ref):
    scale = 1.0 / 256
    terms = near_ref[1:2] + d_ref[...] + h_ref[...]
    for part in range(2):
        term = terms[:, part * NT : part * NT + NT]
        out_ref[part : part + 1] = (
            energy_ref[...] * vector_ref[part : part + 1]
            + (2.0 * scale) * exchange_ref[part : part + 1]
            - scale * term
        )


def params(mib):
    return pltpu.CompilerParams(vmem_limit_bytes=mib * 1024 * 1024)


def cost(rows):
    return pl.CostEstimate(flops=2 * rows * 2 * NMU * NG, bytes_accessed=4 * NMU * NG, transcendentals=0)


def spreads():
    return [pltpu.VMEM((2, 64, NMU), F32), pltpu.VMEM((4, 64, NMU), F32)]


def far_call(*operands):
    return pl.pallas_call(
        far_kernel,
        in_specs=[VMEM] * 8 + [ANY],
        out_specs=VMEM,
        out_shape=pltpu.VMEM((2 * ROWS, 2 * ROWS), F32),
        scratch_shapes=[pltpu.VMEM((4 * ROWS, 2 * NMU), BF16)] + spreads() + [pltpu.VMEM((2 * ROWS, NG), BF16)] * 2,
        compiler_params=params(24),
        cost_estimate=cost(4 * ROWS),
    )(*operands)


def build_call(*operands):
    return pl.pallas_call(
        functools.partial(build_kernel, 1),
        in_specs=[VMEM] * 6 + [ANY],
        out_specs=VMEM,
        out_shape=pltpu.VMEM((4 * ROWS + 32, 2 * NMU), BF16),
        scratch_shapes=spreads(),
        compiler_params=params(12),
    )(*operands)


def near_call(*operands):
    return pl.pallas_call(
        near_kernel,
        in_specs=[VMEM] * 3 + [ANY],
        out_specs=[VMEM] * 2,
        out_shape=[pltpu.VMEM((2 * ROWS, 2 * ROWS), F32), pltpu.VMEM((32, NG), F32)],
        scratch_shapes=[pltpu.VMEM((2 * ROWS, NG), BF16)] * 2,
        compiler_params=params(24),
        cost_estimate=cost(4 * ROWS),
    )(*operands)


def small_call(kernel, shapes, *operands, after=()):
    return pl.pallas_call(
        kernel,
        in_specs=[VMEM] * len(operands) + [ANY] * len(after),
        out_specs=[VMEM] * len(shapes),
        out_shape=[jax.ShapeDtypeStruct(shape, F32) for shape in shapes],
        compiler_params=params(8),
    )(*operands, *after)


def on_device(waves, vector, energies, basis, screening, coulomb, qmap):
    pay = pl.pallas_call(
        pack_kernel,
        in_specs=[ANY] * 2,
        out_specs=VMEM,
        out_shape=pltpu.VMEM((16, WIDTH), BF16),
        scratch_shapes=[pltpu.VMEM((2, NT), F32), pltpu.SemaphoreType.DMA((2,))],
        compiler_params=params(56),
    )(waves.reshape(16, NMU), vector.reshape(2, NT))
    a1 = move(pay, far=1)
    b0 = move(pay, step=1)
    a2 = move(pay, core=1)
    z = basis.reshape(2 * NMU, NG)
    place = pl.pallas_call(
        place_kernel,
        in_specs=[ANY],
        out_specs=VMEM,
        out_shape=jax.ShapeDtypeStruct((8, 128), F32),
        compiler_params=params(8),
        cost_estimate=pl.CostEstimate(flops=4000000000, bytes_accessed=1024, transcendentals=0),
    )(b0)
    weights = pl.pallas_call(
        weights_kernel,
        in_specs=[SMEM, ANY, ANY],
        out_specs=VMEM,
        out_shape=pltpu.VMEM((16, NG), F32),
        scratch_shapes=[pltpu.SemaphoreType.DMA((16,))],
        compiler_params=params(16),
        cost_estimate=pl.CostEstimate(flops=4000000000, bytes_accessed=1024, transcendentals=0),
    )(qmap, screening, place)
    b1, b2 = (move(b0, y=n) for n in (1, 2))
    later = pl.pallas_call(
        relay_kernel,
        in_specs=[VMEM, ANY, ANY],
        out_specs=VMEM,
        out_shape=jax.ShapeDtypeStruct((16, WIDTH), BF16),
        compiler_params=params(8),
    )(b0, a1, b1)
    b3 = move(later, y=3)
    a3 = move(a1, core=1)
    y = pl.pallas_call(
        transitions_kernel,
        in_specs=[VMEM] * 4,
        out_specs=VMEM,
        out_shape=jax.ShapeDtypeStruct((16, 128), F32),
        compiler_params=params(8),
    )(pay, a1, a2, a3)
    b_pays = (b0, b1, b2, b3)
    far_acc = far_call(a1, a3, *b_pays, weights, z, y)
    (y,) = small_call(half_kernel, [(16, 128)], y, move(y, z=1), move(y, z=3, other=(0, 2)), after=(far_acc,))
    swapped = move(y, core=1)
    (far_rows,) = small_call(functools.partial(rows_kernel, 0), [(16, 128)], far_acc, a1, a3, *b_pays)
    lhs = build_call(pay, a2, *b_pays, far_acc)
    (y,) = small_call(join_kernel, [(16, 128)], y, swapped, after=(far_rows, lhs))
    near_acc, rx = near_call(lhs, weights, z, y)
    (y,) = small_call(half_kernel, [(16, 128)], y, move(y, x=1), move(y, x=3, other=(2, 0)), after=(near_acc,))
    swapped = move(y, core=1)
    (rows,) = small_call(functools.partial(rows_kernel, 1), [(16, 128)], near_acc, pay, a2, *b_pays, far_rows)
    mails = small_call(mail_kernel, [(24, 128)] * 4, y, swapped, rows)
    mail = mails[0] + move(mails[2], y=2) + move(mails[1], y=1) + move(mails[3], y=3)
    rows = rows[0:2] + move(rows[2:4], core=1)
    exchange = pl.pallas_call(
        exchange_kernel,
        in_specs=[VMEM] * 4,
        out_specs=VMEM,
        out_shape=jax.ShapeDtypeStruct((2, NT), F32),
        scratch_shapes=[pltpu.VMEM((16, 2 * NMU), BF16)],
        compiler_params=params(24),
        cost_estimate=cost(128),
    )(mail, coulomb.reshape(1, NG), rx, z)

    (out,) = small_call(
        final_kernel,
        [(2, NT)],
        energies,
        vector.reshape(2, NT),
        exchange,
        rows,
        move(rows[0:1], far=1),
        move(mail[16:17], step=3),
    )
    return out.reshape(1, 2, NT)


def solution(mesh):
    return jax.shard_map(
        on_device,
        mesh=mesh,
        in_specs=(
            P(("grp", "kin"), None, None, None),
            P(("grp", "kin"), None, None),
            P(("grp", "kin"), None),
            P(),
            P(),
            P(),
            P(("grp", "kin"), None),
        ),
        out_specs=P(("grp", "kin"), None, None),
        check_vma=False,
    )
```

```python
import functools

import jax
import jax.numpy as jnp
from jax import lax
from jax.experimental import pallas as pl
from jax.experimental.pallas import tpu as pltpu
from jax.sharding import PartitionSpec as P

NT = 16
NMU = 1024
NG = 1536
WIDTH = NMU + 128
ROWS = 128
F32 = jnp.float32
BF16 = jnp.bfloat16
VMEM = pl.BlockSpec(memory_space=pltpu.VMEM)
SMEM = pl.BlockSpec(memory_space=pltpu.SMEM)
ANY = pl.BlockSpec(memory_space=pl.ANY)


def move(value, x=0, z=0, far=0, y=0, core=0, step=0, other=(0, 0)):
    pairs = []
    for a in range(4):
        for b in range(4):
            for c in range(2):
                for d in range(4):
                    for e in range(2):
                        source = (a * 4 + b) * 16 + c * 8 + d * 2 + e
                        to_x, to_z = other if e and any(other) else (x, z)
                        group = (((a + step) % 4) ^ to_x) * 4 + (b ^ to_z)
                        member = (c ^ far) * 8 + (d ^ y) * 2 + (e ^ core)
                        pairs.append((source, group * 16 + member))
    return lax.ppermute(value, ("grp", "kin"), pairs)


def iota(shape, dim):
    return lax.broadcasted_iota(jnp.int32, shape, dim)


def dot(left, right):
    return jnp.dot(left, right, preferred_element_type=F32)


def dot_t(left, right):
    return lax.dot_general(left, right, (((1,), (1,)), ((), ())), preferred_element_type=F32)


def split(value):
    high = value.astype(BF16)
    return high, (value - high.astype(F32)).astype(BF16)


def dot_split(left, right):
    high, low = split(left)
    return dot(high, right) + dot(low, right)


def onehot(condition):
    return jnp.where(condition, 1.0, 0.0).astype(BF16)


def spread(repeat):
    row = iota((64, 16), 0)
    col = iota((64, 16), 1)
    band = (row >> 2) & 3 if repeat else row & 3
    base = jnp.where(row < 32, 4, 0) + jnp.where((row >> 4) & 1 == 1, 8, 0)
    return onehot(col == band + base)


def conj_product(left_re, left_im, right_re, right_im):
    real = (left_re * right_re + left_im * right_im).astype(BF16)
    imag = (left_re * right_im - left_im * right_re).astype(BF16)
    return real, imag


def pack_kernel(waves, vector, pay_ref, vector_ref, sems):
    copies = (
        pltpu.make_async_copy(vector, vector_ref, sems.at[0]),
        pltpu.make_async_copy(waves, pay_ref.at[:, pl.ds(0, NMU)], sems.at[1]),
    )
    for copy in copies:
        copy.start()
    copies[0].wait()
    coarse = vector_ref[...].astype(BF16).astype(F32)
    real = jnp.broadcast_to(coarse[0:1], (16, 16))
    imag = jnp.broadcast_to(coarse[1:2], (16, 16))
    row = iota((16, 16), 0)
    lane = iota((16, 16), 1)
    of_v = lane >> 2 == row & 3
    by_c = onehot(row & 3 == lane & 3)
    real_v = dot(jnp.where(of_v, real, 0.0).astype(BF16), by_c)
    imag_v = dot(jnp.where(of_v, imag, 0.0).astype(BF16), by_c)
    upper = row < 8
    first = jnp.where(upper, real_v, imag_v)
    second = jnp.where(upper, -imag_v, real_v)
    mixer = jnp.where(lane & 8 == 0, first, second)
    mixer = jnp.where((row & 4 == 0) & (lane & 4 == 4), mixer, 0.0).astype(BF16)
    line_re = jnp.where(row == 12, real, 0.0).astype(BF16)
    line_im = jnp.where(row == 12, imag, 0.0).astype(BF16)
    row = iota((16, 128), 0)
    lane = iota((16, 128), 1)
    block = dot(mixer, onehot(lane == row)) + dot(line_re, onehot(lane == row + 16)) + dot(line_im, onehot(lane == row + 32))
    pay_ref[:, NMU:WIDTH] = block.astype(BF16)
    copies[1].wait()


def place_kernel(_, out_ref):
    out_ref[...] = jnp.zeros((8, 128), F32)


def weights_kernel(qmap_ref, screening, _, w_ref, sems):
    own = lax.axis_index("grp")
    member = lax.axis_index("kin")
    partner = (own + 12) & 15
    steps = []
    for m, flip in enumerate((8, 9, 0, 1)):
        from_a = qmap_ref[0, own * 16 + (member ^ flip)]
        for n in range(4):
            from_b = qmap_ref[0, partner * 16 + (member ^ (2 * n))]
            index = (((from_b >> 4) - (from_a >> 4)) & 15) * 16 + ((from_b - from_a) & 15)
            at = m * 4 + n
            copy = pltpu.make_async_copy(screening.at[pl.ds(index, 1)], w_ref.at[pl.ds(at, 1)], sems.at[at])
            copy.start()
            steps.append(copy)
    for copy in steps:
        copy.wait()


def transitions_kernel(a0, a1, a2, a3, y_ref):
    total_re = jnp.zeros((8, NMU), F32)
    total_im = jnp.zeros((8, NMU), F32)
    for pay in (a0, a1, a2, a3):
        waves = pay[:, 0:NMU]
        mixed = dot(pay[:, NMU : NMU + 16], waves)
        waves = waves.astype(F32)
        val_re, val_im = waves[0:8], waves[8:16]
        mix_re, mix_im = mixed[0:8], mixed[8:16]
        total_re += val_re * mix_re + val_im * mix_im
        total_im += val_re * mix_im - val_im * mix_re
    total_re = jnp.sum(total_re, 0, keepdims=True)
    total_im = jnp.sum(total_im, 0, keepdims=True)
    for j in range(8):
        y_ref[j : j + 1] = total_re[:, j * 128 : j * 128 + 128]
        y_ref[8 + j : 9 + j] = total_im[:, j * 128 : j * 128 + 128]


def build_kernel(near, a_near, a_pair, b0, b1, b2, b3, *refs):
    lhs, xa, xb = refs[-3:]
    a_pays = (a_near, a_pair)
    half = lhs.shape[0] // 2

    def put(row, left, right, left_at, right_at):
        real, imag = conj_product(
            left[left_at : left_at + 16],
            left[left_at + 16 : left_at + 32],
            right[right_at : right_at + 16],
            right[right_at + 16 : right_at + 32],
        )
        lhs[row : row + 16, 0:NMU] = real
        lhs[row : row + 16, NMU : 2 * NMU] = -imag
        lhs[half + row : half + row + 16, 0:NMU] = imag
        lhs[half + row : half + row + 16, NMU : 2 * NMU] = real

    rep = spread(True)
    til = spread(False)
    for m in range(2):
        xa[m] = dot(rep, a_pays[m][:, 0:NMU])
    for n, pay in enumerate((b0, b1, b2, b3)):
        xb[n] = dot(til, pay[:, 0:NMU])
    for m in range(2):
        for n in range(4):
            row = (m * 4 + n) * 16
            put(row, xa[m], xb[n], 0, 0)
            put(ROWS + row, xa[m], xb[n], 32, 32)
    if near:
        put(2 * ROWS, xa[0], dot(til, a_pays[0][:, 0:NMU]), 32, 0)


def product_kernel(near, lhs, w_ref, z_ref, acc_ref, rx_ref, ca, cb):
    half = lhs.shape[0] // 2
    z = z_ref[...]
    for side in range(2):
        con = dot(lhs[side * half : side * half + ROWS], z)
        for p in range(8):
            weight = w_ref[8 * near + p : 8 * near + p + 1]
            row = side * ROWS + p * 16
            ca[row : row + 16] = (con[p * 16 : p * 16 + 16] * weight).astype(BF16)
        dens = dot(lhs[side * half + ROWS : side * half + half], z)
        cb[side * ROWS : side * ROWS + ROWS] = dens[0:ROWS].astype(BF16)
        if near:
            rx_ref[side * 16 : side * 16 + 16] = dens[ROWS : ROWS + 16]
    acc_ref[...] = dot_t(ca[...], cb[...])


def far_kernel(a_near, a_pair, b0, b1, b2, b3, w_ref, z_ref, _, acc_ref, lhs, xa, xb, ca, cb):
    build_kernel(0, a_near, a_pair, b0, b1, b2, b3, lhs, xa, xb)
    product_kernel(0, lhs, w_ref, z_ref, acc_ref, None, ca, cb)


def near_kernel(lhs, w_ref, z_ref, _, acc_ref, rx_ref, ca, cb):
    product_kernel(1, lhs, w_ref, z_ref, acc_ref, rx_ref, ca, cb)


def rows_kernel(side, acc, *refs):
    a_pays, b_pays, out_ref = refs[0:2], refs[2:6], refs[-1]
    half = 2 * ROWS

    def line(pay):
        return pay[:, NMU:WIDTH].astype(F32)[12:13]

    from_a = jnp.concatenate([jnp.broadcast_to(line(pay), (64, 128)) for pay in a_pays], 0)
    from_b = jnp.concatenate([jnp.broadcast_to(line(pay), (16, 128)) for pay in b_pays] * 2, 0)
    row = iota((ROWS, 128), 0)
    lane = iota((ROWS, 128), 1)
    same_c = lane & 3 == (row >> 2) & 3
    same_d = lane & 3 == row & 3
    from_a = jnp.where(same_c, from_a, 0.0).astype(BF16)
    from_b = jnp.where(same_d, from_b, 0.0).astype(BF16)
    lane = iota((128, half), 0)
    col = iota((128, half), 1)
    part = lane >> 4 == 1 + (col >> 7)
    x_d = dot(from_b, onehot(part & ((lane >> 2) & 3 == col & 3)))
    x_h = dot(from_a, onehot(part & ((lane >> 2) & 3 == (col >> 2) & 3)))
    pair = iota((ROWS, ROWS), 0) >> 4 == iota((ROWS, ROWS), 1) >> 4
    k_re = jnp.where(pair, acc[0:ROWS, 0:ROWS] + acc[ROWS:half, ROWS:half], 0.0)
    k_im = jnp.where(pair, acc[0:ROWS, ROWS:half] - acc[ROWS:half, 0:ROWS], 0.0)
    row = iota((half, 128), 0)
    lane = iota((half, 128), 1)
    part = lane >> 4 == row >> 7

    def fold(real, imag, picked, kept):
        high, low = split(jnp.concatenate([real, imag], 1))
        both = dot(jnp.concatenate([high, low], 0), onehot(part & picked))
        return split(jnp.where(kept, both[0:ROWS] + both[ROWS:half], 0.0))

    re, im = x_d[:, 0:ROWS], x_d[:, ROWS:half]
    terms = fold(k_re * re - k_im * im, k_re * im + k_im * re, (lane >> 2) & 3 == (row >> 2) & 3, same_c)
    re, im = x_h[:, 0:ROWS], x_h[:, ROWS:half]
    terms += fold(k_re * re + k_im * im, k_re * im - k_im * re, (lane >> 2) & 3 == row & 3, same_d)
    row = iota((16, 4 * ROWS), 0)
    col = iota((16, 4 * ROWS), 1)
    to_a = (col < half) & (row == side + 2 * ((col >> 6) & 1))
    to_b = (col >= half) & (row == 8 + ((col >> 4) & 3))
    total = dot(onehot(to_a | to_b), jnp.concatenate(terms, 0))
    if side:
        total += refs[6][...]
    out_ref[...] = total


def join_kernel(y0, y1, _, __, out_ref):
    out_ref[...] = y0[...] + y1[...]


def half_kernel(y0, y1, y2, _, out_ref):
    out_ref[...] = 0.5 * (y0[...] + y1[...]) + y2[...]


def mail_kernel(y0, y1, rows_ref, *mails):
    total = y0[...] + y1[...]
    for n, mail in enumerate(mails):
        mail[0:16] = total
        mail[16:24] = jnp.broadcast_to(rows_ref[8 + n : 9 + n], (8, 128))


def exchange_kernel(y_ref, c_ref, rx_ref, z_ref, out_ref, lhs):
    pad = jnp.zeros((12, 128), F32)
    for j in range(8):
        real = y_ref[j : j + 1]
        imag = y_ref[8 + j : 9 + j]
        for at, top, bottom in ((0, real, imag), (NMU, -imag, real)):
            high, low = split(jnp.concatenate([top, bottom], 0))
            rows = jnp.concatenate([high.astype(F32), low.astype(F32), pad], 0)
            lhs[:, at + j * 128 : at + j * 128 + 128] = rows.astype(BF16)
    acc_re = jnp.zeros((16, 128), F32)
    acc_im = jnp.zeros((16, 128), F32)
    for start in range(0, NG, 512):
        part = pl.ds(start, 512)
        total = dot(lhs[...], z_ref[:, part])
        pot_re = (total[0:1] + total[2:3]) * c_ref[:, part]
        pot_im = (total[1:2] + total[3:4]) * c_ref[:, part]
        rx_re = rx_ref[0:16, part]
        rx_im = rx_ref[16:32, part]
        real = rx_re * pot_re + rx_im * pot_im
        imag = rx_re * pot_im - rx_im * pot_re
        for at in range(0, 512, 128):
            acc_re += real[:, at : at + 128]
            acc_im += imag[:, at : at + 128]
    ones = jnp.ones((8, 128), BF16)
    out = []
    for acc in (acc_re, acc_im):
        high, low = split(acc)
        out.append((dot_t(ones, high) + dot_t(ones, low))[0:1])
    out_ref[...] = jnp.concatenate(out, 0)


def final_kernel(energy_ref, vector_ref, exchange_ref, near_ref, d_ref, h_ref, out_ref):
    scale = 1.0 / 256
    terms = near_ref[...] + d_ref[...] + h_ref[...]
    for part in range(2):
        term = terms[:, part * NT : part * NT + NT]
        out_ref[part : part + 1] = (
            energy_ref[...] * vector_ref[part : part + 1]
            + (2.0 * scale) * exchange_ref[part : part + 1]
            - scale * term
        )


def params(mib):
    return pltpu.CompilerParams(vmem_limit_bytes=mib * 1024 * 1024)


def cost(rows):
    return pl.CostEstimate(flops=2 * rows * 2 * NMU * NG, bytes_accessed=4 * NMU * NG, transcendentals=0)


def spreads():
    return [pltpu.VMEM((2, 64, NMU), F32), pltpu.VMEM((4, 64, NMU), F32)]


def far_call(*operands):
    return pl.pallas_call(
        far_kernel,
        in_specs=[VMEM] * 8 + [ANY],
        out_specs=VMEM,
        out_shape=pltpu.VMEM((2 * ROWS, 2 * ROWS), F32),
        scratch_shapes=[pltpu.VMEM((4 * ROWS, 2 * NMU), BF16)] + spreads() + [pltpu.VMEM((2 * ROWS, NG), BF16)] * 2,
        compiler_params=params(24),
        cost_estimate=cost(4 * ROWS),
    )(*operands)


def build_call(*operands):
    return pl.pallas_call(
        functools.partial(build_kernel, 1),
        in_specs=[VMEM] * 6 + [ANY],
        out_specs=VMEM,
        out_shape=pltpu.VMEM((4 * ROWS + 32, 2 * NMU), BF16),
        scratch_shapes=spreads(),
        compiler_params=params(12),
    )(*operands)


def near_call(*operands):
    return pl.pallas_call(
        near_kernel,
        in_specs=[VMEM] * 3 + [ANY],
        out_specs=[VMEM] * 2,
        out_shape=[pltpu.VMEM((2 * ROWS, 2 * ROWS), F32), pltpu.VMEM((32, NG), F32)],
        scratch_shapes=[pltpu.VMEM((2 * ROWS, NG), BF16)] * 2,
        compiler_params=params(24),
        cost_estimate=cost(4 * ROWS),
    )(*operands)


def small_call(kernel, shapes, *operands, after=()):
    return pl.pallas_call(
        kernel,
        in_specs=[VMEM] * len(operands) + [ANY] * len(after),
        out_specs=[VMEM] * len(shapes),
        out_shape=[jax.ShapeDtypeStruct(shape, F32) for shape in shapes],
        compiler_params=params(8),
    )(*operands, *after)


def on_device(waves, vector, energies, basis, screening, coulomb, qmap):
    pay = pl.pallas_call(
        pack_kernel,
        in_specs=[ANY] * 2,
        out_specs=VMEM,
        out_shape=pltpu.VMEM((16, WIDTH), BF16),
        scratch_shapes=[pltpu.VMEM((2, NT), F32), pltpu.SemaphoreType.DMA((2,))],
        compiler_params=params(56),
    )(waves.reshape(16, NMU), vector.reshape(2, NT))
    a1 = move(pay, far=1)
    b0 = move(pay, step=1)
    a2 = move(pay, core=1)
    z = basis.reshape(2 * NMU, NG)
    place = pl.pallas_call(
        place_kernel,
        in_specs=[ANY],
        out_specs=VMEM,
        out_shape=jax.ShapeDtypeStruct((8, 128), F32),
        compiler_params=params(8),
        cost_estimate=pl.CostEstimate(flops=4000000000, bytes_accessed=1024, transcendentals=0),
    )(b0)
    weights = pl.pallas_call(
        weights_kernel,
        in_specs=[SMEM, ANY, ANY],
        out_specs=VMEM,
        out_shape=pltpu.VMEM((16, NG), F32),
        scratch_shapes=[pltpu.SemaphoreType.DMA((16,))],
        compiler_params=params(16),
        cost_estimate=pl.CostEstimate(flops=4000000000, bytes_accessed=1024, transcendentals=0),
    )(qmap, screening, place)
    b1, b2, b3 = (move(b0, y=n) for n in (1, 2, 3))
    a3 = move(a1, core=1)
    y = pl.pallas_call(
        transitions_kernel,
        in_specs=[VMEM] * 4,
        out_specs=VMEM,
        out_shape=jax.ShapeDtypeStruct((16, 128), F32),
        compiler_params=params(8),
    )(pay, a1, a2, a3)
    b_pays = (b0, b1, b2, b3)
    far_acc = far_call(a1, a3, *b_pays, weights, z, y)
    (y,) = small_call(half_kernel, [(16, 128)], y, move(y, z=1), move(y, z=3, other=(0, 2)), after=(far_acc,))
    swapped = move(y, core=1)
    (far_rows,) = small_call(functools.partial(rows_kernel, 0), [(16, 128)], far_acc, a1, a3, *b_pays)
    lhs = build_call(pay, a2, *b_pays, far_acc)
    (y,) = small_call(join_kernel, [(16, 128)], y, swapped, after=(far_rows, lhs))
    near_acc, rx = near_call(lhs, weights, z, y)
    (y,) = small_call(half_kernel, [(16, 128)], y, move(y, x=1), move(y, x=3, other=(2, 0)), after=(near_acc,))
    swapped = move(y, core=1)
    (rows,) = small_call(functools.partial(rows_kernel, 1), [(16, 128)], near_acc, pay, a2, *b_pays, far_rows)
    mails = small_call(mail_kernel, [(24, 128)] * 4, y, swapped, rows)
    mail = mails[0] + move(mails[2], y=2) + move(mails[1], y=1) + move(mails[3], y=3)
    far_row = far_rows[0:1] + move(far_rows[2:3], core=1)
    near_row = rows[1:2] + move(rows[3:4], core=1)
    exchange = pl.pallas_call(
        exchange_kernel,
        in_specs=[VMEM] * 4,
        out_specs=VMEM,
        out_shape=jax.ShapeDtypeStruct((2, NT), F32),
        scratch_shapes=[pltpu.VMEM((16, 2 * NMU), BF16)],
        compiler_params=params(24),
        cost_estimate=cost(128),
    )(mail, coulomb.reshape(1, NG), rx, z)

    (out,) = small_call(
        final_kernel,
        [(2, NT)],
        energies,
        vector.reshape(2, NT),
        exchange,
        near_row,
        move(far_row, far=1),
        move(mail[16:17], step=3),
    )
    return out.reshape(1, 2, NT)


def solution(mesh):
    return jax.shard_map(
        on_device,
        mesh=mesh,
        in_specs=(
            P(("grp", "kin"), None, None, None),
            P(("grp", "kin"), None, None),
            P(("grp", "kin"), None),
            P(),
            P(),
            P(),
            P(("grp", "kin"), None),
        ),
        out_specs=P(("grp", "kin"), None, None),
        check_vma=False,
    )
```
